32 devices in a mesh: dp: 4 (over y, core), seq: 8 (over z, x).
Axes of the slice: x: 2, y: 2, z: 4, core: 2. Of those that a mesh axis runs over, the one named last changes fastest.
Arguments:
- tokens: bfloat16 [4096, 1024], P(('dp', 'seq')), may hold values from -6 to 6
- span_order: int32 [4, 16], P('dp'), may hold values from 0 to 15, each once within a row
- w_query: bfloat16 [1024, 2048], P(('dp', 'seq')), may hold values from -0.1875 to 0.1875
- key_matrix: bfloat16 [1024, 1024], P(('dp', 'seq')), may hold values from -0.1875 to 0.1875
- value_matrix: bfloat16 [1024, 1024], P(('dp', 'seq')), may hold values from -0.1875 to 0.1875
- w_output: bfloat16 [2048, 1024], P(None, ('dp', 'seq')), may hold values from -2 to 2
- w_gate: bfloat16 [1024, 3072], P(('dp', 'seq')), may hold values from -0.1875 to 0.1875
- w_up: bfloat16 [1024, 3072], P(('dp', 'seq')), may hold values from -0.1875 to 0.1875
- w_down: bfloat16 [3072, 1024], P(None, ('dp', 'seq')), may hold values from -0.109375 to 0.109375
- norm_gains: bfloat16 [2, 1024], P(None, ('dp', 'seq')), may hold values from 0.5 to 1.5
- head_gains: bfloat16 [2, 128], replicated, may hold values from 0.5 to 1.5
- cotangent: bfloat16 [4096, 1024], P(('dp', 'seq')), may hold values from -6 to 6
Outputs:
- output: bfloat16 [4096, 1024], P(('dp', 'seq'))
- grad_input: bfloat16 [4096, 1024], P(('dp', 'seq'))
- grad_w_query: float32 [1024, 2048], P(('dp', 'seq'))
- grad_w_key: float32 [1024, 1024], P(('dp', 'seq'))
- grad_w_value: float32 [1024, 1024], P(('dp', 'seq'))
- grad_w_output: float32 [2048, 1024], P(None, ('dp', 'seq'))
- grad_w_gate: float32 [1024, 3072], P(('dp', 'seq'))
- grad_w_up: float32 [1024, 3072], P(('dp', 'seq'))
- grad_w_down: float32 [3072, 1024], P(None, ('dp', 'seq'))
- grad_norm_gains: float32 [2, 1024], P(None, ('dp', 'seq'))
- grad_head_gains: float32 [2, 128], replicated
The draws below stay inside these ranges and needn't reach their ends.
Inputs may be any that keep to these rules, and one draw needn't show every extreme that they name: Each row is a permutation of the 16 spans of its sequence; slot k holds the 64 tokens at positions span_order[s, k] * 64 onwards, and device j of seq holds slots 2 j and 2 j + 1.
All inputs are finite; a program needn't handle non-finite values.
Results may differ from the reference program's by a relative error of at most 0.02.
Values may be sent and summed in bfloat16 or wider, within the bound.
No kernel may reach another device: no remote copies, remote signals or barrier semaphores. Data moves between devices by JAX's collectives and lax.ppermute only.
A program may use at most 320 MiB of HBM per device.

```python
import math
import jax
import jax.numpy as jnp
from jax import lax

MODEL_WIDTH = 1024
HQ = 16
KEY_VALUE_HEADS = 8
HEAD_SIZE = 128
FF = 3072
SEQS = 4
SLOTS = 16
ROWS = 4096


def steps_of(stream_key, dims, shards, least, top_value):
    def one(position, shards_of):
        draws = jax.random.uniform(jax.random.fold_in(jax.random.fold_in(stream_key, 6), position), (shards_of,), jnp.float32, least / len(shards), top_value / len(shards))
        return jnp.repeat(jnp.exp(draws), dims[position] // shards_of).reshape((-1,) + (1,) * (len(dims) - position - 1))

    loudness = one(*shards[0])
    for cut in shards[1:]:
        loudness = loudness * one(*cut)
    return loudness


def bell_draw(stream_key, shape, scale, reach, split=(), kind=jnp.bfloat16):
    array = jax.random.normal(stream_key, shape, jnp.float32) * scale
    if len(split) > 0:
        array = steps_of(stream_key, shape, split, -0.22, 0.18) * array
    return jnp.clip(array, min=-reach, max=reach).astype(kind)


def setup_inputs(seed: int = 0) -> dict:
    streams_of = jax.random.split(jax.random.key(seed), 13)
    tokens = bell_draw(streams_of[0], (ROWS, MODEL_WIDTH), 1.0, 6.0, ((0, 32),))
    span_order = jax.vmap(lambda own: jax.random.permutation(own, SLOTS))(jax.random.split(streams_of[1], SEQS)).reshape((SEQS, SLOTS)).astype(jnp.int32)
    w_query = bell_draw(streams_of[2], (MODEL_WIDTH, HQ * HEAD_SIZE), MODEL_WIDTH ** -0.5, 0.1875, ((0, 32),))
    key_matrix = bell_draw(streams_of[3], (MODEL_WIDTH, KEY_VALUE_HEADS * HEAD_SIZE), MODEL_WIDTH ** -0.5, 0.1875, ((0, 32),))
    value_matrix = bell_draw(streams_of[4], (MODEL_WIDTH, KEY_VALUE_HEADS * HEAD_SIZE), MODEL_WIDTH ** -0.5, 0.1875, ((0, 32),))
    w_output = bell_draw(streams_of[5], (HQ * HEAD_SIZE, MODEL_WIDTH), (max(1, HQ * HEAD_SIZE // 256)) ** -0.5, 2.0, ((1, 32),))
    w_gate = bell_draw(streams_of[6], (MODEL_WIDTH, FF), MODEL_WIDTH ** -0.5, 0.1875, ((0, 32),))
    w_up = bell_draw(streams_of[7], (MODEL_WIDTH, FF), MODEL_WIDTH ** -0.5, 0.1875, ((0, 32),))
    w_down = bell_draw(streams_of[8], (FF, MODEL_WIDTH), FF ** -0.5, 0.109375, ((1, 32),))
    norm_gains = jnp.clip(1.0 + 0.1 * jax.random.normal(streams_of[9], (2, MODEL_WIDTH), jnp.float32), 0.5, 1.5).astype(jnp.bfloat16)
    head_gains = jnp.clip(1.0 + 0.1 * jax.random.normal(streams_of[10], (2, HEAD_SIZE), jnp.float32), 0.5, 1.5).astype(jnp.bfloat16)
    cotangent = bell_draw(streams_of[11], (ROWS, MODEL_WIDTH), 1.0, 6.0, ((0, 32),))
    return dict(tokens=tokens, span_order=span_order, w_query=w_query, key_matrix=key_matrix, value_matrix=value_matrix, w_output=w_output, w_gate=w_gate, w_up=w_up, w_down=w_down, norm_gains=norm_gains, head_gains=head_gains, cotangent=cotangent)


eps_model = 1e-06
rope_base = 1000000.0
masked_value = -1e+30
highest = lax.Precision.HIGHEST

@jax.custom_vjp
def low(v):
    return lax.optimization_barrier(v.astype(jnp.bfloat16)).astype(jnp.float32)

@jax.custom_vjp
def low_back(v):
    return v

def low_keep(v):
    return (low(v), None)

def low_pass(kept, grad):
    return (grad,)

def back_keep(v):
    return (v, None)

def back_low(kept, grad):
    return (low(grad),)
low.defvjp(low_keep, low_pass)
low_back.defvjp(back_keep, back_low)

def rms_scale(values, gain):
    inverse = lax.rsqrt(lax.optimization_barrier(jnp.mean(values * values, axis=-1, keepdims=True)) + eps_model)
    return values * inverse * gain

def rope_tables(positions, head_dim):
    half_dim = head_dim // 2
    freqs = rope_base ** (-(jnp.arange(half_dim, dtype=jnp.float32) * 2.0) / head_dim)
    angles = positions.astype(jnp.float32)[:, None] * freqs[None, :]
    cosine = jnp.cos(angles)
    sine = jnp.sin(angles)
    return (jnp.concatenate([cosine, cosine], -1), jnp.concatenate([sine, sine], -1))

def rotate(values, cosine, sine):
    half_dim = values.shape[-1] // 2
    turned = jnp.concatenate([-values[..., half_dim:], values[..., :half_dim]], -1)
    return values * cosine[:, None, :] + turned * sine[:, None, :]

def head_prep(flat, gain, cosine, sine):
    row_count = flat.shape[0]
    shaped = flat.reshape(row_count, -1, gain.shape[0])
    return rotate(rms_scale(shaped, gain), cosine, sine).reshape(row_count, -1)

def matmul(left, right):
    return jnp.dot(left, right, precision=highest, preferred_element_type=jnp.float32)

def layer(inputs, params, positions):
    w_query, key_matrix, value_matrix, w_output, w_gate, w_up, w_down, norm_gains, head_gains = params
    length = inputs.shape[0]
    head_dim = head_gains.shape[1]
    kv_heads = key_matrix.shape[1] // head_dim
    groups = w_query.shape[1] // key_matrix.shape[1]
    cosine, sine = rope_tables(positions, head_dim)
    normed = low(rms_scale(inputs, norm_gains[0]))
    query_pre = low_back(matmul(normed, w_query))
    key_pre = low_back(matmul(normed, key_matrix))
    values = low(low_back(matmul(normed, value_matrix)))
    query = low(head_prep(query_pre, head_gains[0], cosine, sine))
    keys = low(head_prep(key_pre, head_gains[1], cosine, sine))
    block = math.gcd(length, 512)
    number = length // block
    query_blocks = query.reshape(number, block, kv_heads, groups, head_dim)
    pos_blocks = positions.reshape(number, block)
    key_heads = keys.reshape(length, kv_heads, head_dim)
    value_heads = values.reshape(length, kv_heads, head_dim)

    def attend(item):
        query_heads, query_pos = item
        scores = jnp.einsum('tkgd,skd->kgts', query_heads, key_heads, precision=highest) * head_dim ** (-0.5)
        scores = low_back(scores)
        allowed = positions[None, :] <= query_pos[:, None]
        scores = jnp.where(allowed, scores, masked_value)
        probs = low(jax.nn.softmax(scores, axis=-1))
        return jnp.einsum('kgts,skd->tkgd', probs, value_heads, precision=highest)
    attention_output = lax.map(jax.checkpoint(attend), (query_blocks, pos_blocks))
    attention_output = low(low_back(attention_output.reshape(length, -1)))
    middle = inputs + low_back(matmul(attention_output, w_output))
    normed_two = low(rms_scale(middle, norm_gains[1]))
    gate = low_back(matmul(normed_two, w_gate))
    up_proj = low_back(matmul(normed_two, w_up))
    hidden = low(jax.nn.silu(gate) * up_proj)
    return middle + low_back(matmul(hidden, w_down))

def reference(tokens, span_order, w_query, key_matrix, value_matrix, w_output, w_gate, w_up, w_down, norm_gains, head_gains, cotangent):
    seq_count = span_order.shape[0]
    slot_count = span_order.shape[1]
    length = tokens.shape[0] // seq_count
    span_len = length // slot_count
    width = tokens.shape[1]
    params = (w_query.astype(jnp.float32), key_matrix.astype(jnp.float32), value_matrix.astype(jnp.float32), w_output.astype(jnp.float32), w_gate.astype(jnp.float32), w_up.astype(jnp.float32), w_down.astype(jnp.float32), norm_gains.astype(jnp.float32), head_gains.astype(jnp.float32))
    inputs = tokens.astype(jnp.float32).reshape(seq_count, length, width)
    cotangents = cotangent.astype(jnp.float32).reshape(seq_count, length, width)
    row_index = jnp.arange(length, dtype=jnp.int32)

    def add_arrays(first, second):
        return first + second

    def one_sequence(totals, item):
        seq_inputs, seq_cotangent, order_row = item
        positions = (order_row[row_index // span_len] * span_len + row_index % span_len).astype(jnp.int32)

        def forward(values, weights):
            return layer(values, weights, positions)
        result, backward = jax.vjp(forward, seq_inputs, params)
        grad_values, grad_params = backward(seq_cotangent)
        totals = jax.tree.map(add_arrays, totals, grad_params)
        return (totals, (result, grad_values))
    zeros = jax.tree.map(jnp.zeros_like, params)
    totals, (results, grad_inputs) = lax.scan(one_sequence, zeros, (inputs, cotangents, span_order))
    return (results.reshape(-1, width).astype(jnp.bfloat16), grad_inputs.reshape(-1, width).astype(jnp.bfloat16), totals[0], totals[1], totals[2], totals[3], totals[4], totals[5], totals[6], totals[7], totals[8])
```

```python
import math

import jax
import jax.numpy as jnp
from jax import lax
from jax.experimental import pallas as pl
from jax.experimental.pallas import tpu as pltpu
from jax.sharding import PartitionSpec as P

eps_model = 1e-06
rope_base = 1000000.0
masked_value = -1e30


def passed_along(array, axis, by):
    length = lax.axis_size(axis)
    return lax.ppermute(array, axis, [(i, (i + by) % length) for i in range(length)])


def rms_scale(values, gain):
    inverse = lax.rsqrt(jnp.mean(values * values, axis=-1, keepdims=True) + eps_model)
    return values * inverse * gain


def rope_tables(positions, head_dim):
    half_dim = head_dim // 2
    freqs = rope_base ** (-(jnp.arange(half_dim, dtype=jnp.float32) * 2.0) / head_dim)
    angles = positions.astype(jnp.float32)[:, None] * freqs[None, :]
    cosine = jnp.cos(angles)
    sine = jnp.sin(angles)
    return (jnp.concatenate([cosine, cosine], -1), jnp.concatenate([sine, sine], -1))


def rotate(values, cosine, sine):
    half_dim = values.shape[-1] // 2
    turned = jnp.concatenate([-values[..., half_dim:], values[..., :half_dim]], -1)
    return values * cosine[:, None, :] + turned * sine[:, None, :]


def head_prep(flat, gain, cosine, sine):
    row_count = flat.shape[0]
    shaped = flat.reshape(row_count, -1, gain.shape[0])
    return rotate(rms_scale(shaped, gain), cosine, sine).reshape(row_count, -1)


def span_positions(order_row, start, count, span_len):
    row_index = start + jnp.arange(count, dtype=jnp.int32)
    slot_index = row_index // span_len
    table = (
        slot_index[:, None] == jnp.arange(order_row.shape[0], dtype=jnp.int32)[None, :]
    ).astype(jnp.int32)
    return jnp.sum(table * order_row[None, :], axis=1) * span_len + row_index % span_len


def block_size(count):
    return count if count <= 512 else math.gcd(count, 512)


def contract_rows(left, right):
    return lax.dot_general(
        left, right, (((0,), (0,)), ((), ())), preferred_element_type=jnp.float32
    )


def contract_cols(left, right):
    return lax.dot_general(
        left, right, (((1,), (1,)), ((), ())), preferred_element_type=jnp.float32
    )


def forward_block(state, query_heads, query_pos, key_block, value_block, key_pos, head_dim):
    run_max, run_total, accum = state
    kv_heads = key_block.shape[1] // head_dim
    key_heads = key_block.reshape(-1, kv_heads, head_dim)
    value_heads = value_block.reshape(-1, kv_heads, head_dim)
    scores = jnp.einsum(
        "tkgd,skd->kgts", query_heads, key_heads, preferred_element_type=jnp.float32
    ) * head_dim ** (-0.5)
    allowed = key_pos[None, :] <= query_pos[:, None]
    scores = jnp.where(allowed, scores, masked_value)
    new_max = jnp.maximum(run_max, jnp.max(scores, axis=-1))
    probs = jnp.where(allowed, jnp.exp(scores - new_max[..., None]), 0.0)
    factor = jnp.exp(run_max - new_max)
    new_total = run_total * factor + jnp.sum(probs, axis=-1)
    accum = accum * factor[..., None] + jnp.einsum(
        "kgts,skd->kgtd",
        probs.astype(jnp.bfloat16),
        value_heads,
        preferred_element_type=jnp.float32,
    )
    return (new_max, new_total, accum)


def backward_block(
    query_heads, grad_heads, log_total, delta, query_pos, key_block, value_block, key_pos, head_dim
):
    kv_heads = key_block.shape[1] // head_dim
    key_heads = key_block.reshape(-1, kv_heads, head_dim)
    value_heads = value_block.reshape(-1, kv_heads, head_dim)
    scale = head_dim ** (-0.5)
    scores = (
        jnp.einsum("tkgd,skd->kgts", query_heads, key_heads, preferred_element_type=jnp.float32)
        * scale
    )
    allowed = key_pos[None, :] <= query_pos[:, None]
    probs = jnp.where(allowed, jnp.exp(scores - log_total[..., None]), 0.0)
    grad_value = jnp.einsum(
        "kgts,tkgd->skd", probs.astype(jnp.bfloat16), grad_heads, preferred_element_type=jnp.float32
    )
    grad_probs = jnp.einsum(
        "tkgd,skd->kgts", grad_heads, value_heads, preferred_element_type=jnp.float32
    )
    grad_scores = (probs * (grad_probs - delta[..., None])).astype(jnp.bfloat16)
    grad_query = (
        jnp.einsum("kgts,skd->tkgd", grad_scores, key_heads, preferred_element_type=jnp.float32)
        * scale
    )
    grad_key = (
        jnp.einsum("kgts,tkgd->skd", grad_scores, query_heads, preferred_element_type=jnp.float32)
        * scale
    )
    count = key_block.shape[0]
    return (
        grad_query,
        jnp.concatenate([grad_key.reshape(count, -1), grad_value.reshape(count, -1)], 1),
    )


def swiglu(gate, up_proj):
    return jax.nn.silu(gate) * up_proj


def shards(
    tokens,
    span_order,
    w_query,
    key_matrix,
    value_matrix,
    w_output,
    w_gate,
    w_up,
    w_down,
    norm_gains,
    head_gains,
    cotangent,
):
    row_count = tokens.shape[0]
    span_len = row_count // 2
    head_dim = head_gains.shape[1]
    kv_heads = key_matrix.shape[1] // head_dim
    groups = w_query.shape[1] // key_matrix.shape[1]
    order_row = span_order[0]
    seq_devices = lax.axis_size("seq")
    seq_index = lax.axis_index("seq")
    own_start = seq_index * row_count

    def positions_of(start, count):
        return span_positions(order_row, start, count, span_len)

    query_pos = positions_of(own_start, row_count)
    cosine, sine = rope_tables(query_pos, head_dim)
    gains_head = head_gains.astype(jnp.float32)

    def prepare(flat, gain):
        return head_prep(flat, gain, cosine, sine)

    wq_full, wk_full, wv_full, wo_full, gains_full = (
        lax.all_gather(w_query, ("dp", "seq"), axis=0, tiled=True),
        lax.all_gather(key_matrix, ("dp", "seq"), axis=0, tiled=True),
        lax.all_gather(value_matrix, ("dp", "seq"), axis=0, tiled=True),
        lax.all_gather(w_output, ("dp", "seq"), axis=1, tiled=True),
        lax.all_gather(norm_gains, ("dp", "seq"), axis=1, tiled=True),
    )
    gains_full = gains_full.astype(jnp.float32)
    inputs = tokens.astype(jnp.float32)
    normed, norm_back = jax.vjp(rms_scale, inputs, gains_full[0])
    normed_low = normed.astype(jnp.bfloat16)
    query_pre = jnp.dot(normed_low, wq_full, preferred_element_type=jnp.float32)
    key_pre = jnp.dot(normed_low, wk_full, preferred_element_type=jnp.float32)
    value_low = jnp.dot(normed_low, wv_full, preferred_element_type=jnp.float32).astype(
        jnp.bfloat16
    )
    query_rot, query_back = jax.vjp(prepare, query_pre, gains_head[0])
    key_rot, key_back = jax.vjp(prepare, key_pre, gains_head[1])
    query_heads = query_rot.astype(jnp.bfloat16).reshape(row_count, kv_heads, groups, head_dim)
    key_low = key_rot.astype(jnp.bfloat16)
    latest = jnp.max(query_pos)
    start_state = (
        jnp.full((kv_heads, groups, row_count), masked_value, jnp.float32),
        jnp.zeros((kv_heads, groups, row_count), jnp.float32),
        jnp.zeros((kv_heads, groups, row_count, head_dim), jnp.float32),
    )
    state = start_state
    key_piece = lax.all_gather(key_low, "seq", axis=0, tiled=True)
    value_piece = lax.all_gather(value_low, "seq", axis=0, tiled=True)
    count = key_piece.shape[0]
    size = block_size(count)
    number = count // size
    key_blocks = key_piece.reshape(number, size, key_piece.shape[1])
    value_blocks = value_piece.reshape(number, size, value_piece.shape[1])

    def attend_one_block(carried, item):
        index, key_block, value_block = item
        key_pos = positions_of(index * size, size)

        def attend_compute(inner):
            return forward_block(
                inner, query_heads, query_pos, key_block, value_block, key_pos, head_dim
            )

        def attend_unchanged(inner):
            return inner

        return (
            lax.cond(jnp.min(key_pos) <= latest, attend_compute, attend_unchanged, carried),
            None,
        )

    state, _ = lax.scan(
        attend_one_block, state, (jnp.arange(number, dtype=jnp.int32), key_blocks, value_blocks)
    )
    final_max, final_total, accum = state
    attended_heads = (accum / final_total[..., None]).transpose(2, 0, 1, 3)
    attention_output = attended_heads.reshape(row_count, -1)
    log_total = final_max + jnp.log(final_total)
    attended_low = attention_output.astype(jnp.bfloat16)
    middle = inputs + jnp.dot(attended_low, wo_full, preferred_element_type=jnp.float32)
    wg_full, wu_full, wd_full = (
        lax.all_gather(w_gate, ("dp", "seq"), axis=0, tiled=True),
        lax.all_gather(w_up, ("dp", "seq"), axis=0, tiled=True),
        lax.all_gather(w_down, ("dp", "seq"), axis=1, tiled=True),
    )
    normed_two, norm_two_back = jax.vjp(rms_scale, middle, gains_full[1])
    normed_two_low = normed_two.astype(jnp.bfloat16)
    gate = jnp.dot(normed_two_low, wg_full, preferred_element_type=jnp.float32)
    up_proj = jnp.dot(normed_two_low, wu_full, preferred_element_type=jnp.float32)
    hidden, swiglu_back = jax.vjp(swiglu, gate, up_proj)
    hidden_low = hidden.astype(jnp.bfloat16)
    output = middle + jnp.dot(hidden_low, wd_full, preferred_element_type=jnp.float32)
    grad_out = cotangent.astype(jnp.float32)
    wg_full, wu_full, wd_full = (
        lax.all_gather(w_gate, ("dp", "seq"), axis=0, tiled=True),
        lax.all_gather(w_up, ("dp", "seq"), axis=0, tiled=True),
        lax.all_gather(w_down, ("dp", "seq"), axis=1, tiled=True),
    )
    grad_down_turned = contract_rows(cotangent, hidden_low)
    grad_hidden = contract_cols(cotangent, wd_full)
    grad_gate, grad_up = swiglu_back(grad_hidden)
    gate_low = grad_gate.astype(jnp.bfloat16)
    up_low = grad_up.astype(jnp.bfloat16)
    grad_wg = contract_rows(normed_two_low, gate_low)
    grad_wu = contract_rows(normed_two_low, up_low)
    grad_normed_two = contract_cols(gate_low, wg_full) + contract_cols(up_low, wu_full)
    grad_middle_norm, grad_gain_two = norm_two_back(grad_normed_two)
    feed_grads = (
        lax.psum_scatter(grad_wg, ("dp", "seq"), scatter_dimension=0, tiled=True),
        lax.psum_scatter(grad_wu, ("dp", "seq"), scatter_dimension=0, tiled=True),
        lax.psum_scatter(grad_down_turned, ("dp", "seq"), scatter_dimension=0, tiled=True),
    )
    grad_middle = grad_out + grad_middle_norm
    wq_full, wk_full, wv_full, wo_full = (
        lax.all_gather(w_query, ("dp", "seq"), axis=0, tiled=True),
        lax.all_gather(key_matrix, ("dp", "seq"), axis=0, tiled=True),
        lax.all_gather(value_matrix, ("dp", "seq"), axis=0, tiled=True),
        lax.all_gather(w_output, ("dp", "seq"), axis=1, tiled=True),
    )
    middle_low = grad_middle.astype(jnp.bfloat16)
    grad_wo_turned = contract_rows(middle_low, attended_low)
    attention_output_gradient = contract_cols(middle_low, wo_full).astype(jnp.bfloat16)
    grad_heads = attention_output_gradient.reshape(row_count, kv_heads, groups, head_dim)
    delta = jnp.sum(grad_heads.astype(jnp.float32) * attended_heads, axis=-1).transpose(1, 2, 0)

    def piece_back(grad_query_all, key_piece, value_piece, start):
        count = key_piece.shape[0]
        size = block_size(count)
        number = count // size
        key_blocks = key_piece.reshape(number, size, key_piece.shape[1])
        value_blocks = value_piece.reshape(number, size, value_piece.shape[1])

        def piece_one_block(grad_query_run, item):
            index, key_block, value_block = item
            key_pos = positions_of(start + index * size, size)

            def piece_compute(inner):
                grad_query, grad_kv = backward_block(
                    query_heads,
                    grad_heads,
                    log_total,
                    delta,
                    query_pos,
                    key_block,
                    value_block,
                    key_pos,
                    head_dim,
                )
                return (inner + grad_query, grad_kv)

            def piece_unchanged(inner):
                return (inner, jnp.zeros((size, 2 * kv_heads * head_dim), jnp.float32))

            return lax.cond(
                jnp.min(key_pos) <= latest, piece_compute, piece_unchanged, grad_query_run
            )

        grad_query_all, stacked = lax.scan(
            piece_one_block,
            grad_query_all,
            (jnp.arange(number, dtype=jnp.int32), key_blocks, value_blocks),
        )
        return (grad_query_all, stacked.reshape(count, -1))

    start_query = jnp.zeros((row_count, kv_heads, groups, head_dim), jnp.float32)

    def cycle_step(step, carried):
        grad_query_all, key_piece, value_piece, partial_value = carried
        source = (seq_index - step + seq_devices) % seq_devices
        grad_query_all, local_kv = piece_back(
            grad_query_all, key_piece, value_piece, source * row_count
        )
        partial_value = partial_value + local_kv
        key_piece, value_piece = passed_along((key_piece, value_piece), "seq", 1)
        partial_value = passed_along(partial_value.astype(jnp.bfloat16), "seq", 1).astype(
            partial_value.dtype
        )
        return (grad_query_all, key_piece, value_piece, partial_value)

    initial_cycle_step = (
        start_query,
        key_low,
        value_low,
        jnp.zeros((row_count, 2 * kv_heads * head_dim), jnp.float32),
    )
    grad_query_rot, _, _, grad_kv = lax.fori_loop(0, seq_devices, cycle_step, initial_cycle_step)
    split_at = kv_heads * head_dim
    grad_query_pre, grad_gain_query = query_back(grad_query_rot.reshape(row_count, -1))
    grad_key_pre, grad_gain_key = key_back(grad_kv[:, :split_at])
    query_grad_low = grad_query_pre.astype(jnp.bfloat16)
    key_grad_low = grad_key_pre.astype(jnp.bfloat16)
    value_grad_low = grad_kv[:, split_at:].astype(jnp.bfloat16)
    grad_wq = contract_rows(normed_low, query_grad_low)
    grad_wk = contract_rows(normed_low, key_grad_low)
    grad_wv = contract_rows(normed_low, value_grad_low)
    grad_normed = (
        contract_cols(query_grad_low, wq_full)
        + contract_cols(key_grad_low, wk_full)
        + contract_cols(value_grad_low, wv_full)
    )
    grad_input_norm, grad_gain_one = norm_back(grad_normed)
    grad_input = grad_middle + grad_input_norm
    gains_turned = jnp.stack([grad_gain_one, grad_gain_two], axis=1)
    attention_grads = (
        lax.psum_scatter(grad_wq, ("dp", "seq"), scatter_dimension=0, tiled=True),
        lax.psum_scatter(grad_wk, ("dp", "seq"), scatter_dimension=0, tiled=True),
        lax.psum_scatter(grad_wv, ("dp", "seq"), scatter_dimension=0, tiled=True),
        lax.psum_scatter(grad_wo_turned, ("dp", "seq"), scatter_dimension=0, tiled=True),
        lax.psum_scatter(gains_turned, ("dp", "seq"), scatter_dimension=0, tiled=True),
    )
    head_grads = lax.psum(jnp.stack([grad_gain_query, grad_gain_key]), ("dp", "seq"))
    return (
        output.astype(jnp.bfloat16),
        grad_input.astype(jnp.bfloat16),
        attention_grads[0],
        attention_grads[1],
        attention_grads[2],
        attention_grads[3].T,
        feed_grads[0],
        feed_grads[1],
        feed_grads[2].T,
        attention_grads[4].T,
        head_grads,
    )


def dp_order():
    order, bit = [0], lax.axis_size("dp") // 2
    while bit:
        order = order + [i ^ bit for i in order]
        bit //= 2
    return order


def dp_swap(array, bit):
    return lax.ppermute(array, "dp", [(i, i ^ bit) for i in range(lax.axis_size("dp"))])


def dp_gather(array):
    held, bit = array[None], lax.axis_size("dp") // 2
    while bit:
        held = jnp.concatenate([held, dp_swap(held, bit)], 0)
        bit //= 2
    return held


def dp_scatter(partial):
    bit = 1
    while bit < lax.axis_size("dp"):
        half = partial.shape[0] // 2
        partial = partial[:half] + dp_swap(partial[half:].astype(jnp.bfloat16), bit).astype(
            jnp.float32
        )
        bit *= 2
    return partial[0]


def to_seq(array):
    return lax.all_to_all(array, "seq", 0, 0, tiled=True)


def attend_kernel(query_ref, key_ref, value_ref, query_pos_ref, key_pos_ref, out_ref, low_ref, log_ref):
    scale = query_ref.shape[-1] ** (-0.5)
    scores = contract_cols(query_ref[...], key_ref[...]) * scale
    allowed = key_pos_ref[...] <= query_pos_ref[...]
    scores = jnp.where(allowed, scores, masked_value)
    top = jnp.max(scores, axis=-1, keepdims=True)
    weights = jnp.exp(scores - top)
    total = jnp.sum(weights, axis=-1, keepdims=True)
    probs = (weights * (1.0 / total)).astype(jnp.bfloat16)
    attended = jnp.dot(probs, value_ref[...], preferred_element_type=jnp.float32)
    out_ref[...] = attended
    low_ref[...] = attended.astype(jnp.bfloat16)
    log_ref[...] = top + jnp.log(total)


def attend_back_kernel(
    query_ref,
    key_ref,
    value_ref,
    query_pos_ref,
    key_pos_ref,
    out_ref,
    log_ref,
    grad_ref,
    grad_query_ref,
    grad_key_ref,
    grad_value_ref,
):
    @pl.when(pl.program_id(0) == 0)
    def _():
        grad_key_ref[...] = jnp.zeros_like(grad_key_ref)
        grad_value_ref[...] = jnp.zeros_like(grad_value_ref)

    scale = query_ref.shape[-1] ** (-0.5)
    query, key, grad = query_ref[...], key_ref[...], grad_ref[...]
    scores = contract_cols(query, key) * scale
    allowed = key_pos_ref[...] <= query_pos_ref[...]
    probs = jnp.where(allowed, jnp.exp(scores - log_ref[...]), 0.0)
    delta = jnp.sum(grad.astype(jnp.float32) * out_ref[...], axis=-1, keepdims=True)
    grad_probs = contract_cols(grad, value_ref[...])
    grad_scores = (probs * (grad_probs - delta)).astype(jnp.bfloat16)
    grad_value_ref[...] += contract_rows(probs.astype(jnp.bfloat16), grad)
    grad_query_ref[...] = jnp.dot(grad_scores, key, preferred_element_type=jnp.float32) * scale
    grad_key_ref[...] += contract_rows(grad_scores, query) * scale


def attend_specs(rows, length, head_dim, block):
    by_rows = pl.BlockSpec((block, head_dim), lambda i: (i, 0))
    by_row = pl.BlockSpec((block, 1), lambda i: (i, 0))
    whole = pl.BlockSpec((length, head_dim), lambda i: (0, 0))
    key_pos = pl.BlockSpec((1, length), lambda i: (0, 0))
    return (rows // block,), by_rows, by_row, whole, key_pos


def attend(query, key, value, query_pos, key_pos):
    rows, head_dim = query.shape
    length = key.shape[0]
    grid, by_rows, by_row, whole, keys = attend_specs(rows, length, head_dim, 512)
    return pl.pallas_call(
        attend_kernel,
        grid=grid,
        in_specs=[by_rows, whole, whole, by_row, keys],
        out_specs=[by_rows, by_rows, by_row],
        out_shape=[
            jax.ShapeDtypeStruct((rows, head_dim), jnp.float32),
            jax.ShapeDtypeStruct((rows, head_dim), jnp.bfloat16),
            jax.ShapeDtypeStruct((rows, 1), jnp.float32),
        ],
        compiler_params=pltpu.CompilerParams(vmem_limit_bytes=40 * 1024 * 1024),
    )(query, key, value, query_pos, key_pos)


def attend_back(query, key, value, query_pos, key_pos, attended, log_total, grad):
    rows, head_dim = query.shape
    length = key.shape[0]
    grid, by_rows, by_row, whole, keys = attend_specs(rows, length, head_dim, 512)
    return pl.pallas_call(
        attend_back_kernel,
        grid=grid,
        in_specs=[by_rows, whole, whole, by_row, keys, by_rows, by_row, by_rows],
        out_specs=[by_rows, whole, whole],
        out_shape=[
            jax.ShapeDtypeStruct((rows, head_dim), jnp.float32),
            jax.ShapeDtypeStruct((length, head_dim), jnp.float32),
            jax.ShapeDtypeStruct((length, head_dim), jnp.float32),
        ],
        compiler_params=pltpu.CompilerParams(vmem_limit_bytes=48 * 1024 * 1024),
    )(query, key, value, query_pos, key_pos, attended, log_total, grad)


def rotate_rows(values, cosine, sine):
    half_dim = values.shape[-1] // 2
    turned = jnp.concatenate([-values[:, half_dim:], values[:, :half_dim]], -1)
    return values * cosine + turned * sine


def high_low(values):
    high = values.astype(jnp.bfloat16)
    return high, (values - high.astype(jnp.float32)).astype(jnp.bfloat16)


def split_shards(
    tokens,
    span_order,
    w_query,
    key_matrix,
    value_matrix,
    w_output,
    w_gate,
    w_up,
    w_down,
    norm_gains,
    head_gains,
    cotangent,
):
    low, wide = jnp.bfloat16, jnp.float32
    dp_size, seq_size = lax.axis_size("dp"), lax.axis_size("seq")
    row_count, width = tokens.shape
    head_dim = head_gains.shape[1]
    kv_heads = key_matrix.shape[1] // head_dim
    groups = w_query.shape[1] // key_matrix.shape[1]
    own_heads = kv_heads // dp_size
    pair_cols = groups * head_dim
    query_cols, key_cols = own_heads * pair_cols, own_heads * head_dim
    unit_cols = w_gate.shape[1] // dp_size
    weight_rows = w_query.shape[0]
    length = seq_size * row_count
    all_rows = dp_size * row_count
    span_len = row_count // 2
    seq_index = lax.axis_index("seq")

    def cut(weight):
        return weight.reshape(weight_rows, dp_size, -1).transpose(1, 0, 2)

    gain_cols = jnp.pad(norm_gains.T, ((0, 0), (0, 126)))
    gain_cols = jnp.broadcast_to(gain_cols[None], (dp_size, weight_rows, 128))
    first_part = jnp.concatenate(
        [cut(w_query), cut(key_matrix), cut(value_matrix), cut(w_output.T), gain_cols], -1
    )
    second_part = jnp.concatenate([cut(w_gate), cut(w_up), cut(w_down.T)], -1)

    def over_seq(part):
        part = part.reshape(dp_size * weight_rows, -1)
        return lax.all_gather(part, "seq", axis=0, tiled=True)

    def by_width(gathered):
        split = gathered.reshape(seq_size, dp_size, weight_rows, -1)
        return split.transpose(1, 0, 2, 3).reshape(width, -1)

    first_part = lax.all_to_all(first_part, "dp", 0, 0, tiled=True)
    first_part = over_seq(first_part)
    second_part = lax.all_to_all(second_part, "dp", 0, 0, tiled=True)
    first_part, second_part = lax.optimization_barrier((first_part, second_part))
    second_part = over_seq(second_part)
    first_part = by_width(first_part)
    qkv_cols = query_cols + 2 * key_cols
    w_qkv = first_part[:, :qkv_cols]
    wo_turned = first_part[:, qkv_cols : qkv_cols + query_cols]
    gains = first_part[:, qkv_cols + query_cols :][:, :2].T.astype(wide)

    all_tokens = dp_gather(tokens).reshape(all_rows, width)
    orders = dp_gather(span_order[0])
    own_slots = lax.dynamic_slice(orders, (0, 2 * seq_index), (dp_size, 2))
    offsets = jnp.arange(span_len, dtype=jnp.int32)
    row_pos = (own_slots[:, :, None] * span_len + offsets).reshape(all_rows)
    cosine, sine = rope_tables(row_pos, head_dim)
    gains_head = head_gains.astype(wide)
    inputs = tokens.astype(wide)
    all_inputs = all_tokens.astype(wide)
    inverse = lax.rsqrt(jnp.mean(all_inputs * all_inputs, axis=-1, keepdims=True) + eps_model)
    all_scaled = all_inputs * inverse
    normed_low = (all_scaled * gains[0]).astype(low)
    qkv_pre = jnp.dot(normed_low, w_qkv, preferred_element_type=wide)

    def prepare(flat, gain):
        return rotate_rows(rms_scale(flat, gain), cosine, sine)

    def head_of(array, start, n):
        return array[:, start + n * head_dim : start + (n + 1) * head_dim]

    query_rot, query_back, key_rot, key_back = [], [], [], []
    for n in range(own_heads * groups):
        rotated, back = jax.vjp(prepare, head_of(qkv_pre, 0, n), gains_head[0])
        query_rot.append(rotated.astype(low))
        query_back.append(back)
    for n in range(own_heads):
        rotated, back = jax.vjp(prepare, head_of(qkv_pre, query_cols, n), gains_head[1])
        key_rot.append(rotated.astype(low))
        key_back.append(back)
    value_low = qkv_pre[:, query_cols + key_cols :].astype(low)

    def to_pairs(by_head):
        stacked = jnp.stack([a.reshape(dp_size, row_count, -1) for a in by_head], 1)
        return stacked.reshape(seq_size, row_count, -1)

    def from_pairs(array):
        split = array.reshape(dp_size, own_heads, row_count, -1)
        return [split[:, n].reshape(all_rows, -1) for n in range(own_heads)]

    pairs = to_seq(
        to_pairs(
            [
                jnp.concatenate(
                    query_rot[n * groups : (n + 1) * groups]
                    + [key_rot[n], head_of(value_low, 0, n)],
                    -1,
                )
                for n in range(own_heads)
            ]
        )
    ).reshape(length, -1)

    def heads_down(array):
        return jnp.concatenate([head_of(array, 0, n) for n in range(groups)], 0)

    def heads_across(array):
        return jnp.concatenate([array[n * length : (n + 1) * length] for n in range(groups)], 1)

    pair_query = heads_down(pairs[:, :pair_cols])
    pair_key = pairs[:, pair_cols : pair_cols + head_dim]
    pair_value = pairs[:, pair_cols + head_dim :]
    pair_order = lax.dynamic_index_in_dim(orders, seq_index // own_heads, 0, keepdims=False)
    pair_pos = (pair_order[:, None] * span_len + offsets).reshape(length)
    query_pos = jnp.concatenate([pair_pos] * groups)[:, None]
    key_pos = pair_pos[None, :]
    attended, attended_low, log_total = attend(pair_query, pair_key, pair_value, query_pos, key_pos)
    back_to_rows = to_seq(heads_across(attended_low).reshape(seq_size, row_count, pair_cols))
    all_attended = jnp.concatenate(from_pairs(back_to_rows), -1)
    partial = contract_cols(all_attended, wo_turned).reshape(dp_size, row_count, width)
    middle = inputs + dp_scatter(partial)

    second_part = by_width(second_part)
    w_gate_up = second_part[:, : 2 * unit_cols]
    wd_turned = second_part[:, 2 * unit_cols :]
    normed_two, norm_two_back = jax.vjp(rms_scale, middle, gains[1])
    normed_two_low = dp_gather(normed_two.astype(low)).reshape(all_rows, width)
    all_cotangent = dp_gather(cotangent).reshape(all_rows, width)
    gate_up = jnp.dot(normed_two_low, w_gate_up, preferred_element_type=wide)
    hidden, swiglu_back = jax.vjp(swiglu, gate_up[:, :unit_cols], gate_up[:, unit_cols:])
    hidden_low = hidden.astype(low)
    grad_hidden = jnp.dot(all_cotangent, wd_turned, preferred_element_type=wide)
    grad_gate, grad_up = swiglu_back(grad_hidden)
    gate_up_low = jnp.concatenate([grad_gate.astype(low), grad_up.astype(low)], -1)
    partial = contract_cols(gate_up_low, w_gate_up).reshape(dp_size, row_count, width)
    grad_middle_norm, grad_gain_two = norm_two_back(dp_scatter(partial))
    grad_middle = cotangent.astype(wide) + grad_middle_norm
    middle_low = dp_gather(grad_middle.astype(low)).reshape(all_rows, width)
    partial = contract_cols(hidden_low, wd_turned).reshape(dp_size, row_count, width)
    output = middle + dp_scatter(partial)
    grad_att = jnp.dot(middle_low, wo_turned, preferred_element_type=wide).astype(low)
    pair_grad = to_seq(
        to_pairs([grad_att[:, n * pair_cols : (n + 1) * pair_cols] for n in range(own_heads)])
    ).reshape(length, pair_cols)

    second_grads = jnp.concatenate(
        [
            contract_rows(normed_two_low, gate_up_low).astype(low),
            contract_rows(all_cotangent, hidden_low).astype(low),
            contract_rows(middle_low, all_attended).astype(low),
        ],
        -1,
    )
    second_grads = second_grads.reshape(dp_size, seq_size, weight_rows, -1).transpose(1, 0, 2, 3)
    second_grads = second_grads.reshape(width, -1)
    second_grads = lax.psum_scatter(second_grads, "seq", scatter_dimension=0, tiled=True)
    second_grads = second_grads.reshape(dp_size, weight_rows, -1)
    second_grads = lax.all_to_all(second_grads, "dp", 0, 0, tiled=True)

    grad_query, grad_key, grad_value = attend_back(
        pair_query,
        pair_key,
        pair_value,
        query_pos,
        key_pos,
        attended,
        log_total,
        heads_down(pair_grad),
    )
    grad_pairs = jnp.concatenate(
        [heads_across(grad_query.astype(low)), grad_key.astype(low), grad_value.astype(low)], -1
    )
    grad_pairs = from_pairs(to_seq(grad_pairs.reshape(seq_size, row_count, -1)))
    grad_query_pre, grad_key_pre, grad_value_low = [], [], []
    gain_query, gain_key = 0.0, 0.0
    for n in range(own_heads):
        for g in range(groups):
            turned = head_of(grad_pairs[n], 0, g).astype(wide)
            before, gain = query_back[n * groups + g](turned)
            grad_query_pre.append(before.astype(low))
            gain_query = gain_query + gain
        before, gain = key_back[n](head_of(grad_pairs[n], pair_cols, 0).astype(wide))
        grad_key_pre.append(before.astype(low))
        gain_key = gain_key + gain
        grad_value_low.append(grad_pairs[n][:, pair_cols + head_dim :])
    grad_qkv = jnp.concatenate(grad_query_pre + grad_key_pre + grad_value_low, -1)
    first_grads = contract_rows(normed_low, grad_qkv).astype(low)
    partial = contract_cols(grad_qkv, w_qkv)
    grad_gain_one = jnp.sum(partial * all_scaled, axis=0)
    grad_normed = dp_scatter(partial.reshape(dp_size, row_count, width))
    _, norm_back = jax.vjp(lambda values: rms_scale(values, gains[0]), inputs)
    grad_input = grad_middle + norm_back(grad_normed)[0]

    devices = dp_size * seq_size
    blocks = qkv_cols // 128
    first_grads = first_grads.reshape(devices, weight_rows, blocks, 128).transpose(0, 2, 1, 3)
    norm_parts = jnp.stack(
        [
            part.reshape(devices, weight_rows)
            for gain in (grad_gain_one, grad_gain_two)
            for part in high_low(gain)
        ],
        1,
    ).reshape(devices, -1, 128)
    head_parts = jnp.stack([part for gain in (gain_query, gain_key) for part in high_low(gain)])
    head_parts = jnp.broadcast_to(head_parts[None], (devices,) + head_parts.shape)
    gain_parts = jnp.concatenate([norm_parts, head_parts], 1)
    gain_rows = gain_parts.shape[1]
    gain_parts = jnp.pad(gain_parts, ((0, 0), (0, -gain_rows % 16), (0, 0)))
    sent = jnp.concatenate([first_grads.reshape(devices, -1, 128), gain_parts], 1)
    taken = lax.all_to_all(sent, ("dp", "seq"), 0, 0, tiled=True)
    split_at = blocks * weight_rows
    gain_parts = jnp.sum(taken[:, split_at : split_at + gain_rows].astype(wide), 0)
    norm_rows = gain_rows - 4
    grad_norm = gain_parts[:norm_rows].reshape(2, 2, weight_rows).sum(1)
    grad_head = gain_parts[norm_rows:].reshape(2, 2, head_dim).sum(1)
    first_grads = taken[:, :split_at].reshape(dp_size, seq_size, blocks, weight_rows, 128)
    first_grads = jnp.sum(first_grads.astype(wide), 1)

    def joined(start, cols):
        part = first_grads[:, start // 128 : (start + cols) // 128]
        return part.transpose(2, 0, 1, 3).reshape(weight_rows, -1)

    def joined_second(start, cols):
        part = second_grads[:, :, start : start + cols].astype(wide)
        return part.transpose(1, 0, 2).reshape(weight_rows, -1)

    return (
        output.astype(low),
        grad_input.astype(low),
        joined(0, query_cols),
        joined(query_cols, key_cols),
        joined(query_cols + key_cols, key_cols),
        joined_second(3 * unit_cols, query_cols).T,
        joined_second(0, unit_cols),
        joined_second(unit_cols, unit_cols),
        joined_second(2 * unit_cols, unit_cols).T,
        grad_norm,
        grad_head,
    )


def solution(mesh):
    sizes = dict(mesh.shape)

    def layer(*arrays):
        query_cols, key_cols = arrays[2].shape[1], arrays[3].shape[1]
        kv_heads = key_cols // arrays[10].shape[1]
        dp, seq = sizes["dp"], sizes["seq"]
        fits = dp & (dp - 1) == 0 and kv_heads % dp == 0 and kv_heads == seq
        fits = fits and arrays[6].shape[1] % (128 * dp) == 0
        return mapped(split_shards if fits else shards, mesh)(*arrays)

    return layer


def mapped(function, mesh):
    return jax.shard_map(
        function,
        mesh=mesh,
        in_specs=(
            P(("dp", "seq"), None),
            P("dp", None),
            P(("dp", "seq"), None),
            P(("dp", "seq"), None),
            P(("dp", "seq"), None),
            P(None, ("dp", "seq")),
            P(("dp", "seq"), None),
            P(("dp", "seq"), None),
            P(None, ("dp", "seq")),
            P(None, ("dp", "seq")),
            P(),
            P(("dp", "seq"), None),
        ),
        out_specs=(
            P(("dp", "seq"), None),
            P(("dp", "seq"), None),
            P(("dp", "seq"), None),
            P(("dp", "seq"), None),
            P(("dp", "seq"), None),
            P(None, ("dp", "seq")),
            P(("dp", "seq"), None),
            P(("dp", "seq"), None),
            P(None, ("dp", "seq")),
            P(None, ("dp", "seq")),
            P(),
        ),
        check_vma=False,
    )
```

```python
import math

import jax
import jax.numpy as jnp
from jax import lax
from jax.experimental import pallas as pl
from jax.experimental.pallas import tpu as pltpu
from jax.sharding import PartitionSpec as P

eps_model = 1e-06
rope_base = 1000000.0
masked_value = -1e30


def passed_along(array, axis, by):
    length = lax.axis_size(axis)
    return lax.ppermute(array, axis, [(i, (i + by) % length) for i in range(length)])


def rms_scale(values, gain):
    inverse = lax.rsqrt(jnp.mean(values * values, axis=-1, keepdims=True) + eps_model)
    return values * inverse * gain


def rope_tables(positions, head_dim):
    half_dim = head_dim // 2
    freqs = rope_base ** (-(jnp.arange(half_dim, dtype=jnp.float32) * 2.0) / head_dim)
    angles = positions.astype(jnp.float32)[:, None] * freqs[None, :]
    cosine = jnp.cos(angles)
    sine = jnp.sin(angles)
    return (jnp.concatenate([cosine, cosine], -1), jnp.concatenate([sine, sine], -1))


def rotate(values, cosine, sine):
    half_dim = values.shape[-1] // 2
    turned = jnp.concatenate([-values[..., half_dim:], values[..., :half_dim]], -1)
    return values * cosine[:, None, :] + turned * sine[:, None, :]


def head_prep(flat, gain, cosine, sine):
    row_count = flat.shape[0]
    shaped = flat.reshape(row_count, -1, gain.shape[0])
    return rotate(rms_scale(shaped, gain), cosine, sine).reshape(row_count, -1)


def span_positions(order_row, start, count, span_len):
    row_index = start + jnp.arange(count, dtype=jnp.int32)
    slot_index = row_index // span_len
    table = (
        slot_index[:, None] == jnp.arange(order_row.shape[0], dtype=jnp.int32)[None, :]
    ).astype(jnp.int32)
    return jnp.sum(table * order_row[None, :], axis=1) * span_len + row_index % span_len


def block_size(count):
    return count if count <= 512 else math.gcd(count, 512)


def contract_rows(left, right):
    return lax.dot_general(
        left, right, (((0,), (0,)), ((), ())), preferred_element_type=jnp.float32
    )


def contract_cols(left, right):
    return lax.dot_general(
        left, right, (((1,), (1,)), ((), ())), preferred_element_type=jnp.float32
    )


def forward_block(state, query_heads, query_pos, key_block, value_block, key_pos, head_dim):
    run_max, run_total, accum = state
    kv_heads = key_block.shape[1] // head_dim
    key_heads = key_block.reshape(-1, kv_heads, head_dim)
    value_heads = value_block.reshape(-1, kv_heads, head_dim)
    scores = jnp.einsum(
        "tkgd,skd->kgts", query_heads, key_heads, preferred_element_type=jnp.float32
    ) * head_dim ** (-0.5)
    allowed = key_pos[None, :] <= query_pos[:, None]
    scores = jnp.where(allowed, scores, masked_value)
    new_max = jnp.maximum(run_max, jnp.max(scores, axis=-1))
    probs = jnp.where(allowed, jnp.exp(scores - new_max[..., None]), 0.0)
    factor = jnp.exp(run_max - new_max)
    new_total = run_total * factor + jnp.sum(probs, axis=-1)
    accum = accum * factor[..., None] + jnp.einsum(
        "kgts,skd->kgtd",
        probs.astype(jnp.bfloat16),
        value_heads,
        preferred_element_type=jnp.float32,
    )
    return (new_max, new_total, accum)


def backward_block(
    query_heads, grad_heads, log_total, delta, query_pos, key_block, value_block, key_pos, head_dim
):
    kv_heads = key_block.shape[1] // head_dim
    key_heads = key_block.reshape(-1, kv_heads, head_dim)
    value_heads = value_block.reshape(-1, kv_heads, head_dim)
    scale = head_dim ** (-0.5)
    scores = (
        jnp.einsum("tkgd,skd->kgts", query_heads, key_heads, preferred_element_type=jnp.float32)
        * scale
    )
    allowed = key_pos[None, :] <= query_pos[:, None]
    probs = jnp.where(allowed, jnp.exp(scores - log_total[..., None]), 0.0)
    grad_value = jnp.einsum(
        "kgts,tkgd->skd", probs.astype(jnp.bfloat16), grad_heads, preferred_element_type=jnp.float32
    )
    grad_probs = jnp.einsum(
        "tkgd,skd->kgts", grad_heads, value_heads, preferred_element_type=jnp.float32
    )
    grad_scores = (probs * (grad_probs - delta[..., None])).astype(jnp.bfloat16)
    grad_query = (
        jnp.einsum("kgts,skd->tkgd", grad_scores, key_heads, preferred_element_type=jnp.float32)
        * scale
    )
    grad_key = (
        jnp.einsum("kgts,tkgd->skd", grad_scores, query_heads, preferred_element_type=jnp.float32)
        * scale
    )
    count = key_block.shape[0]
    return (
        grad_query,
        jnp.concatenate([grad_key.reshape(count, -1), grad_value.reshape(count, -1)], 1),
    )


def swiglu(gate, up_proj):
    return jax.nn.silu(gate) * up_proj


def shards(
    tokens,
    span_order,
    w_query,
    key_matrix,
    value_matrix,
    w_output,
    w_gate,
    w_up,
    w_down,
    norm_gains,
    head_gains,
    cotangent,
):
    row_count = tokens.shape[0]
    span_len = row_count // 2
    head_dim = head_gains.shape[1]
    kv_heads = key_matrix.shape[1] // head_dim
    groups = w_query.shape[1] // key_matrix.shape[1]
    order_row = span_order[0]
    seq_devices = lax.axis_size("seq")
    seq_index = lax.axis_index("seq")
    own_start = seq_index * row_count

    def positions_of(start, count):
        return span_positions(order_row, start, count, span_len)

    query_pos = positions_of(own_start, row_count)
    cosine, sine = rope_tables(query_pos, head_dim)
    gains_head = head_gains.astype(jnp.float32)

    def prepare(flat, gain):
        return head_prep(flat, gain, cosine, sine)

    wq_full, wk_full, wv_full, wo_full, gains_full = (
        lax.all_gather(w_query, ("dp", "seq"), axis=0, tiled=True),
        lax.all_gather(key_matrix, ("dp", "seq"), axis=0, tiled=True),
        lax.all_gather(value_matrix, ("dp", "seq"), axis=0, tiled=True),
        lax.all_gather(w_output, ("dp", "seq"), axis=1, tiled=True),
        lax.all_gather(norm_gains, ("dp", "seq"), axis=1, tiled=True),
    )
    gains_full = gains_full.astype(jnp.float32)
    inputs = tokens.astype(jnp.float32)
    normed, norm_back = jax.vjp(rms_scale, inputs, gains_full[0])
    normed_low = normed.astype(jnp.bfloat16)
    query_pre = jnp.dot(normed_low, wq_full, preferred_element_type=jnp.float32)
    key_pre = jnp.dot(normed_low, wk_full, preferred_element_type=jnp.float32)
    value_low = jnp.dot(normed_low, wv_full, preferred_element_type=jnp.float32).astype(
        jnp.bfloat16
    )
    query_rot, query_back = jax.vjp(prepare, query_pre, gains_head[0])
    key_rot, key_back = jax.vjp(prepare, key_pre, gains_head[1])
    query_heads = query_rot.astype(jnp.bfloat16).reshape(row_count, kv_heads, groups, head_dim)
    key_low = key_rot.astype(jnp.bfloat16)
    latest = jnp.max(query_pos)
    start_state = (
        jnp.full((kv_heads, groups, row_count), masked_value, jnp.float32),
        jnp.zeros((kv_heads, groups, row_count), jnp.float32),
        jnp.zeros((kv_heads, groups, row_count, head_dim), jnp.float32),
    )
    state = start_state
    key_piece = lax.all_gather(key_low, "seq", axis=0, tiled=True)
    value_piece = lax.all_gather(value_low, "seq", axis=0, tiled=True)
    count = key_piece.shape[0]
    size = block_size(count)
    number = count // size
    key_blocks = key_piece.reshape(number, size, key_piece.shape[1])
    value_blocks = value_piece.reshape(number, size, value_piece.shape[1])

    def attend_one_block(carried, item):
        index, key_block, value_block = item
        key_pos = positions_of(index * size, size)

        def attend_compute(inner):
            return forward_block(
                inner, query_heads, query_pos, key_block, value_block, key_pos, head_dim
            )

        def attend_unchanged(inner):
            return inner

        return (
            lax.cond(jnp.min(key_pos) <= latest, attend_compute, attend_unchanged, carried),
            None,
        )

    state, _ = lax.scan(
        attend_one_block, state, (jnp.arange(number, dtype=jnp.int32), key_blocks, value_blocks)
    )
    final_max, final_total, accum = state
    attended_heads = (accum / final_total[..., None]).transpose(2, 0, 1, 3)
    attention_output = attended_heads.reshape(row_count, -1)
    log_total = final_max + jnp.log(final_total)
    attended_low = attention_output.astype(jnp.bfloat16)
    middle = inputs + jnp.dot(attended_low, wo_full, preferred_element_type=jnp.float32)
    wg_full, wu_full, wd_full = (
        lax.all_gather(w_gate, ("dp", "seq"), axis=0, tiled=True),
        lax.all_gather(w_up, ("dp", "seq"), axis=0, tiled=True),
        lax.all_gather(w_down, ("dp", "seq"), axis=1, tiled=True),
    )
    normed_two, norm_two_back = jax.vjp(rms_scale, middle, gains_full[1])
    normed_two_low = normed_two.astype(jnp.bfloat16)
    gate = jnp.dot(normed_two_low, wg_full, preferred_element_type=jnp.float32)
    up_proj = jnp.dot(normed_two_low, wu_full, preferred_element_type=jnp.float32)
    hidden, swiglu_back = jax.vjp(swiglu, gate, up_proj)
    hidden_low = hidden.astype(jnp.bfloat16)
    output = middle + jnp.dot(hidden_low, wd_full, preferred_element_type=jnp.float32)
    grad_out = cotangent.astype(jnp.float32)
    wg_full, wu_full, wd_full = (
        lax.all_gather(w_gate, ("dp", "seq"), axis=0, tiled=True),
        lax.all_gather(w_up, ("dp", "seq"), axis=0, tiled=True),
        lax.all_gather(w_down, ("dp", "seq"), axis=1, tiled=True),
    )
    grad_down_turned = contract_rows(cotangent, hidden_low)
    grad_hidden = contract_cols(cotangent, wd_full)
    grad_gate, grad_up = swiglu_back(grad_hidden)
    gate_low = grad_gate.astype(jnp.bfloat16)
    up_low = grad_up.astype(jnp.bfloat16)
    grad_wg = contract_rows(normed_two_low, gate_low)
    grad_wu = contract_rows(normed_two_low, up_low)
    grad_normed_two = contract_cols(gate_low, wg_full) + contract_cols(up_low, wu_full)
    grad_middle_norm, grad_gain_two = norm_two_back(grad_normed_two)
    feed_grads = (
        lax.psum_scatter(grad_wg, ("dp", "seq"), scatter_dimension=0, tiled=True),
        lax.psum_scatter(grad_wu, ("dp", "seq"), scatter_dimension=0, tiled=True),
        lax.psum_scatter(grad_down_turned, ("dp", "seq"), scatter_dimension=0, tiled=True),
    )
    grad_middle = grad_out + grad_middle_norm
    wq_full, wk_full, wv_full, wo_full = (
        lax.all_gather(w_query, ("dp", "seq"), axis=0, tiled=True),
        lax.all_gather(key_matrix, ("dp", "seq"), axis=0, tiled=True),
        lax.all_gather(value_matrix, ("dp", "seq"), axis=0, tiled=True),
        lax.all_gather(w_output, ("dp", "seq"), axis=1, tiled=True),
    )
    middle_low = grad_middle.astype(jnp.bfloat16)
    grad_wo_turned = contract_rows(middle_low, attended_low)
    attention_output_gradient = contract_cols(middle_low, wo_full).astype(jnp.bfloat16)
    grad_heads = attention_output_gradient.reshape(row_count, kv_heads, groups, head_dim)
    delta = jnp.sum(grad_heads.astype(jnp.float32) * attended_heads, axis=-1).transpose(1, 2, 0)

    def piece_back(grad_query_all, key_piece, value_piece, start):
        count = key_piece.shape[0]
        size = block_size(count)
        number = count // size
        key_blocks = key_piece.reshape(number, size, key_piece.shape[1])
        value_blocks = value_piece.reshape(number, size, value_piece.shape[1])

        def piece_one_block(grad_query_run, item):
            index, key_block, value_block = item
            key_pos = positions_of(start + index * size, size)

            def piece_compute(inner):
                grad_query, grad_kv = backward_block(
                    query_heads,
                    grad_heads,
                    log_total,
                    delta,
                    query_pos,
                    key_block,
                    value_block,
                    key_pos,
                    head_dim,
                )
                return (inner + grad_query, grad_kv)

            def piece_unchanged(inner):
                return (inner, jnp.zeros((size, 2 * kv_heads * head_dim), jnp.float32))

            return lax.cond(
                jnp.min(key_pos) <= latest, piece_compute, piece_unchanged, grad_query_run
            )

        grad_query_all, stacked = lax.scan(
            piece_one_block,
            grad_query_all,
            (jnp.arange(number, dtype=jnp.int32), key_blocks, value_blocks),
        )
        return (grad_query_all, stacked.reshape(count, -1))

    start_query = jnp.zeros((row_count, kv_heads, groups, head_dim), jnp.float32)

    def cycle_step(step, carried):
        grad_query_all, key_piece, value_piece, partial_value = carried
        source = (seq_index - step + seq_devices) % seq_devices
        grad_query_all, local_kv = piece_back(
            grad_query_all, key_piece, value_piece, source * row_count
        )
        partial_value = partial_value + local_kv
        key_piece, value_piece = passed_along((key_piece, value_piece), "seq", 1)
        partial_value = passed_along(partial_value.astype(jnp.bfloat16), "seq", 1).astype(
            partial_value.dtype
        )
        return (grad_query_all, key_piece, value_piece, partial_value)

    initial_cycle_step = (
        start_query,
        key_low,
        value_low,
        jnp.zeros((row_count, 2 * kv_heads * head_dim), jnp.float32),
    )
    grad_query_rot, _, _, grad_kv = lax.fori_loop(0, seq_devices, cycle_step, initial_cycle_step)
    split_at = kv_heads * head_dim
    grad_query_pre, grad_gain_query = query_back(grad_query_rot.reshape(row_count, -1))
    grad_key_pre, grad_gain_key = key_back(grad_kv[:, :split_at])
    query_grad_low = grad_query_pre.astype(jnp.bfloat16)
    key_grad_low = grad_key_pre.astype(jnp.bfloat16)
    value_grad_low = grad_kv[:, split_at:].astype(jnp.bfloat16)
    grad_wq = contract_rows(normed_low, query_grad_low)
    grad_wk = contract_rows(normed_low, key_grad_low)
    grad_wv = contract_rows(normed_low, value_grad_low)
    grad_normed = (
        contract_cols(query_grad_low, wq_full)
        + contract_cols(key_grad_low, wk_full)
        + contract_cols(value_grad_low, wv_full)
    )
    grad_input_norm, grad_gain_one = norm_back(grad_normed)
    grad_input = grad_middle + grad_input_norm
    gains_turned = jnp.stack([grad_gain_one, grad_gain_two], axis=1)
    attention_grads = (
        lax.psum_scatter(grad_wq, ("dp", "seq"), scatter_dimension=0, tiled=True),
        lax.psum_scatter(grad_wk, ("dp", "seq"), scatter_dimension=0, tiled=True),
        lax.psum_scatter(grad_wv, ("dp", "seq"), scatter_dimension=0, tiled=True),
        lax.psum_scatter(grad_wo_turned, ("dp", "seq"), scatter_dimension=0, tiled=True),
        lax.psum_scatter(gains_turned, ("dp", "seq"), scatter_dimension=0, tiled=True),
    )
    head_grads = lax.psum(jnp.stack([grad_gain_query, grad_gain_key]), ("dp", "seq"))
    return (
        output.astype(jnp.bfloat16),
        grad_input.astype(jnp.bfloat16),
        attention_grads[0],
        attention_grads[1],
        attention_grads[2],
        attention_grads[3].T,
        feed_grads[0],
        feed_grads[1],
        feed_grads[2].T,
        attention_grads[4].T,
        head_grads,
    )


def swapped(array, axis, by):
    return lax.ppermute(array, axis, [(i, i ^ by) for i in range(lax.axis_size(axis))])


def over_dp(array):
    return lax.all_to_all(array, "dp", 0, 0, tiled=True)


def gathered(array, axis):
    return lax.all_gather(array, axis, axis=0, tiled=True)


def summed(array, axis):
    return lax.psum_scatter(array, axis, scatter_dimension=0, tiled=True)


def gather_seq(rows):
    count, place = lax.axis_size("seq"), lax.axis_index("seq")
    row_count = rows.shape[0]
    blocks = [rows, None]
    for n in range(2, count, 2):
        blocks += [swapped(rows, "seq", n), None]
    for n in range(0, count, 2):
        blocks[n + 1] = swapped(blocks[n], "seq", 1)
    held = jnp.zeros((count * row_count,) + rows.shape[1:], rows.dtype)
    for n, block in enumerate(blocks):
        held = lax.dynamic_update_slice_in_dim(held, block, (place ^ n) * row_count, 0)
    return held


def scatter_seq(partial):
    low, wide = jnp.bfloat16, jnp.float32
    count, place = lax.axis_size("seq"), lax.axis_index("seq")
    row_count = partial.shape[0] // count

    def block(n):
        return lax.dynamic_slice_in_dim(partial, (place ^ n) * row_count, row_count)

    order = list(reversed(range(0, count, 2)))
    arrived = [swapped(block(n + 1).astype(low), "seq", 1) for n in order]
    sums = []
    for k, n in enumerate(order):
        if k:
            held = lax.optimization_barrier((arrived[k], *sums[-2:]))
            arrived[k], sums[-2:] = held[0], held[1:]
        pair = block(n) + arrived[k].astype(wide)
        if k:
            sums[-1] = swapped(sums[-1], "seq", order[k - 1])
        sums.append(pair.astype(low) if n else pair)
    total = sums[-1]
    for other in sums[:-1]:
        total = total + other.astype(wide)
    return total


def gather_dp(array):
    size, place = lax.axis_size("dp"), lax.axis_index("dp")
    rows, bit = array.shape[0], size // 2
    held = jnp.zeros((size * rows,) + array.shape[1:], array.dtype)
    blocks, order = array, [0]
    while bit:
        blocks = jnp.concatenate([blocks, swapped(blocks, "dp", bit)], 0)
        order = order + [n ^ bit for n in order]
        bit //= 2
    for k, n in enumerate(order):
        block = blocks[k * rows : (k + 1) * rows]
        held = lax.dynamic_update_slice_in_dim(held, block, (place ^ n) * rows, 0)
    return held


def gather_team(rows):
    bit = lax.axis_size("dp") // 2
    while bit:
        rows = jnp.concatenate([rows, swapped(rows, "dp", bit)], 0)
        bit //= 2
    return rows


def scatter_step(partial, bit):
    half = partial.shape[0] // 2
    other = swapped(partial[half:].astype(jnp.bfloat16), "dp", bit)
    return partial[:half] + other.astype(jnp.float32)


def scatter_rest(partial):
    bit = 2
    while bit < lax.axis_size("dp"):
        partial = scatter_step(partial, bit)
        bit *= 2
    return partial


def sum_row_halves(array, axis, bit):
    mine = ((lax.axis_index(axis) & bit) != 0).astype(jnp.int32)
    half = array.shape[0] // 2
    other = lax.dynamic_slice_in_dim(array, (1 - mine) * half, half).astype(jnp.bfloat16)
    kept = lax.dynamic_slice_in_dim(array, mine * half, half)
    return kept.astype(jnp.float32) + swapped(other, axis, bit).astype(jnp.float32)


def to_seq(array):
    return lax.all_to_all(array, "seq", 0, 0, tiled=True)


def attend_kernel(query_ref, key_ref, value_ref, query_pos_ref, key_pos_ref, out_ref, low_ref, log_ref):
    scale = query_ref.shape[-1] ** (-0.5)
    scores = contract_cols(query_ref[...], key_ref[...]) * scale
    allowed = key_pos_ref[...] <= query_pos_ref[...]
    scores = jnp.where(allowed, scores, masked_value)
    top = jnp.max(scores, axis=-1, keepdims=True)
    weights = jnp.exp(scores - top)
    total = jnp.sum(weights, axis=-1, keepdims=True)
    probs = (weights * (1.0 / total)).astype(jnp.bfloat16)
    attended = jnp.dot(probs, value_ref[...], preferred_element_type=jnp.float32)
    out_ref[...] = attended
    low_ref[...] = attended.astype(jnp.bfloat16)
    log_ref[...] = top + jnp.log(total)


def attend_back_kernel(
    query_ref,
    key_ref,
    value_ref,
    query_pos_ref,
    key_pos_ref,
    out_ref,
    log_ref,
    grad_ref,
    grad_query_ref,
    grad_key_ref,
    grad_value_ref,
):
    @pl.when(pl.program_id(0) == 0)
    def _():
        grad_key_ref[...] = jnp.zeros_like(grad_key_ref)
        grad_value_ref[...] = jnp.zeros_like(grad_value_ref)

    scale = query_ref.shape[-1] ** (-0.5)
    query, key, grad = query_ref[...], key_ref[...], grad_ref[...]
    scores = contract_cols(query, key) * scale
    allowed = key_pos_ref[...] <= query_pos_ref[...]
    probs = jnp.where(allowed, jnp.exp(scores - log_ref[...]), 0.0)
    delta = jnp.sum(grad.astype(jnp.float32) * out_ref[...], axis=-1, keepdims=True)
    grad_probs = contract_cols(grad, value_ref[...])
    grad_scores = (probs * (grad_probs - delta)).astype(jnp.bfloat16)
    grad_value_ref[...] += contract_rows(probs.astype(jnp.bfloat16), grad)
    grad_query_ref[...] = jnp.dot(grad_scores, key, preferred_element_type=jnp.float32) * scale
    grad_key_ref[...] += contract_rows(grad_scores, query) * scale


def attend_specs(rows, length, head_dim, block):
    by_rows = pl.BlockSpec((block, head_dim), lambda i: (i, 0))
    by_row = pl.BlockSpec((block, 1), lambda i: (i, 0))
    whole = pl.BlockSpec((length, head_dim), lambda i: (0, 0))
    key_pos = pl.BlockSpec((1, length), lambda i: (0, 0))
    return (rows // block,), by_rows, by_row, whole, key_pos


def attend_cost(rows, length, head_dim, products):
    return pl.CostEstimate(
        flops=2 * products * rows * length * head_dim,
        bytes_accessed=16 * rows * head_dim,
        transcendentals=rows * length,
    )


def attend(query, key, value, query_pos, key_pos):
    rows, head_dim = query.shape
    length = key.shape[0]
    grid, by_rows, by_row, whole, keys = attend_specs(rows, length, head_dim, 512)
    return pl.pallas_call(
        attend_kernel,
        grid=grid,
        in_specs=[by_rows, whole, whole, by_row, keys],
        out_specs=[by_rows, by_rows, by_row],
        out_shape=[
            jax.ShapeDtypeStruct((rows, head_dim), jnp.float32),
            jax.ShapeDtypeStruct((rows, head_dim), jnp.bfloat16),
            jax.ShapeDtypeStruct((rows, 1), jnp.float32),
        ],
        cost_estimate=attend_cost(rows, length, head_dim, 2),
        compiler_params=pltpu.CompilerParams(vmem_limit_bytes=40 * 1024 * 1024),
    )(query, key, value, query_pos, key_pos)


def attend_back(query, key, value, query_pos, key_pos, attended, log_total, grad):
    rows, head_dim = query.shape
    length = key.shape[0]
    grid, by_rows, by_row, whole, keys = attend_specs(rows, length, head_dim, 512)
    return pl.pallas_call(
        attend_back_kernel,
        grid=grid,
        in_specs=[by_rows, whole, whole, by_row, keys, by_rows, by_row, by_rows],
        out_specs=[by_rows, whole, whole],
        out_shape=[
            jax.ShapeDtypeStruct((rows, head_dim), jnp.float32),
            jax.ShapeDtypeStruct((length, head_dim), jnp.float32),
            jax.ShapeDtypeStruct((length, head_dim), jnp.float32),
        ],
        cost_estimate=attend_cost(rows, length, head_dim, 5),
        compiler_params=pltpu.CompilerParams(vmem_limit_bytes=48 * 1024 * 1024),
    )(query, key, value, query_pos, key_pos, attended, log_total, grad)


def rotate_rows(values, cosine, sine):
    half_dim = values.shape[-1] // 2
    turned = jnp.concatenate([-values[:, half_dim:], values[:, :half_dim]], -1)
    return values * cosine + turned * sine


def split_shards(
    tokens,
    span_order,
    w_query,
    key_matrix,
    value_matrix,
    w_output,
    w_gate,
    w_up,
    w_down,
    norm_gains,
    head_gains,
    cotangent,
):
    low, wide = jnp.bfloat16, jnp.float32
    dp_size, seq_size = lax.axis_size("dp"), lax.axis_size("seq")
    row_count, width = tokens.shape
    head_dim = head_gains.shape[1]
    groups = w_query.shape[1] // key_matrix.shape[1]
    pair_cols = groups * head_dim
    qkv_cols = pair_cols + 2 * head_dim
    unit_cols = w_gate.shape[1] // dp_size
    weight_rows = w_query.shape[0]
    length = seq_size * row_count
    span_len = row_count // 2
    seq_index = lax.axis_index("seq")

    seq_tokens = gathered(tokens, "seq")
    cotangent, tokens = lax.optimization_barrier((cotangent, tokens))

    def cut(weight, parts):
        return weight.reshape(weight_rows, parts, -1).transpose(1, 0, 2)

    gain_cols = jnp.pad(norm_gains.T, ((0, 0), (0, 126)))
    gain_cols = jnp.broadcast_to(gain_cols[None], (seq_size, weight_rows, 128))
    first_part = [cut(w, seq_size) for w in (w_query, key_matrix, value_matrix, w_output.T)]
    first_part = to_seq(jnp.concatenate(first_part + [gain_cols], -1))
    first_part = first_part.reshape(seq_size * weight_rows, -1)
    first_part = gather_dp(first_part)
    team_cotangent = gather_team(cotangent)
    first_part, w_gate, w_up, w_down = lax.optimization_barrier((first_part, w_gate, w_up, w_down))
    second_part = jnp.concatenate([cut(w, dp_size) for w in (w_gate, w_up, w_down.T)], -1)
    second_part = over_dp(second_part).reshape(dp_size * weight_rows, -1)
    seq_tokens, second_part = lax.optimization_barrier((seq_tokens, second_part))
    second_part = gathered(second_part, "seq").reshape(seq_size, dp_size, weight_rows, -1)
    second_part = second_part.transpose(1, 0, 2, 3).reshape(width, -1)
    w_gate_up = second_part[:, : 2 * unit_cols]
    wd_turned = second_part[:, 2 * unit_cols :]
    w_qkv = first_part[:, :qkv_cols]
    wo_turned = first_part[:, qkv_cols : qkv_cols + pair_cols]
    gains = first_part[:, qkv_cols + pair_cols :][:, :2].T.astype(wide)
    offsets = jnp.arange(span_len, dtype=jnp.int32)
    positions = (span_order[0][:, None] * span_len + offsets).reshape(length)
    cosine, sine = rope_tables(positions, head_dim)
    gains_head = head_gains.astype(wide)
    inputs = tokens.astype(wide)
    seq_inputs = seq_tokens.astype(wide)
    inverse = lax.rsqrt(jnp.mean(seq_inputs * seq_inputs, axis=-1, keepdims=True) + eps_model)
    seq_scaled = seq_inputs * inverse
    normed_low = (seq_scaled * gains[0]).astype(low)
    qkv_pre = jnp.dot(normed_low, w_qkv, preferred_element_type=wide)

    def prepare(flat, gain):
        return rotate_rows(rms_scale(flat, gain), cosine, sine)

    def head_of(array, n):
        return array[:, n * head_dim : (n + 1) * head_dim]

    query_rot, query_back = [], []
    for n in range(groups):
        rotated, back = jax.vjp(prepare, head_of(qkv_pre, n), gains_head[0])
        query_rot.append(rotated.astype(low))
        query_back.append(back)
    key_rot, key_back = jax.vjp(prepare, head_of(qkv_pre, groups), gains_head[1])
    key_low = key_rot.astype(low)
    value_low = head_of(qkv_pre, groups + 1).astype(low)
    query_low = jnp.concatenate(query_rot, 0)

    def heads_down(array):
        return jnp.concatenate([head_of(array, n) for n in range(groups)], 0)

    def heads_across(array):
        return jnp.concatenate([array[n * length : (n + 1) * length] for n in range(groups)], 1)

    query_pos = jnp.concatenate([positions] * groups)[:, None]
    key_pos = positions[None, :]
    attended, attended_low, log_total = attend(query_low, key_low, value_low, query_pos, key_pos)
    attended_low = heads_across(attended_low)
    middle = inputs + scatter_seq(contract_cols(attended_low, wo_turned))

    normed_two, norm_two_back = jax.vjp(rms_scale, middle, gains[1])
    normed_two_low = gather_team(normed_two.astype(low))
    gate_up = jnp.dot(normed_two_low, w_gate_up, preferred_element_type=wide)
    hidden, swiglu_back = jax.vjp(swiglu, gate_up[:, :unit_cols], gate_up[:, unit_cols:])
    hidden_low = hidden.astype(low)
    grad_hidden = jnp.dot(team_cotangent, wd_turned, preferred_element_type=wide)
    grad_gate, grad_up = swiglu_back(grad_hidden)
    gate_up_low = jnp.concatenate([grad_gate.astype(low), grad_up.astype(low)], -1)
    partial = contract_cols(gate_up_low, w_gate_up)
    partial, normed_two_low, gate_up_low = lax.optimization_barrier(
        (partial, normed_two_low, gate_up_low)
    )
    second_grads = jnp.concatenate(
        [contract_rows(normed_two_low, gate_up_low), contract_rows(team_cotangent, hidden_low)], -1
    ).astype(low)
    second_grads = second_grads.reshape(dp_size, seq_size, weight_rows, -1)
    second_grads = second_grads.transpose(1, 0, 2, 3).reshape(width, -1)
    partial = scatter_step(partial, 1)
    partial, second_grads = lax.optimization_barrier((partial, second_grads))
    second_grads = summed(second_grads, "seq")
    grad_middle_norm, grad_gain_two = norm_two_back(scatter_rest(partial))
    grad_middle = cotangent.astype(wide) + grad_middle_norm
    middle_low = gather_seq(grad_middle.astype(low))
    out_partial = contract_cols(hidden_low, wd_turned)
    out_partial, middle_low = lax.optimization_barrier((out_partial, middle_low))
    out_partial = scatter_step(out_partial, 1)

    grad_att = jnp.dot(middle_low, wo_turned, preferred_element_type=wide).astype(low)
    grad_att, out_partial = lax.optimization_barrier((grad_att, out_partial))
    output = middle + scatter_rest(out_partial)
    grad_query, grad_key, grad_value = attend_back(
        query_low,
        key_low,
        value_low,
        query_pos,
        key_pos,
        attended,
        log_total,
        heads_down(grad_att),
    )
    grad_query, grad_key, grad_value, output = lax.optimization_barrier(
        (grad_query, grad_key, grad_value, output)
    )
    grad_qkv, gain_query = [], 0.0
    for n in range(groups):
        before, gain = query_back[n](grad_query[n * length : (n + 1) * length])
        grad_qkv.append(before.astype(low))
        gain_query = gain_query + gain
    before, gain_key = key_back(grad_key)
    grad_qkv = jnp.concatenate(grad_qkv + [before.astype(low), grad_value.astype(low)], -1)
    partial = contract_cols(grad_qkv, w_qkv)
    grad_gain_one = jnp.sum(partial * seq_scaled, axis=0)
    def in_columns(cols):
        return jnp.pad(cols, ((0, 0), (0, 128 - cols.shape[1])))

    seq_rows = seq_size * weight_rows
    head_gain = jnp.stack([gain_query, gain_key], 1)
    head_gain = jnp.pad(head_gain, ((0, seq_rows - head_dim), (0, 0)))
    head_gain = jnp.concatenate([head_gain] * dp_size, 0)
    gain_cols = jnp.concatenate([jnp.stack([grad_gain_one, grad_gain_two], 1), head_gain], 1)
    first_grads = jnp.concatenate(
        [
            contract_rows(normed_low, grad_qkv).astype(low),
            contract_rows(middle_low, attended_low).astype(low),
            in_columns(gain_cols).astype(low),
        ],
        1,
    )
    first_grads, partial = lax.optimization_barrier((first_grads, partial))
    bit = dp_size // 2
    while bit:
        first_grads = sum_row_halves(first_grads, "dp", bit)
        bit //= 2
    grad_normed = scatter_seq(partial)
    grad_normed, first_grads, second_grads = lax.optimization_barrier(
        (grad_normed, first_grads.astype(low), second_grads)
    )
    _, norm_back = jax.vjp(lambda values: rms_scale(values, gains[0]), inputs)
    grad_input = grad_middle + norm_back(grad_normed)[0]

    matrix_cols = qkv_cols + pair_cols
    gain_cols = first_grads[:, matrix_cols:]
    head_gain = gain_cols[:head_dim, 2:4].reshape(weight_rows, -1)
    head_width = head_gain.shape[1]
    head_gain = jnp.concatenate([head_gain] * seq_size, 0)
    gain_cols = in_columns(jnp.concatenate([gain_cols[:, :2], head_gain], 1))
    first_grads = jnp.concatenate([first_grads[:, :matrix_cols], gain_cols], 1)
    first_grads = to_seq(first_grads.reshape(seq_size, weight_rows, -1))
    gain_cols = jnp.sum(first_grads[..., matrix_cols:].astype(wide), 0)
    grad_norm = gain_cols[:, :2].T
    grad_head = gain_cols[:, 2 : 2 + head_width].reshape(head_dim, 2).T

    second_grads = over_dp(second_grads.reshape(dp_size, weight_rows, -1))

    def joined(blocks, start, cols):
        parts = [blocks[n, :, start : start + cols] for n in range(blocks.shape[0])]
        return jnp.concatenate(parts, 1).astype(wide)

    return (
        output.astype(low),
        grad_input.astype(low),
        joined(first_grads, 0, pair_cols),
        joined(first_grads, pair_cols, head_dim),
        joined(first_grads, pair_cols + head_dim, head_dim),
        joined(first_grads, qkv_cols, pair_cols).T,
        joined(second_grads, 0, unit_cols),
        joined(second_grads, unit_cols, unit_cols),
        joined(second_grads, 2 * unit_cols, unit_cols).T,
        grad_norm,
        grad_head,
    )


def solution(mesh):
    sizes = dict(mesh.shape)

    def layer(*arrays):
        query_cols, key_cols = arrays[2].shape[1], arrays[3].shape[1]
        kv_heads = key_cols // arrays[10].shape[1]
        dp, seq = sizes["dp"], sizes["seq"]
        fits = dp > 1 and dp & (dp - 1) == 0 and seq & (seq - 1) == 0 and kv_heads == seq
        fits = fits and arrays[6].shape[1] % (128 * dp) == 0
        return mapped(split_shards if fits else shards, mesh)(*arrays)

    return layer


def mapped(function, mesh):
    return jax.shard_map(
        function,
        mesh=mesh,
        in_specs=(
            P(("dp", "seq"), None),
            P("dp", None),
            P(("dp", "seq"), None),
            P(("dp", "seq"), None),
            P(("dp", "seq"), None),
            P(None, ("dp", "seq")),
            P(("dp", "seq"), None),
            P(("dp", "seq"), None),
            P(None, ("dp", "seq")),
            P(None, ("dp", "seq")),
            P(),
            P(("dp", "seq"), None),
        ),
        out_specs=(
            P(("dp", "seq"), None),
            P(("dp", "seq"), None),
            P(("dp", "seq"), None),
            P(("dp", "seq"), None),
            P(("dp", "seq"), None),
            P(None, ("dp", "seq")),
            P(("dp", "seq"), None),
            P(("dp", "seq"), None),
            P(None, ("dp", "seq")),
            P(None, ("dp", "seq")),
            P(),
        ),
        check_vma=False,
    )
```

```python
import functools
import math

import jax
import jax.numpy as jnp
from jax import lax
from jax.experimental import pallas as pl
from jax.experimental.pallas import tpu as pltpu
from jax.sharding import PartitionSpec as P

eps_model = 1e-06
rope_base = 1000000.0
masked_value = -1e30


def passed_along(array, axis, by):
    length = lax.axis_size(axis)
    return lax.ppermute(array, axis, [(i, (i + by) % length) for i in range(length)])


def rms_scale(values, gain):
    inverse = lax.rsqrt(jnp.mean(values * values, axis=-1, keepdims=True) + eps_model)
    return values * inverse * gain


def rope_tables(positions, head_dim):
    half_dim = head_dim // 2
    freqs = rope_base ** (-(jnp.arange(half_dim, dtype=jnp.float32) * 2.0) / head_dim)
    angles = positions.astype(jnp.float32)[:, None] * freqs[None, :]
    cosine = jnp.cos(angles)
    sine = jnp.sin(angles)
    return (jnp.concatenate([cosine, cosine], -1), jnp.concatenate([sine, sine], -1))


def rotate(values, cosine, sine):
    half_dim = values.shape[-1] // 2
    turned = jnp.concatenate([-values[..., half_dim:], values[..., :half_dim]], -1)
    return values * cosine[:, None, :] + turned * sine[:, None, :]


def head_prep(flat, gain, cosine, sine):
    row_count = flat.shape[0]
    shaped = flat.reshape(row_count, -1, gain.shape[0])
    return rotate(rms_scale(shaped, gain), cosine, sine).reshape(row_count, -1)


def span_positions(order_row, start, count, span_len):
    row_index = start + jnp.arange(count, dtype=jnp.int32)
    slot_index = row_index // span_len
    table = (
        slot_index[:, None] == jnp.arange(order_row.shape[0], dtype=jnp.int32)[None, :]
    ).astype(jnp.int32)
    return jnp.sum(table * order_row[None, :], axis=1) * span_len + row_index % span_len


def block_size(count):
    return count if count <= 512 else math.gcd(count, 512)


def contract_rows(left, right):
    return lax.dot_general(
        left, right, (((0,), (0,)), ((), ())), preferred_element_type=jnp.float32
    )


def contract_cols(left, right):
    return lax.dot_general(
        left, right, (((1,), (1,)), ((), ())), preferred_element_type=jnp.float32
    )


def forward_block(state, query_heads, query_pos, key_block, value_block, key_pos, head_dim):
    run_max, run_total, accum = state
    kv_heads = key_block.shape[1] // head_dim
    key_heads = key_block.reshape(-1, kv_heads, head_dim)
    value_heads = value_block.reshape(-1, kv_heads, head_dim)
    scores = jnp.einsum(
        "tkgd,skd->kgts", query_heads, key_heads, preferred_element_type=jnp.float32
    ) * head_dim ** (-0.5)
    allowed = key_pos[None, :] <= query_pos[:, None]
    scores = jnp.where(allowed, scores, masked_value)
    new_max = jnp.maximum(run_max, jnp.max(scores, axis=-1))
    probs = jnp.where(allowed, jnp.exp(scores - new_max[..., None]), 0.0)
    factor = jnp.exp(run_max - new_max)
    new_total = run_total * factor + jnp.sum(probs, axis=-1)
    accum = accum * factor[..., None] + jnp.einsum(
        "kgts,skd->kgtd",
        probs.astype(jnp.bfloat16),
        value_heads,
        preferred_element_type=jnp.float32,
    )
    return (new_max, new_total, accum)


def backward_block(
    query_heads, grad_heads, log_total, delta, query_pos, key_block, value_block, key_pos, head_dim
):
    kv_heads = key_block.shape[1] // head_dim
    key_heads = key_block.reshape(-1, kv_heads, head_dim)
    value_heads = value_block.reshape(-1, kv_heads, head_dim)
    scale = head_dim ** (-0.5)
    scores = (
        jnp.einsum("tkgd,skd->kgts", query_heads, key_heads, preferred_element_type=jnp.float32)
        * scale
    )
    allowed = key_pos[None, :] <= query_pos[:, None]
    probs = jnp.where(allowed, jnp.exp(scores - log_total[..., None]), 0.0)
    grad_value = jnp.einsum(
        "kgts,tkgd->skd", probs.astype(jnp.bfloat16), grad_heads, preferred_element_type=jnp.float32
    )
    grad_probs = jnp.einsum(
        "tkgd,skd->kgts", grad_heads, value_heads, preferred_element_type=jnp.float32
    )
    grad_scores = (probs * (grad_probs - delta[..., None])).astype(jnp.bfloat16)
    grad_query = (
        jnp.einsum("kgts,skd->tkgd", grad_scores, key_heads, preferred_element_type=jnp.float32)
        * scale
    )
    grad_key = (
        jnp.einsum("kgts,tkgd->skd", grad_scores, query_heads, preferred_element_type=jnp.float32)
        * scale
    )
    count = key_block.shape[0]
    return (
        grad_query,
        jnp.concatenate([grad_key.reshape(count, -1), grad_value.reshape(count, -1)], 1),
    )


def swiglu(gate, up_proj):
    return jax.nn.silu(gate) * up_proj


def shards(
    tokens,
    span_order,
    w_query,
    key_matrix,
    value_matrix,
    w_output,
    w_gate,
    w_up,
    w_down,
    norm_gains,
    head_gains,
    cotangent,
):
    row_count = tokens.shape[0]
    span_len = row_count // 2
    head_dim = head_gains.shape[1]
    kv_heads = key_matrix.shape[1] // head_dim
    groups = w_query.shape[1] // key_matrix.shape[1]
    order_row = span_order[0]
    seq_devices = lax.axis_size("seq")
    seq_index = lax.axis_index("seq")
    own_start = seq_index * row_count

    def positions_of(start, count):
        return span_positions(order_row, start, count, span_len)

    query_pos = positions_of(own_start, row_count)
    cosine, sine = rope_tables(query_pos, head_dim)
    gains_head = head_gains.astype(jnp.float32)

    def prepare(flat, gain):
        return head_prep(flat, gain, cosine, sine)

    wq_full, wk_full, wv_full, wo_full, gains_full = (
        lax.all_gather(w_query, ("dp", "seq"), axis=0, tiled=True),
        lax.all_gather(key_matrix, ("dp", "seq"), axis=0, tiled=True),
        lax.all_gather(value_matrix, ("dp", "seq"), axis=0, tiled=True),
        lax.all_gather(w_output, ("dp", "seq"), axis=1, tiled=True),
        lax.all_gather(norm_gains, ("dp", "seq"), axis=1, tiled=True),
    )
    gains_full = gains_full.astype(jnp.float32)
    inputs = tokens.astype(jnp.float32)
    normed, norm_back = jax.vjp(rms_scale, inputs, gains_full[0])
    normed_low = normed.astype(jnp.bfloat16)
    query_pre = jnp.dot(normed_low, wq_full, preferred_element_type=jnp.float32)
    key_pre = jnp.dot(normed_low, wk_full, preferred_element_type=jnp.float32)
    value_low = jnp.dot(normed_low, wv_full, preferred_element_type=jnp.float32).astype(
        jnp.bfloat16
    )
    query_rot, query_back = jax.vjp(prepare, query_pre, gains_head[0])
    key_rot, key_back = jax.vjp(prepare, key_pre, gains_head[1])
    query_heads = query_rot.astype(jnp.bfloat16).reshape(row_count, kv_heads, groups, head_dim)
    key_low = key_rot.astype(jnp.bfloat16)
    latest = jnp.max(query_pos)
    start_state = (
        jnp.full((kv_heads, groups, row_count), masked_value, jnp.float32),
        jnp.zeros((kv_heads, groups, row_count), jnp.float32),
        jnp.zeros((kv_heads, groups, row_count, head_dim), jnp.float32),
    )
    state = start_state
    key_piece = lax.all_gather(key_low, "seq", axis=0, tiled=True)
    value_piece = lax.all_gather(value_low, "seq", axis=0, tiled=True)
    count = key_piece.shape[0]
    size = block_size(count)
    number = count // size
    key_blocks = key_piece.reshape(number, size, key_piece.shape[1])
    value_blocks = value_piece.reshape(number, size, value_piece.shape[1])

    def attend_one_block(carried, item):
        index, key_block, value_block = item
        key_pos = positions_of(index * size, size)

        def attend_compute(inner):
            return forward_block(
                inner, query_heads, query_pos, key_block, value_block, key_pos, head_dim
            )

        def attend_unchanged(inner):
            return inner

        return (
            lax.cond(jnp.min(key_pos) <= latest, attend_compute, attend_unchanged, carried),
            None,
        )

    state, _ = lax.scan(
        attend_one_block, state, (jnp.arange(number, dtype=jnp.int32), key_blocks, value_blocks)
    )
    final_max, final_total, accum = state
    attended_heads = (accum / final_total[..., None]).transpose(2, 0, 1, 3)
    attention_output = attended_heads.reshape(row_count, -1)
    log_total = final_max + jnp.log(final_total)
    attended_low = attention_output.astype(jnp.bfloat16)
    middle = inputs + jnp.dot(attended_low, wo_full, preferred_element_type=jnp.float32)
    wg_full, wu_full, wd_full = (
        lax.all_gather(w_gate, ("dp", "seq"), axis=0, tiled=True),
        lax.all_gather(w_up, ("dp", "seq"), axis=0, tiled=True),
        lax.all_gather(w_down, ("dp", "seq"), axis=1, tiled=True),
    )
    normed_two, norm_two_back = jax.vjp(rms_scale, middle, gains_full[1])
    normed_two_low = normed_two.astype(jnp.bfloat16)
    gate = jnp.dot(normed_two_low, wg_full, preferred_element_type=jnp.float32)
    up_proj = jnp.dot(normed_two_low, wu_full, preferred_element_type=jnp.float32)
    hidden, swiglu_back = jax.vjp(swiglu, gate, up_proj)
    hidden_low = hidden.astype(jnp.bfloat16)
    output = middle + jnp.dot(hidden_low, wd_full, preferred_element_type=jnp.float32)
    grad_out = cotangent.astype(jnp.float32)
    wg_full, wu_full, wd_full = (
        lax.all_gather(w_gate, ("dp", "seq"), axis=0, tiled=True),
        lax.all_gather(w_up, ("dp", "seq"), axis=0, tiled=True),
        lax.all_gather(w_down, ("dp", "seq"), axis=1, tiled=True),
    )
    grad_down_turned = contract_rows(cotangent, hidden_low)
    grad_hidden = contract_cols(cotangent, wd_full)
    grad_gate, grad_up = swiglu_back(grad_hidden)
    gate_low = grad_gate.astype(jnp.bfloat16)
    up_low = grad_up.astype(jnp.bfloat16)
    grad_wg = contract_rows(normed_two_low, gate_low)
    grad_wu = contract_rows(normed_two_low, up_low)
    grad_normed_two = contract_cols(gate_low, wg_full) + contract_cols(up_low, wu_full)
    grad_middle_norm, grad_gain_two = norm_two_back(grad_normed_two)
    feed_grads = (
        lax.psum_scatter(grad_wg, ("dp", "seq"), scatter_dimension=0, tiled=True),
        lax.psum_scatter(grad_wu, ("dp", "seq"), scatter_dimension=0, tiled=True),
        lax.psum_scatter(grad_down_turned, ("dp", "seq"), scatter_dimension=0, tiled=True),
    )
    grad_middle = grad_out + grad_middle_norm
    wq_full, wk_full, wv_full, wo_full = (
        lax.all_gather(w_query, ("dp", "seq"), axis=0, tiled=True),
        lax.all_gather(key_matrix, ("dp", "seq"), axis=0, tiled=True),
        lax.all_gather(value_matrix, ("dp", "seq"), axis=0, tiled=True),
        lax.all_gather(w_output, ("dp", "seq"), axis=1, tiled=True),
    )
    middle_low = grad_middle.astype(jnp.bfloat16)
    grad_wo_turned = contract_rows(middle_low, attended_low)
    attention_output_gradient = contract_cols(middle_low, wo_full).astype(jnp.bfloat16)
    grad_heads = attention_output_gradient.reshape(row_count, kv_heads, groups, head_dim)
    delta = jnp.sum(grad_heads.astype(jnp.float32) * attended_heads, axis=-1).transpose(1, 2, 0)

    def piece_back(grad_query_all, key_piece, value_piece, start):
        count = key_piece.shape[0]
        size = block_size(count)
        number = count // size
        key_blocks = key_piece.reshape(number, size, key_piece.shape[1])
        value_blocks = value_piece.reshape(number, size, value_piece.shape[1])

        def piece_one_block(grad_query_run, item):
            index, key_block, value_block = item
            key_pos = positions_of(start + index * size, size)

            def piece_compute(inner):
                grad_query, grad_kv = backward_block(
                    query_heads,
                    grad_heads,
                    log_total,
                    delta,
                    query_pos,
                    key_block,
                    value_block,
                    key_pos,
                    head_dim,
                )
                return (inner + grad_query, grad_kv)

            def piece_unchanged(inner):
                return (inner, jnp.zeros((size, 2 * kv_heads * head_dim), jnp.float32))

            return lax.cond(
                jnp.min(key_pos) <= latest, piece_compute, piece_unchanged, grad_query_run
            )

        grad_query_all, stacked = lax.scan(
            piece_one_block,
            grad_query_all,
            (jnp.arange(number, dtype=jnp.int32), key_blocks, value_blocks),
        )
        return (grad_query_all, stacked.reshape(count, -1))

    start_query = jnp.zeros((row_count, kv_heads, groups, head_dim), jnp.float32)

    def cycle_step(step, carried):
        grad_query_all, key_piece, value_piece, partial_value = carried
        source = (seq_index - step + seq_devices) % seq_devices
        grad_query_all, local_kv = piece_back(
            grad_query_all, key_piece, value_piece, source * row_count
        )
        partial_value = partial_value + local_kv
        key_piece, value_piece = passed_along((key_piece, value_piece), "seq", 1)
        partial_value = passed_along(partial_value.astype(jnp.bfloat16), "seq", 1).astype(
            partial_value.dtype
        )
        return (grad_query_all, key_piece, value_piece, partial_value)

    initial_cycle_step = (
        start_query,
        key_low,
        value_low,
        jnp.zeros((row_count, 2 * kv_heads * head_dim), jnp.float32),
    )
    grad_query_rot, _, _, grad_kv = lax.fori_loop(0, seq_devices, cycle_step, initial_cycle_step)
    split_at = kv_heads * head_dim
    grad_query_pre, grad_gain_query = query_back(grad_query_rot.reshape(row_count, -1))
    grad_key_pre, grad_gain_key = key_back(grad_kv[:, :split_at])
    query_grad_low = grad_query_pre.astype(jnp.bfloat16)
    key_grad_low = grad_key_pre.astype(jnp.bfloat16)
    value_grad_low = grad_kv[:, split_at:].astype(jnp.bfloat16)
    grad_wq = contract_rows(normed_low, query_grad_low)
    grad_wk = contract_rows(normed_low, key_grad_low)
    grad_wv = contract_rows(normed_low, value_grad_low)
    grad_normed = (
        contract_cols(query_grad_low, wq_full)
        + contract_cols(key_grad_low, wk_full)
        + contract_cols(value_grad_low, wv_full)
    )
    grad_input_norm, grad_gain_one = norm_back(grad_normed)
    grad_input = grad_middle + grad_input_norm
    gains_turned = jnp.stack([grad_gain_one, grad_gain_two], axis=1)
    attention_grads = (
        lax.psum_scatter(grad_wq, ("dp", "seq"), scatter_dimension=0, tiled=True),
        lax.psum_scatter(grad_wk, ("dp", "seq"), scatter_dimension=0, tiled=True),
        lax.psum_scatter(grad_wv, ("dp", "seq"), scatter_dimension=0, tiled=True),
        lax.psum_scatter(grad_wo_turned, ("dp", "seq"), scatter_dimension=0, tiled=True),
        lax.psum_scatter(gains_turned, ("dp", "seq"), scatter_dimension=0, tiled=True),
    )
    head_grads = lax.psum(jnp.stack([grad_gain_query, grad_gain_key]), ("dp", "seq"))
    return (
        output.astype(jnp.bfloat16),
        grad_input.astype(jnp.bfloat16),
        attention_grads[0],
        attention_grads[1],
        attention_grads[2],
        attention_grads[3].T,
        feed_grads[0],
        feed_grads[1],
        feed_grads[2].T,
        attention_grads[4].T,
        head_grads,
    )


def swapped(array, axis, by):
    return lax.ppermute(array, axis, [(i, i ^ by) for i in range(lax.axis_size(axis))])


def over_dp(array):
    return lax.all_to_all(array, "dp", 0, 0, tiled=True)


def gathered(array, axis):
    return lax.all_gather(array, axis, axis=0, tiled=True)


def summed(array, axis):
    return lax.psum_scatter(array, axis, scatter_dimension=0, tiled=True)


def gather_seq(rows, later=None):
    count = lax.axis_size("seq")
    upper = [rows] + [swapped(rows, "seq", n) for n in range(2, count, 2)]
    if later is not None:
        *upper, later = lax.optimization_barrier((*upper, later))
    blocks = []
    for block in upper:
        blocks += [block, swapped(block, "seq", 1)]
    return blocks if later is None else (blocks, later)


def scatter_seq(partial, later=()):
    low, wide = jnp.bfloat16, jnp.float32
    count, place = lax.axis_size("seq"), lax.axis_index("seq")
    row_count = partial.shape[0] // count

    def block(n):
        return lax.dynamic_slice_in_dim(partial, (place ^ n) * row_count, row_count)

    order = list(reversed(range(0, count, 2)))
    arrived = [swapped(block(n + 1).astype(low), "seq", 1) for n in order]
    sums = []
    for k, n in enumerate(order):
        if k:
            held = lax.optimization_barrier((arrived[k], *sums[-2:]))
            arrived[k], sums[-2:] = held[0], held[1:]
        if later and k == len(order) // 2:
            arrived[k], *later = lax.optimization_barrier((arrived[k], *later))
        pair = block(n) + arrived[k].astype(wide)
        if k:
            sums[-1] = swapped(sums[-1], "seq", order[k - 1])
        sums.append(pair.astype(low) if n else pair)
    total = sums[-1]
    for other in sums[:-1]:
        total = total + other.astype(wide)
    return (total, *later) if later else total


def gather_dp(array):
    blocks, bit = {0: array}, lax.axis_size("dp") // 2
    while bit:
        blocks.update({n ^ bit: swapped(block, "dp", bit) for n, block in list(blocks.items())})
        bit //= 2
    return [blocks[n] for n in range(len(blocks))]


def gather_team(rows):
    bit = lax.axis_size("dp") // 2
    while bit:
        rows = jnp.concatenate([rows, swapped(rows, "dp", bit)], 0)
        bit //= 2
    return rows


def scatter_step(partial, bit):
    half = partial.shape[0] // 2
    other = swapped(partial[half:].astype(jnp.bfloat16), "dp", bit)
    return partial[:half] + other.astype(jnp.float32)


def scatter_rest(partial):
    bit = 2
    while bit < lax.axis_size("dp"):
        partial = scatter_step(partial, bit)
        bit *= 2
    return partial


def row_halves(array, axis, bit):
    mine = ((lax.axis_index(axis) & bit) != 0).astype(jnp.int32)
    half = array.shape[0] // 2
    other = lax.dynamic_slice_in_dim(array, (1 - mine) * half, half).astype(jnp.bfloat16)
    kept = lax.dynamic_slice_in_dim(array, mine * half, half)
    return kept, swapped(other, axis, bit)


def to_seq(array):
    return lax.all_to_all(array, "seq", 0, 0, tiled=True)


def attend_kernel(query_ref, key_ref, value_ref, query_pos_ref, key_pos_ref, out_ref, low_ref, log_ref):
    scale = query_ref.shape[-1] ** (-0.5)
    scores = contract_cols(query_ref[...], key_ref[...]) * scale
    allowed = key_pos_ref[...] <= query_pos_ref[...]
    scores = jnp.where(allowed, scores, masked_value)
    top = jnp.max(scores, axis=-1, keepdims=True)
    weights = jnp.exp(scores - top)
    total = jnp.sum(weights, axis=-1, keepdims=True)
    probs = (weights * (1.0 / total)).astype(jnp.bfloat16)
    attended = jnp.dot(probs, value_ref[...], preferred_element_type=jnp.float32)
    out_ref[...] = attended
    low_ref[...] = attended.astype(jnp.bfloat16)
    log_ref[...] = top + jnp.log(total)


def rope_rows(values, cosine, sine):
    return values * cosine + pltpu.roll(values, values.shape[-1] // 2, 1) * sine


def rope_rows_back(grad, cosine, sine):
    return grad * cosine + pltpu.roll(grad * sine, grad.shape[-1] // 2, 1)


def rms_back(grad, values, gain):
    inverse = lax.rsqrt(jnp.mean(values * values, axis=-1, keepdims=True) + eps_model)
    weighted = grad * gain
    shared = inverse * inverse * jnp.mean(weighted * values, axis=-1, keepdims=True)
    gain_grad = jnp.sum(grad * values * inverse, axis=0, keepdims=True)
    return inverse * (weighted - values * shared), gain_grad


def prepare_kernel(groups, parts, place_ref, tokens_ref, *refs):
    weights = refs[:parts]
    cosine_ref, sine_ref, head_gains_ref = refs[parts : parts + 3]
    (matrix_ref, gains_ref, normed_ref, pre_ref, query_ref, key_ref, value_ref) = refs[parts + 3 :]
    part_rows = weights[0].shape[0]
    length, head_dim = tokens_ref.shape[0], head_gains_ref.shape[1]
    qkv_cols = (groups + 2) * head_dim
    for n in range(parts):
        start = pl.multiple_of((place_ref[1] ^ n) * part_rows, part_rows)
        matrix_ref[pl.ds(start, part_rows), :] = weights[n][...]
    matrix_cols = matrix_ref.shape[1]
    gains = matrix_ref[:, matrix_cols - 128 :].astype(jnp.float32).T[:8]
    gains_ref[...] = gains
    step = math.gcd(length, 256)
    for start in range(0, length, step):
        here = slice(start, start + step)
        normed = rms_scale(tokens_ref[here, :].astype(jnp.float32), gains[:1])
        normed_ref[here, :] = normed.astype(jnp.bfloat16)
        pre = jnp.dot(
            normed_ref[here, :], matrix_ref[:, :qkv_cols], preferred_element_type=jnp.float32
        )
        pre_ref[here, :] = pre[:, : qkv_cols - head_dim]
        value_ref[here, :] = pre[:, qkv_cols - head_dim :].astype(jnp.bfloat16)
        cosine, sine = cosine_ref[here, :], sine_ref[here, :]
        for n in range(groups + 1):
            gain = head_gains_ref[(0 if n < groups else 1), :][None]
            head = rms_scale(pre[:, n * head_dim : (n + 1) * head_dim], gain)
            head = rope_rows(head, cosine, sine).astype(jnp.bfloat16)
            if n < groups:
                query_ref[n * length + start : n * length + start + step, :] = head
            else:
                key_ref[here, :] = head


def attend_back_kernel(groups, count, place_ref, *refs):
    blocks = refs[:count]
    (matrix_ref, query_ref, key_ref, value_ref, query_pos_ref, key_pos_ref, out_ref, log_ref) = refs[
        count : count + 8
    ]
    (pre_ref, cosine_ref, sine_ref, head_gains_ref, tokens_ref, normed_ref) = refs[
        count + 8 : count + 14
    ]
    (partial_ref, grads_ref, gain_ref, head_gain_ref) = refs[count + 14 : count + 18]
    middle, grad_qkv, grad_key, grad_value = refs[count + 18 :]
    low, wide = jnp.bfloat16, jnp.float32
    row_count = blocks[0].shape[0]
    length, head_dim = key_ref.shape
    pair_cols = groups * head_dim
    qkv_cols = pair_cols + 2 * head_dim
    scale = head_dim ** (-0.5)
    for n in range(count):
        start = pl.multiple_of((place_ref[0] ^ n) * row_count, row_count)
        middle[pl.ds(start, row_count), :] = blocks[n][...]
    grad_key[...] = jnp.zeros_like(grad_key)
    grad_value[...] = jnp.zeros_like(grad_value)
    key, value = key_ref[...], value_ref[...]
    query_gain, key_gain = head_gains_ref[0, :][None], head_gains_ref[1, :][None]
    gain_query = jnp.zeros((1, head_dim), wide)
    step = 2 * row_count
    for start in range(0, length, step):
        here = slice(start, start + step)
        grad_att = jnp.dot(
            middle[here, :],
            matrix_ref[:, qkv_cols : qkv_cols + pair_cols],
            preferred_element_type=wide,
        ).astype(low)
        allowed = key_pos_ref[...] <= query_pos_ref[here, :]
        for n in range(groups):
            there = slice(n * length + start, n * length + start + step)
            cols = slice(n * head_dim, (n + 1) * head_dim)
            query, grad = query_ref[there, :], grad_att[:, cols]
            scores = contract_cols(query, key) * scale
            probs = jnp.where(allowed, jnp.exp(scores - log_ref[there, :]), 0.0)
            delta = jnp.sum(grad.astype(wide) * out_ref[there, :], axis=-1, keepdims=True)
            grad_scores = (probs * (contract_cols(grad, value) - delta)).astype(low)
            grad_value[...] += contract_rows(probs.astype(low), grad)
            grad_key[...] += contract_rows(grad_scores, query) * scale
            turned = jnp.dot(grad_scores, key, preferred_element_type=wide) * scale
            turned = rope_rows_back(turned, cosine_ref[here, :], sine_ref[here, :])
            before, gain = rms_back(turned, pre_ref[here, cols], query_gain)
            grad_qkv[here, cols] = before.astype(low)
            gain_query = gain_query + gain
    turned = rope_rows_back(grad_key[...], cosine_ref[...], sine_ref[...])
    before, gain_key = rms_back(turned, pre_ref[:, pair_cols : pair_cols + head_dim], key_gain)
    grad_qkv[:, pair_cols : pair_cols + head_dim] = before.astype(low)
    grad_qkv[:, pair_cols + head_dim :] = grad_value[...].astype(low)
    head_gain_ref[0:1, :] = gain_query
    head_gain_ref[1:2, :] = gain_key
    gain_one = jnp.zeros((1, tokens_ref.shape[1]), wide)
    for start in range(0, length, step):
        here = slice(start, start + step)
        partial = contract_cols(grad_qkv[here, :], matrix_ref[:, :qkv_cols])
        partial_ref[here, :] = partial
        rows = tokens_ref[here, :].astype(wide)
        inverse = lax.rsqrt(jnp.mean(rows * rows, axis=-1, keepdims=True) + eps_model)
        gain_one = gain_one + jnp.sum(partial * (rows * inverse), axis=0, keepdims=True)
    gain_ref[0:1, :] = gain_one
    grads_ref[:, :qkv_cols] = contract_rows(normed_ref[...], grad_qkv[...]).astype(low)
    for n in range(groups):
        attended = out_ref[n * length : (n + 1) * length, :].astype(low)
        cols = slice(qkv_cols + n * head_dim, qkv_cols + (n + 1) * head_dim)
        grads_ref[:, cols] = contract_rows(middle[...], attended).astype(low)


def whole_specs(arrays):
    return [pl.BlockSpec(memory_space=pltpu.VMEM) for _ in arrays]


def prepare(place, rows, weights, cosine, sine, head_gains, groups):
    low, wide = jnp.bfloat16, jnp.float32
    length, width = rows.shape
    head_dim = head_gains.shape[1]
    matrix_rows, matrix_cols = len(weights) * weights[0].shape[0], weights[0].shape[1]
    operands = (rows, *weights, cosine, sine, head_gains)
    outs = [
        ((matrix_rows, matrix_cols), low),
        ((8, width), wide),
        ((length, width), low),
        ((length, (groups + 1) * head_dim), wide),
        ((groups * length, head_dim), low),
        ((length, head_dim), low),
        ((length, head_dim), low),
    ]
    return pl.pallas_call(
        functools.partial(prepare_kernel, groups, len(weights)),
        in_specs=[pl.BlockSpec(memory_space=pltpu.SMEM)] + whole_specs(operands),
        out_specs=whole_specs(outs),
        out_shape=[jax.ShapeDtypeStruct(*out) for out in outs],
        compiler_params=pltpu.CompilerParams(vmem_limit_bytes=48 * 1024 * 1024),
    )(place, *operands)


def attend_back(place, blocks, operands, groups):
    low, wide = jnp.bfloat16, jnp.float32
    row_count, width = blocks[0].shape
    length, head_dim = operands[2].shape
    qkv_cols = (groups + 2) * head_dim
    operands = (*blocks, *operands)
    outs = [
        ((length, width), wide),
        ((width, qkv_cols + groups * head_dim), low),
        ((8, width), wide),
        ((8, head_dim), wide),
    ]
    return pl.pallas_call(
        functools.partial(attend_back_kernel, groups, len(blocks)),
        in_specs=[pl.BlockSpec(memory_space=pltpu.SMEM)] + whole_specs(operands),
        out_specs=whole_specs(outs),
        out_shape=[jax.ShapeDtypeStruct(*out) for out in outs],
        scratch_shapes=[
            pltpu.VMEM((length, width), low),
            pltpu.VMEM((length, qkv_cols), low),
            pltpu.VMEM((length, head_dim), wide),
            pltpu.VMEM((length, head_dim), wide),
        ],
        compiler_params=pltpu.CompilerParams(vmem_limit_bytes=56 * 1024 * 1024),
    )(place, *operands)


def attend_specs(rows, length, head_dim, block):
    by_rows = pl.BlockSpec((block, head_dim), lambda i: (i, 0))
    by_row = pl.BlockSpec((block, 1), lambda i: (i, 0))
    whole = pl.BlockSpec((length, head_dim), lambda i: (0, 0))
    key_pos = pl.BlockSpec((1, length), lambda i: (0, 0))
    return (rows // block,), by_rows, by_row, whole, key_pos


def attend_cost(rows, length, head_dim, products):
    return pl.CostEstimate(
        flops=2 * products * rows * length * head_dim,
        bytes_accessed=16 * rows * head_dim,
        transcendentals=rows * length,
    )


def attend(query, key, value, query_pos, key_pos):
    rows, head_dim = query.shape
    length = key.shape[0]
    grid, by_rows, by_row, whole, keys = attend_specs(rows, length, head_dim, 512)
    return pl.pallas_call(
        attend_kernel,
        grid=grid,
        in_specs=[by_rows, whole, whole, by_row, keys],
        out_specs=[by_rows, by_rows, by_row],
        out_shape=[
            jax.ShapeDtypeStruct((rows, head_dim), jnp.float32),
            jax.ShapeDtypeStruct((rows, head_dim), jnp.bfloat16),
            jax.ShapeDtypeStruct((rows, 1), jnp.float32),
        ],
        cost_estimate=attend_cost(rows, length, head_dim, 2),
        compiler_params=pltpu.CompilerParams(vmem_limit_bytes=40 * 1024 * 1024),
    )(query, key, value, query_pos, key_pos)


def split_shards(
    tokens,
    span_order,
    w_query,
    key_matrix,
    value_matrix,
    w_output,
    w_gate,
    w_up,
    w_down,
    norm_gains,
    head_gains,
    cotangent,
):
    low, wide = jnp.bfloat16, jnp.float32
    dp_size, seq_size = lax.axis_size("dp"), lax.axis_size("seq")
    row_count, width = tokens.shape
    head_dim = head_gains.shape[1]
    groups = w_query.shape[1] // key_matrix.shape[1]
    pair_cols = groups * head_dim
    qkv_cols = pair_cols + 2 * head_dim
    unit_cols = w_gate.shape[1] // dp_size
    weight_rows = w_query.shape[0]
    length = seq_size * row_count
    span_len = row_count // 2
    seq_index = lax.axis_index("seq")

    def cut(weight, parts):
        return weight.reshape(weight_rows, parts, -1).transpose(1, 0, 2)

    seq_tokens = gathered(tokens, "seq")
    cotangent, tokens = lax.optimization_barrier((cotangent, tokens))

    gain_cols = jnp.pad(norm_gains.T, ((0, 0), (0, 126)))
    gain_cols = jnp.broadcast_to(gain_cols[None], (seq_size, weight_rows, 128))
    first_part = [cut(w, seq_size) for w in (w_query, key_matrix, value_matrix, w_output.T)]
    first_part = jnp.concatenate(first_part + [gain_cols], -1)
    first_part = to_seq(first_part)
    first_part = first_part.reshape(seq_size * weight_rows, -1)
    first_part = gather_dp(first_part)
    *first_part, w_gate, w_up, w_down = lax.optimization_barrier(
        (*first_part, w_gate, w_up, w_down)
    )
    second_part = jnp.concatenate([cut(w, dp_size) for w in (w_gate, w_up, w_down.T)], -1)
    second_part = over_dp(second_part).reshape(dp_size * weight_rows, -1)
    seq_tokens, second_part = lax.optimization_barrier((seq_tokens, second_part))
    second_part = gathered(second_part, "seq").reshape(seq_size, dp_size, weight_rows, -1)
    second_part = second_part.transpose(1, 0, 2, 3).reshape(width, -1)
    w_gate_up = second_part[:, : 2 * unit_cols]
    wd_turned = second_part[:, 2 * unit_cols :]
    offsets = jnp.arange(span_len, dtype=jnp.int32)
    positions = (span_order[0][:, None] * span_len + offsets).reshape(length)
    cosine, sine = rope_tables(positions, head_dim)
    half_dim = head_dim // 2
    sine = jnp.concatenate([-sine[:, :half_dim], sine[:, half_dim:]], 1)
    gains_head = head_gains.astype(wide)
    inputs = tokens.astype(wide)
    place = jnp.stack([seq_index, lax.axis_index("dp")]).astype(jnp.int32)
    matrix, gains, normed_low, qkv_pre, query_low, key_low, value_low = prepare(
        place, seq_tokens, first_part, cosine, sine, gains_head, groups
    )
    wo_turned = matrix[:, qkv_cols : qkv_cols + pair_cols]

    def heads_across(array):
        return jnp.concatenate([array[n * length : (n + 1) * length] for n in range(groups)], 1)

    query_pos = jnp.concatenate([positions] * groups)[:, None]
    key_pos = positions[None, :]
    attended, attended_low, log_total = attend(query_low, key_low, value_low, query_pos, key_pos)
    middle = inputs + scatter_seq(contract_cols(heads_across(attended_low), wo_turned))

    team_cotangent = gather_team(cotangent)
    normed_two, norm_two_back = jax.vjp(rms_scale, middle, gains[1])
    normed_two_low = gather_team(normed_two.astype(low))
    gate_up = jnp.dot(normed_two_low, w_gate_up, preferred_element_type=wide)
    hidden, swiglu_back = jax.vjp(swiglu, gate_up[:, :unit_cols], gate_up[:, unit_cols:])
    hidden_low = hidden.astype(low)
    grad_hidden = jnp.dot(team_cotangent, wd_turned, preferred_element_type=wide)
    grad_gate, grad_up = swiglu_back(grad_hidden)
    gate_up_low = jnp.concatenate([grad_gate.astype(low), grad_up.astype(low)], -1)
    partial = contract_cols(gate_up_low, w_gate_up)
    partial, normed_two_low, gate_up_low = lax.optimization_barrier(
        (partial, normed_two_low, gate_up_low)
    )
    second_grads = jnp.concatenate(
        [contract_rows(normed_two_low, gate_up_low), contract_rows(team_cotangent, hidden_low)], -1
    ).astype(low)
    second_grads = second_grads.reshape(dp_size, seq_size, weight_rows, -1)
    second_grads = second_grads.transpose(1, 0, 2, 3).reshape(width, -1)
    partial = scatter_step(partial, 1)
    partial, second_grads = lax.optimization_barrier((partial, second_grads))
    second_grads = summed(second_grads, "seq")
    grad_middle_norm, grad_gain_two = norm_two_back(scatter_rest(partial))
    grad_middle = cotangent.astype(wide) + grad_middle_norm
    middle_low = gather_seq(grad_middle.astype(low))
    out_partial = contract_cols(hidden_low, wd_turned)
    out_partial, *middle_low = lax.optimization_barrier((out_partial, *middle_low))
    out_partial = scatter_step(out_partial, 1)

    middle_low[0], out_partial = lax.optimization_barrier((middle_low[0], out_partial))
    output = middle + scatter_rest(out_partial)
    operands = (matrix, query_low, key_low, value_low, query_pos, key_pos, attended, log_total)
    operands = operands + (qkv_pre, cosine, sine, gains_head, seq_tokens, normed_low)
    partial, first_grads, grad_gain_one, head_gain = attend_back(place, middle_low, operands, groups)
    partial, first_grads, output = lax.optimization_barrier((partial, first_grads, output))
    _, norm_back = jax.vjp(lambda values: rms_scale(values, gains[0]), inputs)
    def in_columns(cols):
        return jnp.pad(cols, ((0, 0), (0, 128 - cols.shape[1])))

    seq_rows = seq_size * weight_rows
    head_gain = head_gain[:2].T
    head_gain = jnp.pad(head_gain, ((0, seq_rows - head_dim), (0, 0)))
    head_gain = jnp.concatenate([head_gain] * dp_size, 0)
    gain_cols = jnp.concatenate([jnp.stack([grad_gain_one[0], grad_gain_two], 1), head_gain], 1)
    first_grads = jnp.concatenate([first_grads, in_columns(gain_cols).astype(low)], 1)
    first_grads, partial = lax.optimization_barrier((first_grads, partial))
    first_grads, other = row_halves(first_grads, "dp", dp_size // 2)
    grad_normed, other, second_grads = scatter_seq(partial, (other, second_grads))
    first_grads = first_grads.astype(wide) + other.astype(wide)
    bit = dp_size // 4
    while bit:
        first_grads, other = row_halves(first_grads, "dp", bit)
        first_grads = first_grads.astype(wide) + other.astype(wide)
        bit //= 2
    first_grads = first_grads.astype(low)
    second_grads = over_dp(second_grads.reshape(dp_size, weight_rows, -1))
    _, norm_back = jax.vjp(lambda values: rms_scale(values, gains[0]), inputs)
    grad_input = grad_middle + norm_back(grad_normed)[0]

    matrix_cols = qkv_cols + pair_cols
    gain_cols = first_grads[:, matrix_cols:]
    head_gain = gain_cols[:head_dim, 2:4].reshape(weight_rows, -1)
    head_width = head_gain.shape[1]
    head_gain = jnp.concatenate([head_gain] * seq_size, 0)
    gain_cols = in_columns(jnp.concatenate([gain_cols[:, :2], head_gain], 1))
    first_grads = jnp.concatenate([first_grads[:, :matrix_cols], gain_cols], 1)
    first_grads, second_grads = lax.optimization_barrier((first_grads, second_grads))
    first_grads = to_seq(first_grads.reshape(seq_size, weight_rows, -1))
    gain_cols = jnp.sum(first_grads[..., matrix_cols:].astype(wide), 0)
    grad_norm = gain_cols[:, :2].T
    grad_head = gain_cols[:, 2 : 2 + head_width].reshape(head_dim, 2).T

    def joined(blocks, start, cols):
        parts = [blocks[n, :, start : start + cols] for n in range(blocks.shape[0])]
        return jnp.concatenate(parts, 1).astype(wide)

    return (
        output.astype(low),
        grad_input.astype(low),
        joined(first_grads, 0, pair_cols),
        joined(first_grads, pair_cols, head_dim),
        joined(first_grads, pair_cols + head_dim, head_dim),
        joined(first_grads, qkv_cols, pair_cols).T,
        joined(second_grads, 0, unit_cols),
        joined(second_grads, unit_cols, unit_cols),
        joined(second_grads, 2 * unit_cols, unit_cols).T,
        grad_norm,
        grad_head,
    )


def solution(mesh):
    sizes = dict(mesh.shape)

    def layer(*arrays):
        query_cols, key_cols = arrays[2].shape[1], arrays[3].shape[1]
        kv_heads = key_cols // arrays[10].shape[1]
        dp, seq = sizes["dp"], sizes["seq"]
        fits = dp > 1 and dp & (dp - 1) == 0 and seq & (seq - 1) == 0 and kv_heads == seq
        fits = fits and arrays[6].shape[1] % (128 * dp) == 0
        return mapped(split_shards if fits else shards, mesh)(*arrays)

    return layer


def mapped(function, mesh):
    return jax.shard_map(
        function,
        mesh=mesh,
        in_specs=(
            P(("dp", "seq"), None),
            P("dp", None),
            P(("dp", "seq"), None),
            P(("dp", "seq"), None),
            P(("dp", "seq"), None),
            P(None, ("dp", "seq")),
            P(("dp", "seq"), None),
            P(("dp", "seq"), None),
            P(None, ("dp", "seq")),
            P(None, ("dp", "seq")),
            P(),
            P(("dp", "seq"), None),
        ),
        out_specs=(
            P(("dp", "seq"), None),
            P(("dp", "seq"), None),
            P(("dp", "seq"), None),
            P(("dp", "seq"), None),
            P(("dp", "seq"), None),
            P(None, ("dp", "seq")),
            P(("dp", "seq"), None),
            P(("dp", "seq"), None),
            P(None, ("dp", "seq")),
            P(None, ("dp", "seq")),
            P(),
        ),
        check_vma=False,
    )
```

```python
import functools
import math

import jax
import jax.numpy as jnp
from jax import lax
from jax.experimental import pallas as pl
from jax.experimental.pallas import tpu as pltpu
from jax.sharding import PartitionSpec as P

eps_model = 1e-06
rope_base = 1000000.0
masked_value = -1e30


def passed_along(array, axis, by):
    length = lax.axis_size(axis)
    return lax.ppermute(array, axis, [(i, (i + by) % length) for i in range(length)])


def rms_scale(values, gain):
    inverse = lax.rsqrt(jnp.mean(values * values, axis=-1, keepdims=True) + eps_model)
    return values * inverse * gain


def rope_tables(positions, head_dim):
    half_dim = head_dim // 2
    freqs = rope_base ** (-(jnp.arange(half_dim, dtype=jnp.float32) * 2.0) / head_dim)
    angles = positions.astype(jnp.float32)[:, None] * freqs[None, :]
    cosine = jnp.cos(angles)
    sine = jnp.sin(angles)
    return (jnp.concatenate([cosine, cosine], -1), jnp.concatenate([sine, sine], -1))


def rotate(values, cosine, sine):
    half_dim = values.shape[-1] // 2
    turned = jnp.concatenate([-values[..., half_dim:], values[..., :half_dim]], -1)
    return values * cosine[:, None, :] + turned * sine[:, None, :]


def head_prep(flat, gain, cosine, sine):
    row_count = flat.shape[0]
    shaped = flat.reshape(row_count, -1, gain.shape[0])
    return rotate(rms_scale(shaped, gain), cosine, sine).reshape(row_count, -1)


def span_positions(order_row, start, count, span_len):
    row_index = start + jnp.arange(count, dtype=jnp.int32)
    slot_index = row_index // span_len
    table = (
        slot_index[:, None] == jnp.arange(order_row.shape[0], dtype=jnp.int32)[None, :]
    ).astype(jnp.int32)
    return jnp.sum(table * order_row[None, :], axis=1) * span_len + row_index % span_len


def block_size(count):
    return count if count <= 512 else math.gcd(count, 512)


def contract_rows(left, right):
    return lax.dot_general(
        left, right, (((0,), (0,)), ((), ())), preferred_element_type=jnp.float32
    )


def contract_cols(left, right):
    return lax.dot_general(
        left, right, (((1,), (1,)), ((), ())), preferred_element_type=jnp.float32
    )


def forward_block(state, query_heads, query_pos, key_block, value_block, key_pos, head_dim):
    run_max, run_total, accum = state
    kv_heads = key_block.shape[1] // head_dim
    key_heads = key_block.reshape(-1, kv_heads, head_dim)
    value_heads = value_block.reshape(-1, kv_heads, head_dim)
    scores = jnp.einsum(
        "tkgd,skd->kgts", query_heads, key_heads, preferred_element_type=jnp.float32
    ) * head_dim ** (-0.5)
    allowed = key_pos[None, :] <= query_pos[:, None]
    scores = jnp.where(allowed, scores, masked_value)
    new_max = jnp.maximum(run_max, jnp.max(scores, axis=-1))
    probs = jnp.where(allowed, jnp.exp(scores - new_max[..., None]), 0.0)
    factor = jnp.exp(run_max - new_max)
    new_total = run_total * factor + jnp.sum(probs, axis=-1)
    accum = accum * factor[..., None] + jnp.einsum(
        "kgts,skd->kgtd",
        probs.astype(jnp.bfloat16),
        value_heads,
        preferred_element_type=jnp.float32,
    )
    return (new_max, new_total, accum)


def backward_block(
    query_heads, grad_heads, log_total, delta, query_pos, key_block, value_block, key_pos, head_dim
):
    kv_heads = key_block.shape[1] // head_dim
    key_heads = key_block.reshape(-1, kv_heads, head_dim)
    value_heads = value_block.reshape(-1, kv_heads, head_dim)
    scale = head_dim ** (-0.5)
    scores = (
        jnp.einsum("tkgd,skd->kgts", query_heads, key_heads, preferred_element_type=jnp.float32)
        * scale
    )
    allowed = key_pos[None, :] <= query_pos[:, None]
    probs = jnp.where(allowed, jnp.exp(scores - log_total[..., None]), 0.0)
    grad_value = jnp.einsum(
        "kgts,tkgd->skd", probs.astype(jnp.bfloat16), grad_heads, preferred_element_type=jnp.float32
    )
    grad_probs = jnp.einsum(
        "tkgd,skd->kgts", grad_heads, value_heads, preferred_element_type=jnp.float32
    )
    grad_scores = (probs * (grad_probs - delta[..., None])).astype(jnp.bfloat16)
    grad_query = (
        jnp.einsum("kgts,skd->tkgd", grad_scores, key_heads, preferred_element_type=jnp.float32)
        * scale
    )
    grad_key = (
        jnp.einsum("kgts,tkgd->skd", grad_scores, query_heads, preferred_element_type=jnp.float32)
        * scale
    )
    count = key_block.shape[0]
    return (
        grad_query,
        jnp.concatenate([grad_key.reshape(count, -1), grad_value.reshape(count, -1)], 1),
    )


def swiglu(gate, up_proj):
    return jax.nn.silu(gate) * up_proj


def shards(
    tokens,
    span_order,
    w_query,
    key_matrix,
    value_matrix,
    w_output,
    w_gate,
    w_up,
    w_down,
    norm_gains,
    head_gains,
    cotangent,
):
    row_count = tokens.shape[0]
    span_len = row_count // 2
    head_dim = head_gains.shape[1]
    kv_heads = key_matrix.shape[1] // head_dim
    groups = w_query.shape[1] // key_matrix.shape[1]
    order_row = span_order[0]
    seq_devices = lax.axis_size("seq")
    seq_index = lax.axis_index("seq")
    own_start = seq_index * row_count

    def positions_of(start, count):
        return span_positions(order_row, start, count, span_len)

    query_pos = positions_of(own_start, row_count)
    cosine, sine = rope_tables(query_pos, head_dim)
    gains_head = head_gains.astype(jnp.float32)

    def prepare(flat, gain):
        return head_prep(flat, gain, cosine, sine)

    wq_full, wk_full, wv_full, wo_full, gains_full = (
        lax.all_gather(w_query, ("dp", "seq"), axis=0, tiled=True),
        lax.all_gather(key_matrix, ("dp", "seq"), axis=0, tiled=True),
        lax.all_gather(value_matrix, ("dp", "seq"), axis=0, tiled=True),
        lax.all_gather(w_output, ("dp", "seq"), axis=1, tiled=True),
        lax.all_gather(norm_gains, ("dp", "seq"), axis=1, tiled=True),
    )
    gains_full = gains_full.astype(jnp.float32)
    inputs = tokens.astype(jnp.float32)
    normed, norm_back = jax.vjp(rms_scale, inputs, gains_full[0])
    normed_low = normed.astype(jnp.bfloat16)
    query_pre = jnp.dot(normed_low, wq_full, preferred_element_type=jnp.float32)
    key_pre = jnp.dot(normed_low, wk_full, preferred_element_type=jnp.float32)
    value_low = jnp.dot(normed_low, wv_full, preferred_element_type=jnp.float32).astype(
        jnp.bfloat16
    )
    query_rot, query_back = jax.vjp(prepare, query_pre, gains_head[0])
    key_rot, key_back = jax.vjp(prepare, key_pre, gains_head[1])
    query_heads = query_rot.astype(jnp.bfloat16).reshape(row_count, kv_heads, groups, head_dim)
    key_low = key_rot.astype(jnp.bfloat16)
    latest = jnp.max(query_pos)
    start_state = (
        jnp.full((kv_heads, groups, row_count), masked_value, jnp.float32),
        jnp.zeros((kv_heads, groups, row_count), jnp.float32),
        jnp.zeros((kv_heads, groups, row_count, head_dim), jnp.float32),
    )
    state = start_state
    key_piece = lax.all_gather(key_low, "seq", axis=0, tiled=True)
    value_piece = lax.all_gather(value_low, "seq", axis=0, tiled=True)
    count = key_piece.shape[0]
    size = block_size(count)
    number = count // size
    key_blocks = key_piece.reshape(number, size, key_piece.shape[1])
    value_blocks = value_piece.reshape(number, size, value_piece.shape[1])

    def attend_one_block(carried, item):
        index, key_block, value_block = item
        key_pos = positions_of(index * size, size)

        def attend_compute(inner):
            return forward_block(
                inner, query_heads, query_pos, key_block, value_block, key_pos, head_dim
            )

        def attend_unchanged(inner):
            return inner

        return (
            lax.cond(jnp.min(key_pos) <= latest, attend_compute, attend_unchanged, carried),
            None,
        )

    state, _ = lax.scan(
        attend_one_block, state, (jnp.arange(number, dtype=jnp.int32), key_blocks, value_blocks)
    )
    final_max, final_total, accum = state
    attended_heads = (accum / final_total[..., None]).transpose(2, 0, 1, 3)
    attention_output = attended_heads.reshape(row_count, -1)
    log_total = final_max + jnp.log(final_total)
    attended_low = attention_output.astype(jnp.bfloat16)
    middle = inputs + jnp.dot(attended_low, wo_full, preferred_element_type=jnp.float32)
    wg_full, wu_full, wd_full = (
        lax.all_gather(w_gate, ("dp", "seq"), axis=0, tiled=True),
        lax.all_gather(w_up, ("dp", "seq"), axis=0, tiled=True),
        lax.all_gather(w_down, ("dp", "seq"), axis=1, tiled=True),
    )
    normed_two, norm_two_back = jax.vjp(rms_scale, middle, gains_full[1])
    normed_two_low = normed_two.astype(jnp.bfloat16)
    gate = jnp.dot(normed_two_low, wg_full, preferred_element_type=jnp.float32)
    up_proj = jnp.dot(normed_two_low, wu_full, preferred_element_type=jnp.float32)
    hidden, swiglu_back = jax.vjp(swiglu, gate, up_proj)
    hidden_low = hidden.astype(jnp.bfloat16)
    output = middle + jnp.dot(hidden_low, wd_full, preferred_element_type=jnp.float32)
    grad_out = cotangent.astype(jnp.float32)
    wg_full, wu_full, wd_full = (
        lax.all_gather(w_gate, ("dp", "seq"), axis=0, tiled=True),
        lax.all_gather(w_up, ("dp", "seq"), axis=0, tiled=True),
        lax.all_gather(w_down, ("dp", "seq"), axis=1, tiled=True),
    )
    grad_down_turned = contract_rows(cotangent, hidden_low)
    grad_hidden = contract_cols(cotangent, wd_full)
    grad_gate, grad_up = swiglu_back(grad_hidden)
    gate_low = grad_gate.astype(jnp.bfloat16)
    up_low = grad_up.astype(jnp.bfloat16)
    grad_wg = contract_rows(normed_two_low, gate_low)
    grad_wu = contract_rows(normed_two_low, up_low)
    grad_normed_two = contract_cols(gate_low, wg_full) + contract_cols(up_low, wu_full)
    grad_middle_norm, grad_gain_two = norm_two_back(grad_normed_two)
    feed_grads = (
        lax.psum_scatter(grad_wg, ("dp", "seq"), scatter_dimension=0, tiled=True),
        lax.psum_scatter(grad_wu, ("dp", "seq"), scatter_dimension=0, tiled=True),
        lax.psum_scatter(grad_down_turned, ("dp", "seq"), scatter_dimension=0, tiled=True),
    )
    grad_middle = grad_out + grad_middle_norm
    wq_full, wk_full, wv_full, wo_full = (
        lax.all_gather(w_query, ("dp", "seq"), axis=0, tiled=True),
        lax.all_gather(key_matrix, ("dp", "seq"), axis=0, tiled=True),
        lax.all_gather(value_matrix, ("dp", "seq"), axis=0, tiled=True),
        lax.all_gather(w_output, ("dp", "seq"), axis=1, tiled=True),
    )
    middle_low = grad_middle.astype(jnp.bfloat16)
    grad_wo_turned = contract_rows(middle_low, attended_low)
    attention_output_gradient = contract_cols(middle_low, wo_full).astype(jnp.bfloat16)
    grad_heads = attention_output_gradient.reshape(row_count, kv_heads, groups, head_dim)
    delta = jnp.sum(grad_heads.astype(jnp.float32) * attended_heads, axis=-1).transpose(1, 2, 0)

    def piece_back(grad_query_all, key_piece, value_piece, start):
        count = key_piece.shape[0]
        size = block_size(count)
        number = count // size
        key_blocks = key_piece.reshape(number, size, key_piece.shape[1])
        value_blocks = value_piece.reshape(number, size, value_piece.shape[1])

        def piece_one_block(grad_query_run, item):
            index, key_block, value_block = item
            key_pos = positions_of(start + index * size, size)

            def piece_compute(inner):
                grad_query, grad_kv = backward_block(
                    query_heads,
                    grad_heads,
                    log_total,
                    delta,
                    query_pos,
                    key_block,
                    value_block,
                    key_pos,
                    head_dim,
                )
                return (inner + grad_query, grad_kv)

            def piece_unchanged(inner):
                return (inner, jnp.zeros((size, 2 * kv_heads * head_dim), jnp.float32))

            return lax.cond(
                jnp.min(key_pos) <= latest, piece_compute, piece_unchanged, grad_query_run
            )

        grad_query_all, stacked = lax.scan(
            piece_one_block,
            grad_query_all,
            (jnp.arange(number, dtype=jnp.int32), key_blocks, value_blocks),
        )
        return (grad_query_all, stacked.reshape(count, -1))

    start_query = jnp.zeros((row_count, kv_heads, groups, head_dim), jnp.float32)

    def cycle_step(step, carried):
        grad_query_all, key_piece, value_piece, partial_value = carried
        source = (seq_index - step + seq_devices) % seq_devices
        grad_query_all, local_kv = piece_back(
            grad_query_all, key_piece, value_piece, source * row_count
        )
        partial_value = partial_value + local_kv
        key_piece, value_piece = passed_along((key_piece, value_piece), "seq", 1)
        partial_value = passed_along(partial_value.astype(jnp.bfloat16), "seq", 1).astype(
            partial_value.dtype
        )
        return (grad_query_all, key_piece, value_piece, partial_value)

    initial_cycle_step = (
        start_query,
        key_low,
        value_low,
        jnp.zeros((row_count, 2 * kv_heads * head_dim), jnp.float32),
    )
    grad_query_rot, _, _, grad_kv = lax.fori_loop(0, seq_devices, cycle_step, initial_cycle_step)
    split_at = kv_heads * head_dim
    grad_query_pre, grad_gain_query = query_back(grad_query_rot.reshape(row_count, -1))
    grad_key_pre, grad_gain_key = key_back(grad_kv[:, :split_at])
    query_grad_low = grad_query_pre.astype(jnp.bfloat16)
    key_grad_low = grad_key_pre.astype(jnp.bfloat16)
    value_grad_low = grad_kv[:, split_at:].astype(jnp.bfloat16)
    grad_wq = contract_rows(normed_low, query_grad_low)
    grad_wk = contract_rows(normed_low, key_grad_low)
    grad_wv = contract_rows(normed_low, value_grad_low)
    grad_normed = (
        contract_cols(query_grad_low, wq_full)
        + contract_cols(key_grad_low, wk_full)
        + contract_cols(value_grad_low, wv_full)
    )
    grad_input_norm, grad_gain_one = norm_back(grad_normed)
    grad_input = grad_middle + grad_input_norm
    gains_turned = jnp.stack([grad_gain_one, grad_gain_two], axis=1)
    attention_grads = (
        lax.psum_scatter(grad_wq, ("dp", "seq"), scatter_dimension=0, tiled=True),
        lax.psum_scatter(grad_wk, ("dp", "seq"), scatter_dimension=0, tiled=True),
        lax.psum_scatter(grad_wv, ("dp", "seq"), scatter_dimension=0, tiled=True),
        lax.psum_scatter(grad_wo_turned, ("dp", "seq"), scatter_dimension=0, tiled=True),
        lax.psum_scatter(gains_turned, ("dp", "seq"), scatter_dimension=0, tiled=True),
    )
    head_grads = lax.psum(jnp.stack([grad_gain_query, grad_gain_key]), ("dp", "seq"))
    return (
        output.astype(jnp.bfloat16),
        grad_input.astype(jnp.bfloat16),
        attention_grads[0],
        attention_grads[1],
        attention_grads[2],
        attention_grads[3].T,
        feed_grads[0],
        feed_grads[1],
        feed_grads[2].T,
        attention_grads[4].T,
        head_grads,
    )


def swapped(array, axis, by):
    return lax.ppermute(array, axis, [(i, i ^ by) for i in range(lax.axis_size(axis))])


def over_dp(array):
    return lax.all_to_all(array, "dp", 0, 0, tiled=True)


def gathered(array, axis):
    return lax.all_gather(array, axis, axis=0, tiled=True)


def summed(array, axis):
    return lax.psum_scatter(array, axis, scatter_dimension=0, tiled=True)


def gather_seq(rows, later=None):
    count = lax.axis_size("seq")
    upper = [rows] + [swapped(rows, "seq", n) for n in range(2, count, 2)]
    if later is not None:
        *upper, later = lax.optimization_barrier((*upper, later))
    blocks = []
    for block in upper:
        blocks += [block, swapped(block, "seq", 1)]
    return blocks if later is None else (blocks, later)


def scatter_seq(blocks, later=()):
    low, wide = jnp.bfloat16, jnp.float32
    count = len(blocks)
    order = list(reversed(range(0, count, 2)))
    arrived = [swapped(blocks[n + 1], "seq", 1) for n in order]
    sums = []
    for k, n in enumerate(order):
        if k:
            held = lax.optimization_barrier((arrived[k], *sums[-2:]))
            arrived[k], sums[-2:] = held[0], held[1:]
        if later and k == 1:
            arrived[k], *later = lax.optimization_barrier((arrived[k], *later))
        pair = blocks[n].astype(wide) + arrived[k].astype(wide)
        if k:
            sums[-1] = swapped(sums[-1], "seq", order[k - 1])
        sums.append(pair.astype(low) if n else pair)
    total = sums[-1]
    for other in sums[:-1]:
        total = total + other.astype(wide)
    return (total, *later) if later else total


def gather_dp(array):
    blocks, bit = {0: array}, lax.axis_size("dp") // 2
    while bit:
        blocks.update({n ^ bit: swapped(block, "dp", bit) for n, block in list(blocks.items())})
        bit //= 2
    return [blocks[n] for n in range(len(blocks))]


def gather_team(rows):
    bit = lax.axis_size("dp") // 2
    while bit:
        rows = jnp.concatenate([rows, swapped(rows, "dp", bit)], 0)
        bit //= 2
    return rows


def scatter_step(partial, bit):
    half = partial.shape[0] // 2
    other = swapped(partial[half:].astype(jnp.bfloat16), "dp", bit)
    return partial[:half] + other.astype(jnp.float32)


def scatter_rest(partial):
    bit = 2
    while bit < lax.axis_size("dp"):
        partial = scatter_step(partial, bit)
        bit *= 2
    return partial


def to_seq(array):
    return lax.all_to_all(array, "seq", 0, 0, tiled=True)


def attend_kernel(groups, count, place_ref, *refs):
    query_ref, key_ref, value_ref, query_pos_ref, key_pos_ref, matrix_ref = refs[:6]
    out_ref, log_ref = refs[6:8]
    blocks, partial = refs[8 : 8 + count], refs[8 + count]
    length, head_dim = key_ref.shape
    row_count = length // count
    first_col = (groups + 2) * head_dim
    key, value = key_ref[...], value_ref[...]
    step = 2 * row_count
    for start in range(0, length, step):
        here = slice(start, start + step)
        allowed = key_pos_ref[...] <= query_pos_ref[here, :]
        heads = []
        for n in range(groups):
            there = slice(n * length + start, n * length + start + step)
            scores = contract_cols(query_ref[there, :], key) * head_dim ** (-0.5)
            scores = jnp.where(allowed, scores, masked_value)
            top = jnp.max(scores, axis=-1, keepdims=True)
            weights = jnp.exp(scores - top)
            total = jnp.sum(weights, axis=-1, keepdims=True)
            probs = (weights * (1.0 / total)).astype(jnp.bfloat16)
            attended = jnp.dot(probs, value, preferred_element_type=jnp.float32)
            out_ref[there, :] = attended
            log_ref[there, :] = top + jnp.log(total)
            heads.append(attended.astype(jnp.bfloat16))
        weights = matrix_ref[:, first_col : first_col + groups * head_dim]
        partial[here, :] = contract_cols(jnp.concatenate(heads, 1), weights).astype(jnp.bfloat16)
    for n in range(count):
        start = pl.multiple_of((place_ref[0] ^ n) * row_count, row_count)
        blocks[n][...] = partial[pl.ds(start, row_count), :]


def rope_rows(values, cosine, sine):
    return values * cosine + pltpu.roll(values, values.shape[-1] // 2, 1) * sine


def rope_rows_back(grad, cosine, sine):
    return grad * cosine + pltpu.roll(grad * sine, grad.shape[-1] // 2, 1)


def rms_back(grad, values, gain):
    inverse = lax.rsqrt(jnp.mean(values * values, axis=-1, keepdims=True) + eps_model)
    weighted = grad * gain
    shared = inverse * inverse * jnp.mean(weighted * values, axis=-1, keepdims=True)
    gain_grad = jnp.sum(grad * values * inverse, axis=0, keepdims=True)
    return inverse * (weighted - values * shared), gain_grad


def prepare_kernel(groups, parts, place_ref, tokens_ref, *refs):
    weights = refs[:parts]
    cosine_ref, sine_ref, head_gains_ref = refs[parts : parts + 3]
    (matrix_ref, gains_ref, normed_ref, pre_ref, query_ref, key_ref, value_ref) = refs[parts + 3 :]
    part_rows = weights[0].shape[0]
    length, head_dim = tokens_ref.shape[0], head_gains_ref.shape[1]
    qkv_cols = (groups + 2) * head_dim
    for n in range(parts):
        start = pl.multiple_of((place_ref[1] ^ n) * part_rows, part_rows)
        matrix_ref[pl.ds(start, part_rows), :] = weights[n][...]
    matrix_cols = matrix_ref.shape[1]
    gains = matrix_ref[:, matrix_cols - 128 :].astype(jnp.float32).T[:8]
    gains_ref[...] = gains
    step = math.gcd(length, 256)
    for start in range(0, length, step):
        here = slice(start, start + step)
        normed = rms_scale(tokens_ref[here, :].astype(jnp.float32), gains[:1])
        normed_ref[here, :] = normed.astype(jnp.bfloat16)
        pre = jnp.dot(
            normed_ref[here, :], matrix_ref[:, :qkv_cols], preferred_element_type=jnp.float32
        )
        pre_ref[here, :] = pre[:, : qkv_cols - head_dim]
        value_ref[here, :] = pre[:, qkv_cols - head_dim :].astype(jnp.bfloat16)
        cosine, sine = cosine_ref[here, :], sine_ref[here, :]
        for n in range(groups + 1):
            gain = head_gains_ref[(0 if n < groups else 1), :][None]
            head = rms_scale(pre[:, n * head_dim : (n + 1) * head_dim], gain)
            head = rope_rows(head, cosine, sine).astype(jnp.bfloat16)
            if n < groups:
                query_ref[n * length + start : n * length + start + step, :] = head
            else:
                key_ref[here, :] = head


def attend_back_kernel(groups, count, place_ref, *refs):
    blocks = refs[:count]
    (matrix_ref, query_ref, key_ref, value_ref, query_pos_ref, key_pos_ref, out_ref, log_ref) = refs[
        count : count + 8
    ]
    (pre_ref, cosine_ref, sine_ref, head_gains_ref, tokens_ref, normed_ref) = refs[
        count + 8 : count + 14
    ]
    (grads_ref, gain_ref, head_gain_ref) = refs[count + 14 : count + 17]
    sent = refs[count + 17 : 2 * count + 17]
    middle, grad_qkv, grad_key, grad_value, partials = refs[2 * count + 17 :]
    low, wide = jnp.bfloat16, jnp.float32
    row_count = blocks[0].shape[0]
    length, head_dim = key_ref.shape
    pair_cols = groups * head_dim
    qkv_cols = pair_cols + 2 * head_dim
    scale = head_dim ** (-0.5)
    for n in range(count):
        start = pl.multiple_of((place_ref[0] ^ n) * row_count, row_count)
        middle[pl.ds(start, row_count), :] = blocks[n][...]
    grad_key[...] = jnp.zeros_like(grad_key)
    grad_value[...] = jnp.zeros_like(grad_value)
    key, value = key_ref[...], value_ref[...]
    query_gain, key_gain = head_gains_ref[0, :][None], head_gains_ref[1, :][None]
    gain_query = jnp.zeros((1, head_dim), wide)
    step = 2 * row_count
    for start in range(0, length, step):
        here = slice(start, start + step)
        grad_att = jnp.dot(
            middle[here, :],
            matrix_ref[:, qkv_cols : qkv_cols + pair_cols],
            preferred_element_type=wide,
        ).astype(low)
        allowed = key_pos_ref[...] <= query_pos_ref[here, :]
        for n in range(groups):
            there = slice(n * length + start, n * length + start + step)
            cols = slice(n * head_dim, (n + 1) * head_dim)
            query, grad = query_ref[there, :], grad_att[:, cols]
            scores = contract_cols(query, key) * scale
            probs = jnp.where(allowed, jnp.exp(scores - log_ref[there, :]), 0.0)
            delta = jnp.sum(grad.astype(wide) * out_ref[there, :], axis=-1, keepdims=True)
            grad_scores = (probs * (contract_cols(grad, value) - delta)).astype(low)
            grad_value[...] += contract_rows(probs.astype(low), grad)
            grad_key[...] += contract_rows(grad_scores, query) * scale
            turned = jnp.dot(grad_scores, key, preferred_element_type=wide) * scale
            turned = rope_rows_back(turned, cosine_ref[here, :], sine_ref[here, :])
            before, gain = rms_back(turned, pre_ref[here, cols], query_gain)
            grad_qkv[here, cols] = before.astype(low)
            gain_query = gain_query + gain
    turned = rope_rows_back(grad_key[...], cosine_ref[...], sine_ref[...])
    before, gain_key = rms_back(turned, pre_ref[:, pair_cols : pair_cols + head_dim], key_gain)
    grad_qkv[:, pair_cols : pair_cols + head_dim] = before.astype(low)
    grad_qkv[:, pair_cols + head_dim :] = grad_value[...].astype(low)
    head_gain_ref[0:1, :] = gain_query
    head_gain_ref[1:2, :] = gain_key
    gain_one = jnp.zeros((1, tokens_ref.shape[1]), wide)
    for start in range(0, length, step):
        here = slice(start, start + step)
        partial = contract_cols(grad_qkv[here, :], matrix_ref[:, :qkv_cols])
        partials[here, :] = partial.astype(low)
        rows = tokens_ref[here, :].astype(wide)
        inverse = lax.rsqrt(jnp.mean(rows * rows, axis=-1, keepdims=True) + eps_model)
        gain_one = gain_one + jnp.sum(partial * (rows * inverse), axis=0, keepdims=True)
    gain_ref[0:1, :] = gain_one
    for n in range(count):
        start = pl.multiple_of((place_ref[0] ^ n) * row_count, row_count)
        sent[n][...] = partials[pl.ds(start, row_count), :]
    grads_ref[:, :qkv_cols] = contract_rows(normed_ref[...], grad_qkv[...]).astype(low)
    for n in range(groups):
        attended = out_ref[n * length : (n + 1) * length, :].astype(low)
        cols = slice(qkv_cols + n * head_dim, qkv_cols + (n + 1) * head_dim)
        grads_ref[:, cols] = contract_rows(middle[...], attended).astype(low)


def whole_specs(arrays):
    return [pl.BlockSpec(memory_space=pltpu.VMEM) for _ in arrays]


def prepare(place, rows, weights, cosine, sine, head_gains, groups):
    low, wide = jnp.bfloat16, jnp.float32
    length, width = rows.shape
    head_dim = head_gains.shape[1]
    matrix_rows, matrix_cols = len(weights) * weights[0].shape[0], weights[0].shape[1]
    operands = (rows, *weights, cosine, sine, head_gains)
    outs = [
        ((matrix_rows, matrix_cols), low),
        ((8, width), wide),
        ((length, width), low),
        ((length, (groups + 1) * head_dim), wide),
        ((groups * length, head_dim), low),
        ((length, head_dim), low),
        ((length, head_dim), low),
    ]
    return pl.pallas_call(
        functools.partial(prepare_kernel, groups, len(weights)),
        in_specs=[pl.BlockSpec(memory_space=pltpu.SMEM)] + whole_specs(operands),
        out_specs=whole_specs(outs),
        out_shape=[jax.ShapeDtypeStruct(*out) for out in outs],
        compiler_params=pltpu.CompilerParams(vmem_limit_bytes=48 * 1024 * 1024),
    )(place, *operands)


def attend_back(place, blocks, operands, groups):
    low, wide = jnp.bfloat16, jnp.float32
    row_count, width = blocks[0].shape
    length, head_dim = operands[2].shape
    qkv_cols = (groups + 2) * head_dim
    operands = (*blocks, *operands)
    outs = [
        ((width, qkv_cols + groups * head_dim), low),
        ((8, width), wide),
        ((8, head_dim), wide),
    ] + [((row_count, width), low)] * len(blocks)
    return pl.pallas_call(
        functools.partial(attend_back_kernel, groups, len(blocks)),
        in_specs=[pl.BlockSpec(memory_space=pltpu.SMEM)] + whole_specs(operands),
        out_specs=whole_specs(outs),
        out_shape=[jax.ShapeDtypeStruct(*out) for out in outs],
        scratch_shapes=[
            pltpu.VMEM((length, width), low),
            pltpu.VMEM((length, qkv_cols), low),
            pltpu.VMEM((length, head_dim), wide),
            pltpu.VMEM((length, head_dim), wide),
            pltpu.VMEM((length, width), low),
        ],
        compiler_params=pltpu.CompilerParams(vmem_limit_bytes=56 * 1024 * 1024),
    )(place, *operands)


def attend(place, operands, groups, count):
    low, wide = jnp.bfloat16, jnp.float32
    length, head_dim = operands[1].shape
    width = operands[5].shape[0]
    outs = [((groups * length, head_dim), wide), ((groups * length, 1), wide)]
    outs = outs + [((length // count, width), low)] * count
    return pl.pallas_call(
        functools.partial(attend_kernel, groups, count),
        in_specs=[pl.BlockSpec(memory_space=pltpu.SMEM)] + whole_specs(operands),
        out_specs=whole_specs(outs),
        out_shape=[jax.ShapeDtypeStruct(*out) for out in outs],
        scratch_shapes=[pltpu.VMEM((length, width), low)],
        compiler_params=pltpu.CompilerParams(vmem_limit_bytes=48 * 1024 * 1024),
    )(place, *operands)


def split_shards(
    tokens,
    span_order,
    w_query,
    key_matrix,
    value_matrix,
    w_output,
    w_gate,
    w_up,
    w_down,
    norm_gains,
    head_gains,
    cotangent,
):
    low, wide = jnp.bfloat16, jnp.float32
    dp_size, seq_size = lax.axis_size("dp"), lax.axis_size("seq")
    row_count, width = tokens.shape
    head_dim = head_gains.shape[1]
    groups = w_query.shape[1] // key_matrix.shape[1]
    pair_cols = groups * head_dim
    qkv_cols = pair_cols + 2 * head_dim
    unit_cols = w_gate.shape[1] // dp_size
    weight_rows = w_query.shape[0]
    length = seq_size * row_count
    span_len = row_count // 2
    seq_index = lax.axis_index("seq")

    def cut(weight, parts):
        return weight.reshape(weight_rows, parts, -1).transpose(1, 0, 2)

    seq_tokens = gathered(tokens, "seq")
    cotangent, tokens = lax.optimization_barrier((cotangent, tokens))

    gain_cols = jnp.pad(norm_gains.T, ((0, 0), (0, 126)))
    gain_cols = jnp.broadcast_to(gain_cols[None], (seq_size, weight_rows, 128))
    first_part = [cut(w, seq_size) for w in (w_query, key_matrix, value_matrix, w_output.T)]
    first_part = jnp.concatenate(first_part + [gain_cols], -1)
    first_part = to_seq(first_part)
    first_part = first_part.reshape(seq_size * weight_rows, -1)
    first_part = gather_dp(first_part)
    *first_part, w_gate, w_up, w_down = lax.optimization_barrier(
        (*first_part, w_gate, w_up, w_down)
    )
    second_part = jnp.concatenate([cut(w, dp_size) for w in (w_gate, w_up, w_down.T)], -1)
    second_part = over_dp(second_part).reshape(dp_size * weight_rows, -1)
    seq_tokens, second_part = lax.optimization_barrier((seq_tokens, second_part))
    second_part = gathered(second_part, "seq").reshape(seq_size, dp_size, weight_rows, -1)
    second_part = second_part.transpose(1, 0, 2, 3).reshape(width, -1)
    w_gate_up = second_part[:, : 2 * unit_cols]
    wd_turned = second_part[:, 2 * unit_cols :]
    offsets = jnp.arange(span_len, dtype=jnp.int32)
    positions = (span_order[0][:, None] * span_len + offsets).reshape(length)
    cosine, sine = rope_tables(positions, head_dim)
    half_dim = head_dim // 2
    sine = jnp.concatenate([-sine[:, :half_dim], sine[:, half_dim:]], 1)
    gains_head = head_gains.astype(wide)
    inputs = tokens.astype(wide)
    place = jnp.stack([seq_index, lax.axis_index("dp")]).astype(jnp.int32)
    matrix, gains, normed_low, qkv_pre, query_low, key_low, value_low = prepare(
        place, seq_tokens, first_part, cosine, sine, gains_head, groups
    )

    query_pos = jnp.concatenate([positions] * groups)[:, None]
    key_pos = positions[None, :]
    operands = (query_low, key_low, value_low, query_pos, key_pos, matrix)
    attended, log_total, *blocks = attend(place, operands, groups, seq_size)
    middle = inputs + scatter_seq(blocks)

    team_cotangent = gather_team(cotangent)
    normed_two, norm_two_back = jax.vjp(rms_scale, middle, gains[1])
    normed_two_low = gather_team(normed_two.astype(low))
    gate_up = jnp.dot(normed_two_low, w_gate_up, preferred_element_type=wide)
    hidden, swiglu_back = jax.vjp(swiglu, gate_up[:, :unit_cols], gate_up[:, unit_cols:])
    hidden_low = hidden.astype(low)
    grad_hidden = jnp.dot(team_cotangent, wd_turned, preferred_element_type=wide)
    grad_gate, grad_up = swiglu_back(grad_hidden)
    gate_up_low = jnp.concatenate([grad_gate.astype(low), grad_up.astype(low)], -1)
    partial = contract_cols(gate_up_low, w_gate_up)
    partial, normed_two_low, gate_up_low = lax.optimization_barrier(
        (partial, normed_two_low, gate_up_low)
    )
    second_grads = jnp.concatenate(
        [contract_rows(normed_two_low, gate_up_low), contract_rows(team_cotangent, hidden_low)], -1
    ).astype(low)
    second_grads = second_grads.reshape(dp_size, seq_size, weight_rows, -1)
    second_grads = second_grads.transpose(1, 0, 2, 3).reshape(width, -1)
    partial = scatter_step(partial, 1)
    partial, second_grads = lax.optimization_barrier((partial, second_grads))
    second_grads = summed(second_grads, "seq")
    grad_middle_norm, grad_gain_two = norm_two_back(scatter_rest(partial))
    grad_middle = cotangent.astype(wide) + grad_middle_norm
    middle_low = gather_seq(grad_middle.astype(low))
    out_partial = contract_cols(hidden_low, wd_turned)
    out_partial, *middle_low = lax.optimization_barrier((out_partial, *middle_low))
    out_partial = scatter_step(out_partial, 1)

    middle_low[0], out_partial = lax.optimization_barrier((middle_low[0], out_partial))
    output = middle + scatter_rest(out_partial)
    operands = (matrix, query_low, key_low, value_low, query_pos, key_pos, attended, log_total)
    operands = operands + (qkv_pre, cosine, sine, gains_head, seq_tokens, normed_low)
    first_grads, grad_gain_one, head_gain, *blocks = attend_back(place, middle_low, operands, groups)
    first_grads, output, *blocks = lax.optimization_barrier((first_grads, output, *blocks))
    _, norm_back = jax.vjp(lambda values: rms_scale(values, gains[0]), inputs)
    def in_columns(cols):
        return jnp.pad(cols, ((0, 0), (0, 128 - cols.shape[1])))

    seq_rows = seq_size * weight_rows
    head_gain = head_gain[:2].T
    head_gain = jnp.pad(head_gain, ((0, seq_rows - head_dim), (0, 0)))
    head_gain = jnp.concatenate([head_gain] * dp_size, 0)
    gain_cols = jnp.concatenate([jnp.stack([grad_gain_one[0], grad_gain_two], 1), head_gain], 1)
    first_grads = jnp.concatenate([first_grads, in_columns(gain_cols).astype(low)], 1)
    dp_index = lax.axis_index("dp")

    def rows_for(n):
        return lax.dynamic_slice_in_dim(first_grads, (dp_index ^ n) * seq_rows, seq_rows)

    others = [swapped(rows_for(n), "dp", n) for n in range(1, dp_size)]
    grad_normed, second_grads, *others = scatter_seq(blocks, (second_grads, *others))
    first_grads = rows_for(0).astype(wide)
    for other in others:
        first_grads = first_grads + other.astype(wide)
    first_grads = first_grads.astype(low)
    second_grads = over_dp(second_grads.reshape(dp_size, weight_rows, -1))
    _, norm_back = jax.vjp(lambda values: rms_scale(values, gains[0]), inputs)
    grad_input = grad_middle + norm_back(grad_normed)[0]

    matrix_cols = qkv_cols + pair_cols
    gain_cols = first_grads[:, matrix_cols:]
    head_gain = gain_cols[:head_dim, 2:4].reshape(weight_rows, -1)
    head_width = head_gain.shape[1]
    head_gain = jnp.concatenate([head_gain] * seq_size, 0)
    gain_cols = in_columns(jnp.concatenate([gain_cols[:, :2], head_gain], 1))
    first_grads = jnp.concatenate([first_grads[:, :matrix_cols], gain_cols], 1)
    first_grads, second_grads = lax.optimization_barrier((first_grads, second_grads))
    first_grads = to_seq(first_grads.reshape(seq_size, weight_rows, -1))
    gain_cols = jnp.sum(first_grads[..., matrix_cols:].astype(wide), 0)
    grad_norm = gain_cols[:, :2].T
    grad_head = gain_cols[:, 2 : 2 + head_width].reshape(head_dim, 2).T

    def joined(blocks, start, cols):
        parts = [blocks[n, :, start : start + cols] for n in range(blocks.shape[0])]
        return jnp.concatenate(parts, 1).astype(wide)

    return (
        output.astype(low),
        grad_input.astype(low),
        joined(first_grads, 0, pair_cols),
        joined(first_grads, pair_cols, head_dim),
        joined(first_grads, pair_cols + head_dim, head_dim),
        joined(first_grads, qkv_cols, pair_cols).T,
        joined(second_grads, 0, unit_cols),
        joined(second_grads, unit_cols, unit_cols),
        joined(second_grads, 2 * unit_cols, unit_cols).T,
        grad_norm,
        grad_head,
    )


def solution(mesh):
    sizes = dict(mesh.shape)

    def layer(*arrays):
        query_cols, key_cols = arrays[2].shape[1], arrays[3].shape[1]
        kv_heads = key_cols // arrays[10].shape[1]
        dp, seq = sizes["dp"], sizes["seq"]
        fits = dp > 1 and dp & (dp - 1) == 0 and seq & (seq - 1) == 0 and kv_heads == seq
        fits = fits and arrays[6].shape[1] % (128 * dp) == 0
        return mapped(split_shards if fits else shards, mesh)(*arrays)

    return layer


def mapped(function, mesh):
    return jax.shard_map(
        function,
        mesh=mesh,
        in_specs=(
            P(("dp", "seq"), None),
            P("dp", None),
            P(("dp", "seq"), None),
            P(("dp", "seq"), None),
            P(("dp", "seq"), None),
            P(None, ("dp", "seq")),
            P(("dp", "seq"), None),
            P(("dp", "seq"), None),
            P(None, ("dp", "seq")),
            P(None, ("dp", "seq")),
            P(),
            P(("dp", "seq"), None),
        ),
        out_specs=(
            P(("dp", "seq"), None),
            P(("dp", "seq"), None),
            P(("dp", "seq"), None),
            P(("dp", "seq"), None),
            P(("dp", "seq"), None),
            P(None, ("dp", "seq")),
            P(("dp", "seq"), None),
            P(("dp", "seq"), None),
            P(None, ("dp", "seq")),
            P(None, ("dp", "seq")),
            P(),
        ),
        check_vma=False,
    )
```

```python
import functools
import math

import jax
import jax.numpy as jnp
from jax import lax
from jax.experimental import pallas as pl
from jax.experimental.pallas import tpu as pltpu
from jax.sharding import PartitionSpec as P

eps_model = 1e-06
rope_base = 1000000.0
masked_value = -1e30


def passed_along(array, axis, by):
    length = lax.axis_size(axis)
    return lax.ppermute(array, axis, [(i, (i + by) % length) for i in range(length)])


def rms_scale(values, gain):
    inverse = lax.rsqrt(jnp.mean(values * values, axis=-1, keepdims=True) + eps_model)
    return values * inverse * gain


def rope_tables(positions, head_dim):
    half_dim = head_dim // 2
    freqs = rope_base ** (-(jnp.arange(half_dim, dtype=jnp.float32) * 2.0) / head_dim)
    angles = positions.astype(jnp.float32)[:, None] * freqs[None, :]
    cosine = jnp.cos(angles)
    sine = jnp.sin(angles)
    return (jnp.concatenate([cosine, cosine], -1), jnp.concatenate([sine, sine], -1))


def rotate(values, cosine, sine):
    half_dim = values.shape[-1] // 2
    turned = jnp.concatenate([-values[..., half_dim:], values[..., :half_dim]], -1)
    return values * cosine[:, None, :] + turned * sine[:, None, :]


def head_prep(flat, gain, cosine, sine):
    row_count = flat.shape[0]
    shaped = flat.reshape(row_count, -1, gain.shape[0])
    return rotate(rms_scale(shaped, gain), cosine, sine).reshape(row_count, -1)


def span_positions(order_row, start, count, span_len):
    row_index = start + jnp.arange(count, dtype=jnp.int32)
    slot_index = row_index // span_len
    table = (
        slot_index[:, None] == jnp.arange(order_row.shape[0], dtype=jnp.int32)[None, :]
    ).astype(jnp.int32)
    return jnp.sum(table * order_row[None, :], axis=1) * span_len + row_index % span_len


def block_size(count):
    return count if count <= 512 else math.gcd(count, 512)


def contract_rows(left, right):
    return lax.dot_general(
        left, right, (((0,), (0,)), ((), ())), preferred_element_type=jnp.float32
    )


def contract_cols(left, right):
    return lax.dot_general(
        left, right, (((1,), (1,)), ((), ())), preferred_element_type=jnp.float32
    )


def forward_block(state, query_heads, query_pos, key_block, value_block, key_pos, head_dim):
    run_max, run_total, accum = state
    kv_heads = key_block.shape[1] // head_dim
    key_heads = key_block.reshape(-1, kv_heads, head_dim)
    value_heads = value_block.reshape(-1, kv_heads, head_dim)
    scores = jnp.einsum(
        "tkgd,skd->kgts", query_heads, key_heads, preferred_element_type=jnp.float32
    ) * head_dim ** (-0.5)
    allowed = key_pos[None, :] <= query_pos[:, None]
    scores = jnp.where(allowed, scores, masked_value)
    new_max = jnp.maximum(run_max, jnp.max(scores, axis=-1))
    probs = jnp.where(allowed, jnp.exp(scores - new_max[..., None]), 0.0)
    factor = jnp.exp(run_max - new_max)
    new_total = run_total * factor + jnp.sum(probs, axis=-1)
    accum = accum * factor[..., None] + jnp.einsum(
        "kgts,skd->kgtd",
        probs.astype(jnp.bfloat16),
        value_heads,
        preferred_element_type=jnp.float32,
    )
    return (new_max, new_total, accum)


def backward_block(
    query_heads, grad_heads, log_total, delta, query_pos, key_block, value_block, key_pos, head_dim
):
    kv_heads = key_block.shape[1] // head_dim
    key_heads = key_block.reshape(-1, kv_heads, head_dim)
    value_heads = value_block.reshape(-1, kv_heads, head_dim)
    scale = head_dim ** (-0.5)
    scores = (
        jnp.einsum("tkgd,skd->kgts", query_heads, key_heads, preferred_element_type=jnp.float32)
        * scale
    )
    allowed = key_pos[None, :] <= query_pos[:, None]
    probs = jnp.where(allowed, jnp.exp(scores - log_total[..., None]), 0.0)
    grad_value = jnp.einsum(
        "kgts,tkgd->skd", probs.astype(jnp.bfloat16), grad_heads, preferred_element_type=jnp.float32
    )
    grad_probs = jnp.einsum(
        "tkgd,skd->kgts", grad_heads, value_heads, preferred_element_type=jnp.float32
    )
    grad_scores = (probs * (grad_probs - delta[..., None])).astype(jnp.bfloat16)
    grad_query = (
        jnp.einsum("kgts,skd->tkgd", grad_scores, key_heads, preferred_element_type=jnp.float32)
        * scale
    )
    grad_key = (
        jnp.einsum("kgts,tkgd->skd", grad_scores, query_heads, preferred_element_type=jnp.float32)
        * scale
    )
    count = key_block.shape[0]
    return (
        grad_query,
        jnp.concatenate([grad_key.reshape(count, -1), grad_value.reshape(count, -1)], 1),
    )


def swiglu(gate, up_proj):
    return jax.nn.silu(gate) * up_proj


def shards(
    tokens,
    span_order,
    w_query,
    key_matrix,
    value_matrix,
    w_output,
    w_gate,
    w_up,
    w_down,
    norm_gains,
    head_gains,
    cotangent,
):
    row_count = tokens.shape[0]
    span_len = row_count // 2
    head_dim = head_gains.shape[1]
    kv_heads = key_matrix.shape[1] // head_dim
    groups = w_query.shape[1] // key_matrix.shape[1]
    order_row = span_order[0]
    seq_devices = lax.axis_size("seq")
    seq_index = lax.axis_index("seq")
    own_start = seq_index * row_count

    def positions_of(start, count):
        return span_positions(order_row, start, count, span_len)

    query_pos = positions_of(own_start, row_count)
    cosine, sine = rope_tables(query_pos, head_dim)
    gains_head = head_gains.astype(jnp.float32)

    def prepare(flat, gain):
        return head_prep(flat, gain, cosine, sine)

    wq_full, wk_full, wv_full, wo_full, gains_full = (
        lax.all_gather(w_query, ("dp", "seq"), axis=0, tiled=True),
        lax.all_gather(key_matrix, ("dp", "seq"), axis=0, tiled=True),
        lax.all_gather(value_matrix, ("dp", "seq"), axis=0, tiled=True),
        lax.all_gather(w_output, ("dp", "seq"), axis=1, tiled=True),
        lax.all_gather(norm_gains, ("dp", "seq"), axis=1, tiled=True),
    )
    gains_full = gains_full.astype(jnp.float32)
    inputs = tokens.astype(jnp.float32)
    normed, norm_back = jax.vjp(rms_scale, inputs, gains_full[0])
    normed_low = normed.astype(jnp.bfloat16)
    query_pre = jnp.dot(normed_low, wq_full, preferred_element_type=jnp.float32)
    key_pre = jnp.dot(normed_low, wk_full, preferred_element_type=jnp.float32)
    value_low = jnp.dot(normed_low, wv_full, preferred_element_type=jnp.float32).astype(
        jnp.bfloat16
    )
    query_rot, query_back = jax.vjp(prepare, query_pre, gains_head[0])
    key_rot, key_back = jax.vjp(prepare, key_pre, gains_head[1])
    query_heads = query_rot.astype(jnp.bfloat16).reshape(row_count, kv_heads, groups, head_dim)
    key_low = key_rot.astype(jnp.bfloat16)
    latest = jnp.max(query_pos)
    start_state = (
        jnp.full((kv_heads, groups, row_count), masked_value, jnp.float32),
        jnp.zeros((kv_heads, groups, row_count), jnp.float32),
        jnp.zeros((kv_heads, groups, row_count, head_dim), jnp.float32),
    )
    state = start_state
    key_piece = lax.all_gather(key_low, "seq", axis=0, tiled=True)
    value_piece = lax.all_gather(value_low, "seq", axis=0, tiled=True)
    count = key_piece.shape[0]
    size = block_size(count)
    number = count // size
    key_blocks = key_piece.reshape(number, size, key_piece.shape[1])
    value_blocks = value_piece.reshape(number, size, value_piece.shape[1])

    def attend_one_block(carried, item):
        index, key_block, value_block = item
        key_pos = positions_of(index * size, size)

        def attend_compute(inner):
            return forward_block(
                inner, query_heads, query_pos, key_block, value_block, key_pos, head_dim
            )

        def attend_unchanged(inner):
            return inner

        return (
            lax.cond(jnp.min(key_pos) <= latest, attend_compute, attend_unchanged, carried),
            None,
        )

    state, _ = lax.scan(
        attend_one_block, state, (jnp.arange(number, dtype=jnp.int32), key_blocks, value_blocks)
    )
    final_max, final_total, accum = state
    attended_heads = (accum / final_total[..., None]).transpose(2, 0, 1, 3)
    attention_output = attended_heads.reshape(row_count, -1)
    log_total = final_max + jnp.log(final_total)
    attended_low = attention_output.astype(jnp.bfloat16)
    middle = inputs + jnp.dot(attended_low, wo_full, preferred_element_type=jnp.float32)
    wg_full, wu_full, wd_full = (
        lax.all_gather(w_gate, ("dp", "seq"), axis=0, tiled=True),
        lax.all_gather(w_up, ("dp", "seq"), axis=0, tiled=True),
        lax.all_gather(w_down, ("dp", "seq"), axis=1, tiled=True),
    )
    normed_two, norm_two_back = jax.vjp(rms_scale, middle, gains_full[1])
    normed_two_low = normed_two.astype(jnp.bfloat16)
    gate = jnp.dot(normed_two_low, wg_full, preferred_element_type=jnp.float32)
    up_proj = jnp.dot(normed_two_low, wu_full, preferred_element_type=jnp.float32)
    hidden, swiglu_back = jax.vjp(swiglu, gate, up_proj)
    hidden_low = hidden.astype(jnp.bfloat16)
    output = middle + jnp.dot(hidden_low, wd_full, preferred_element_type=jnp.float32)
    grad_out = cotangent.astype(jnp.float32)
    wg_full, wu_full, wd_full = (
        lax.all_gather(w_gate, ("dp", "seq"), axis=0, tiled=True),
        lax.all_gather(w_up, ("dp", "seq"), axis=0, tiled=True),
        lax.all_gather(w_down, ("dp", "seq"), axis=1, tiled=True),
    )
    grad_down_turned = contract_rows(cotangent, hidden_low)
    grad_hidden = contract_cols(cotangent, wd_full)
    grad_gate, grad_up = swiglu_back(grad_hidden)
    gate_low = grad_gate.astype(jnp.bfloat16)
    up_low = grad_up.astype(jnp.bfloat16)
    grad_wg = contract_rows(normed_two_low, gate_low)
    grad_wu = contract_rows(normed_two_low, up_low)
    grad_normed_two = contract_cols(gate_low, wg_full) + contract_cols(up_low, wu_full)
    grad_middle_norm, grad_gain_two = norm_two_back(grad_normed_two)
    feed_grads = (
        lax.psum_scatter(grad_wg, ("dp", "seq"), scatter_dimension=0, tiled=True),
        lax.psum_scatter(grad_wu, ("dp", "seq"), scatter_dimension=0, tiled=True),
        lax.psum_scatter(grad_down_turned, ("dp", "seq"), scatter_dimension=0, tiled=True),
    )
    grad_middle = grad_out + grad_middle_norm
    wq_full, wk_full, wv_full, wo_full = (
        lax.all_gather(w_query, ("dp", "seq"), axis=0, tiled=True),
        lax.all_gather(key_matrix, ("dp", "seq"), axis=0, tiled=True),
        lax.all_gather(value_matrix, ("dp", "seq"), axis=0, tiled=True),
        lax.all_gather(w_output, ("dp", "seq"), axis=1, tiled=True),
    )
    middle_low = grad_middle.astype(jnp.bfloat16)
    grad_wo_turned = contract_rows(middle_low, attended_low)
    attention_output_gradient = contract_cols(middle_low, wo_full).astype(jnp.bfloat16)
    grad_heads = attention_output_gradient.reshape(row_count, kv_heads, groups, head_dim)
    delta = jnp.sum(grad_heads.astype(jnp.float32) * attended_heads, axis=-1).transpose(1, 2, 0)

    def piece_back(grad_query_all, key_piece, value_piece, start):
        count = key_piece.shape[0]
        size = block_size(count)
        number = count // size
        key_blocks = key_piece.reshape(number, size, key_piece.shape[1])
        value_blocks = value_piece.reshape(number, size, value_piece.shape[1])

        def piece_one_block(grad_query_run, item):
            index, key_block, value_block = item
            key_pos = positions_of(start + index * size, size)

            def piece_compute(inner):
                grad_query, grad_kv = backward_block(
                    query_heads,
                    grad_heads,
                    log_total,
                    delta,
                    query_pos,
                    key_block,
                    value_block,
                    key_pos,
                    head_dim,
                )
                return (inner + grad_query, grad_kv)

            def piece_unchanged(inner):
                return (inner, jnp.zeros((size, 2 * kv_heads * head_dim), jnp.float32))

            return lax.cond(
                jnp.min(key_pos) <= latest, piece_compute, piece_unchanged, grad_query_run
            )

        grad_query_all, stacked = lax.scan(
            piece_one_block,
            grad_query_all,
            (jnp.arange(number, dtype=jnp.int32), key_blocks, value_blocks),
        )
        return (grad_query_all, stacked.reshape(count, -1))

    start_query = jnp.zeros((row_count, kv_heads, groups, head_dim), jnp.float32)

    def cycle_step(step, carried):
        grad_query_all, key_piece, value_piece, partial_value = carried
        source = (seq_index - step + seq_devices) % seq_devices
        grad_query_all, local_kv = piece_back(
            grad_query_all, key_piece, value_piece, source * row_count
        )
        partial_value = partial_value + local_kv
        key_piece, value_piece = passed_along((key_piece, value_piece), "seq", 1)
        partial_value = passed_along(partial_value.astype(jnp.bfloat16), "seq", 1).astype(
            partial_value.dtype
        )
        return (grad_query_all, key_piece, value_piece, partial_value)

    initial_cycle_step = (
        start_query,
        key_low,
        value_low,
        jnp.zeros((row_count, 2 * kv_heads * head_dim), jnp.float32),
    )
    grad_query_rot, _, _, grad_kv = lax.fori_loop(0, seq_devices, cycle_step, initial_cycle_step)
    split_at = kv_heads * head_dim
    grad_query_pre, grad_gain_query = query_back(grad_query_rot.reshape(row_count, -1))
    grad_key_pre, grad_gain_key = key_back(grad_kv[:, :split_at])
    query_grad_low = grad_query_pre.astype(jnp.bfloat16)
    key_grad_low = grad_key_pre.astype(jnp.bfloat16)
    value_grad_low = grad_kv[:, split_at:].astype(jnp.bfloat16)
    grad_wq = contract_rows(normed_low, query_grad_low)
    grad_wk = contract_rows(normed_low, key_grad_low)
    grad_wv = contract_rows(normed_low, value_grad_low)
    grad_normed = (
        contract_cols(query_grad_low, wq_full)
        + contract_cols(key_grad_low, wk_full)
        + contract_cols(value_grad_low, wv_full)
    )
    grad_input_norm, grad_gain_one = norm_back(grad_normed)
    grad_input = grad_middle + grad_input_norm
    gains_turned = jnp.stack([grad_gain_one, grad_gain_two], axis=1)
    attention_grads = (
        lax.psum_scatter(grad_wq, ("dp", "seq"), scatter_dimension=0, tiled=True),
        lax.psum_scatter(grad_wk, ("dp", "seq"), scatter_dimension=0, tiled=True),
        lax.psum_scatter(grad_wv, ("dp", "seq"), scatter_dimension=0, tiled=True),
        lax.psum_scatter(grad_wo_turned, ("dp", "seq"), scatter_dimension=0, tiled=True),
        lax.psum_scatter(gains_turned, ("dp", "seq"), scatter_dimension=0, tiled=True),
    )
    head_grads = lax.psum(jnp.stack([grad_gain_query, grad_gain_key]), ("dp", "seq"))
    return (
        output.astype(jnp.bfloat16),
        grad_input.astype(jnp.bfloat16),
        attention_grads[0],
        attention_grads[1],
        attention_grads[2],
        attention_grads[3].T,
        feed_grads[0],
        feed_grads[1],
        feed_grads[2].T,
        attention_grads[4].T,
        head_grads,
    )


def swapped(array, axis, by):
    return lax.ppermute(array, axis, [(i, i ^ by) for i in range(lax.axis_size(axis))])


def over_dp(array):
    return lax.all_to_all(array, "dp", 0, 0, tiled=True)


def gathered(array, axis):
    return lax.all_gather(array, axis, axis=0, tiled=True)


def summed(array, axis):
    return lax.psum_scatter(array, axis, scatter_dimension=0, tiled=True)


def gather_seq(rows, later=None):
    count = lax.axis_size("seq")
    upper = [rows] + [swapped(rows, "seq", n) for n in range(2, count, 2)]
    if later is not None:
        *upper, later = lax.optimization_barrier((*upper, later))
    blocks = []
    for block in upper:
        blocks += [block, swapped(block, "seq", 1)]
    return blocks if later is None else (blocks, later)


def scatter_seq(blocks, later=()):
    low, wide = jnp.bfloat16, jnp.float32
    count = len(blocks)
    order = list(reversed(range(0, count, 2)))
    arrived = [swapped(blocks[n + 1], "seq", 1) for n in order]
    sums = []
    for k, n in enumerate(order):
        if k:
            kept = sums[-1:] if k == len(order) - 1 else sums[-2:]
            held = lax.optimization_barrier((arrived[k], *kept))
            arrived[k], sums[-len(kept) :] = held[0], held[1:]
        if later and k == 1:
            arrived[k], *later = lax.optimization_barrier((arrived[k], *later))
        pair = blocks[n].astype(wide) + arrived[k].astype(wide)
        if k:
            sums[-1] = swapped(sums[-1], "seq", order[k - 1])
        sums.append(pair.astype(low) if n else pair)
    total = sums[-1]
    for other in sums[:-1]:
        total = total + other.astype(wide)
    return (total, *later) if later else total


def gather_dp(array):
    blocks, bit = {0: array}, lax.axis_size("dp") // 2
    while bit:
        blocks.update({n ^ bit: swapped(block, "dp", bit) for n, block in list(blocks.items())})
        bit //= 2
    return [blocks[n] for n in range(len(blocks))]


def gather_team(rows):
    bit = lax.axis_size("dp") // 2
    while bit:
        rows = jnp.concatenate([rows, swapped(rows, "dp", bit)], 0)
        bit //= 2
    return rows


def scatter_step(partial, bit):
    half = partial.shape[0] // 2
    other = swapped(partial[half:].astype(jnp.bfloat16), "dp", bit)
    return partial[:half] + other.astype(jnp.float32)


def scatter_rest(partial):
    bit = 2
    while bit < lax.axis_size("dp"):
        partial = scatter_step(partial, bit)
        bit *= 2
    return partial


def to_seq(array):
    return lax.all_to_all(array, "seq", 0, 0, tiled=True)


def attend_kernel(groups, count, place_ref, *refs):
    query_ref, key_ref, value_ref, query_pos_ref, key_pos_ref, matrix_ref = refs[:6]
    out_ref, log_ref = refs[6:8]
    blocks, partial = refs[8 : 8 + count], refs[8 + count]
    length, head_dim = key_ref.shape
    row_count = length // count
    first_col = (groups + 2) * head_dim
    key, value = key_ref[...], value_ref[...]
    step = 2 * row_count
    for start in range(0, length, step):
        here = slice(start, start + step)
        allowed = key_pos_ref[...] <= query_pos_ref[here, :]
        heads = []
        for n in range(groups):
            there = slice(n * length + start, n * length + start + step)
            scores = contract_cols(query_ref[there, :], key) * head_dim ** (-0.5)
            scores = jnp.where(allowed, scores, masked_value)
            top = jnp.max(scores, axis=-1, keepdims=True)
            weights = jnp.exp(scores - top)
            total = jnp.sum(weights, axis=-1, keepdims=True)
            probs = (weights * (1.0 / total)).astype(jnp.bfloat16)
            attended = jnp.dot(probs, value, preferred_element_type=jnp.float32)
            out_ref[there, :] = attended
            log_ref[there, :] = top + jnp.log(total)
            heads.append(attended.astype(jnp.bfloat16))
        weights = matrix_ref[:, first_col : first_col + groups * head_dim]
        partial[here, :] = contract_cols(jnp.concatenate(heads, 1), weights).astype(jnp.bfloat16)
    for n in range(count):
        start = pl.multiple_of((place_ref[0] ^ n) * row_count, row_count)
        blocks[n][...] = partial[pl.ds(start, row_count), :]


def rope_rows(values, cosine, sine):
    return values * cosine + pltpu.roll(values, values.shape[-1] // 2, 1) * sine


def rope_rows_back(grad, cosine, sine):
    return grad * cosine + pltpu.roll(grad * sine, grad.shape[-1] // 2, 1)


def rms_back(grad, values, gain):
    inverse = lax.rsqrt(jnp.mean(values * values, axis=-1, keepdims=True) + eps_model)
    weighted = grad * gain
    shared = inverse * inverse * jnp.mean(weighted * values, axis=-1, keepdims=True)
    gain_grad = jnp.sum(grad * values * inverse, axis=0, keepdims=True)
    return inverse * (weighted - values * shared), gain_grad


def prepare_kernel(groups, parts, place_ref, tokens_ref, *refs):
    weights = refs[:parts]
    cosine_ref, sine_ref, head_gains_ref = refs[parts : parts + 3]
    (matrix_ref, gains_ref, normed_ref, pre_ref, query_ref, key_ref, value_ref) = refs[parts + 3 :]
    part_rows = weights[0].shape[0]
    length, head_dim = tokens_ref.shape[0], head_gains_ref.shape[1]
    qkv_cols = (groups + 2) * head_dim
    for n in range(parts):
        start = pl.multiple_of((place_ref[1] ^ n) * part_rows, part_rows)
        matrix_ref[pl.ds(start, part_rows), :] = weights[n][...]
    matrix_cols = matrix_ref.shape[1]
    gains = matrix_ref[:, matrix_cols - 128 :].astype(jnp.float32).T[:8]
    gains_ref[...] = gains
    step = math.gcd(length, 256)
    for start in range(0, length, step):
        here = slice(start, start + step)
        normed = rms_scale(tokens_ref[here, :].astype(jnp.float32), gains[:1])
        normed_ref[here, :] = normed.astype(jnp.bfloat16)
        pre = jnp.dot(
            normed_ref[here, :], matrix_ref[:, :qkv_cols], preferred_element_type=jnp.float32
        )
        pre_ref[here, :] = pre[:, : qkv_cols - head_dim]
        value_ref[here, :] = pre[:, qkv_cols - head_dim :].astype(jnp.bfloat16)
        cosine, sine = cosine_ref[here, :], sine_ref[here, :]
        for n in range(groups + 1):
            gain = head_gains_ref[(0 if n < groups else 1), :][None]
            head = rms_scale(pre[:, n * head_dim : (n + 1) * head_dim], gain)
            head = rope_rows(head, cosine, sine).astype(jnp.bfloat16)
            if n < groups:
                query_ref[n * length + start : n * length + start + step, :] = head
            else:
                key_ref[here, :] = head


def attend_back_kernel(groups, count, place_ref, *refs):
    blocks = refs[:count]
    (matrix_ref, query_ref, key_ref, value_ref, query_pos_ref, key_pos_ref, out_ref, log_ref) = refs[
        count : count + 8
    ]
    (pre_ref, cosine_ref, sine_ref, head_gains_ref, tokens_ref, normed_ref) = refs[
        count + 8 : count + 14
    ]
    (grads_ref, gain_ref, head_gain_ref) = refs[count + 14 : count + 17]
    sent = refs[count + 17 : 2 * count + 17]
    middle, grad_qkv, grad_key, grad_value, partials = refs[2 * count + 17 :]
    low, wide = jnp.bfloat16, jnp.float32
    row_count = blocks[0].shape[0]
    length, head_dim = key_ref.shape
    pair_cols = groups * head_dim
    qkv_cols = pair_cols + 2 * head_dim
    scale = head_dim ** (-0.5)
    for n in range(count):
        start = pl.multiple_of((place_ref[0] ^ n) * row_count, row_count)
        middle[pl.ds(start, row_count), :] = blocks[n][...]
    grad_key[...] = jnp.zeros_like(grad_key)
    grad_value[...] = jnp.zeros_like(grad_value)
    key, value = key_ref[...], value_ref[...]
    query_gain, key_gain = head_gains_ref[0, :][None], head_gains_ref[1, :][None]
    gain_query = jnp.zeros((1, head_dim), wide)
    step = 2 * row_count
    for start in range(0, length, step):
        here = slice(start, start + step)
        grad_att = jnp.dot(
            middle[here, :],
            matrix_ref[:, qkv_cols : qkv_cols + pair_cols],
            preferred_element_type=wide,
        ).astype(low)
        allowed = key_pos_ref[...] <= query_pos_ref[here, :]
        for n in range(groups):
            there = slice(n * length + start, n * length + start + step)
            cols = slice(n * head_dim, (n + 1) * head_dim)
            query, grad = query_ref[there, :], grad_att[:, cols]
            scores = contract_cols(query, key) * scale
            probs = jnp.where(allowed, jnp.exp(scores - log_ref[there, :]), 0.0)
            delta = jnp.sum(grad.astype(wide) * out_ref[there, :], axis=-1, keepdims=True)
            grad_scores = (probs * (contract_cols(grad, value) - delta)).astype(low)
            grad_value[...] += contract_rows(probs.astype(low), grad)
            grad_key[...] += contract_rows(grad_scores, query) * scale
            turned = jnp.dot(grad_scores, key, preferred_element_type=wide) * scale
            turned = rope_rows_back(turned, cosine_ref[here, :], sine_ref[here, :])
            before, gain = rms_back(turned, pre_ref[here, cols], query_gain)
            grad_qkv[here, cols] = before.astype(low)
            gain_query = gain_query + gain
    turned = rope_rows_back(grad_key[...], cosine_ref[...], sine_ref[...])
    before, gain_key = rms_back(turned, pre_ref[:, pair_cols : pair_cols + head_dim], key_gain)
    grad_qkv[:, pair_cols : pair_cols + head_dim] = before.astype(low)
    grad_qkv[:, pair_cols + head_dim :] = grad_value[...].astype(low)
    head_gain_ref[0:1, :] = gain_query
    head_gain_ref[1:2, :] = gain_key
    gain_one = jnp.zeros((1, tokens_ref.shape[1]), wide)
    for start in range(0, length, step):
        here = slice(start, start + step)
        partial = contract_cols(grad_qkv[here, :], matrix_ref[:, :qkv_cols])
        partials[here, :] = partial.astype(low)
        rows = tokens_ref[here, :].astype(wide)
        inverse = lax.rsqrt(jnp.mean(rows * rows, axis=-1, keepdims=True) + eps_model)
        gain_one = gain_one + jnp.sum(partial * (rows * inverse), axis=0, keepdims=True)
    gain_ref[0:1, :] = gain_one
    for n in range(count):
        start = pl.multiple_of((place_ref[0] ^ n) * row_count, row_count)
        sent[n][...] = partials[pl.ds(start, row_count), :]
    grads_ref[:, :qkv_cols] = contract_rows(normed_ref[...], grad_qkv[...]).astype(low)
    for n in range(groups):
        attended = out_ref[n * length : (n + 1) * length, :].astype(low)
        cols = slice(qkv_cols + n * head_dim, qkv_cols + (n + 1) * head_dim)
        grads_ref[:, cols] = contract_rows(middle[...], attended).astype(low)


def whole_specs(arrays):
    return [pl.BlockSpec(memory_space=pltpu.VMEM) for _ in arrays]


def prepare(place, rows, weights, cosine, sine, head_gains, groups):
    low, wide = jnp.bfloat16, jnp.float32
    length, width = rows.shape
    head_dim = head_gains.shape[1]
    matrix_rows, matrix_cols = len(weights) * weights[0].shape[0], weights[0].shape[1]
    operands = (rows, *weights, cosine, sine, head_gains)
    outs = [
        ((matrix_rows, matrix_cols), low),
        ((8, width), wide),
        ((length, width), low),
        ((length, (groups + 1) * head_dim), wide),
        ((groups * length, head_dim), low),
        ((length, head_dim), low),
        ((length, head_dim), low),
    ]
    return pl.pallas_call(
        functools.partial(prepare_kernel, groups, len(weights)),
        in_specs=[pl.BlockSpec(memory_space=pltpu.SMEM)] + whole_specs(operands),
        out_specs=whole_specs(outs),
        out_shape=[jax.ShapeDtypeStruct(*out) for out in outs],
        compiler_params=pltpu.CompilerParams(vmem_limit_bytes=48 * 1024 * 1024),
    )(place, *operands)


def attend_back(place, blocks, operands, groups):
    low, wide = jnp.bfloat16, jnp.float32
    row_count, width = blocks[0].shape
    length, head_dim = operands[2].shape
    qkv_cols = (groups + 2) * head_dim
    operands = (*blocks, *operands)
    outs = [
        ((width, qkv_cols + groups * head_dim), low),
        ((8, width), wide),
        ((8, head_dim), wide),
    ] + [((row_count, width), low)] * len(blocks)
    return pl.pallas_call(
        functools.partial(attend_back_kernel, groups, len(blocks)),
        in_specs=[pl.BlockSpec(memory_space=pltpu.SMEM)] + whole_specs(operands),
        out_specs=whole_specs(outs),
        out_shape=[jax.ShapeDtypeStruct(*out) for out in outs],
        scratch_shapes=[
            pltpu.VMEM((length, width), low),
            pltpu.VMEM((length, qkv_cols), low),
            pltpu.VMEM((length, head_dim), wide),
            pltpu.VMEM((length, head_dim), wide),
            pltpu.VMEM((length, width), low),
        ],
        compiler_params=pltpu.CompilerParams(vmem_limit_bytes=56 * 1024 * 1024),
    )(place, *operands)


def attend(place, operands, groups, count):
    low, wide = jnp.bfloat16, jnp.float32
    length, head_dim = operands[1].shape
    width = operands[5].shape[0]
    outs = [((groups * length, head_dim), wide), ((groups * length, 1), wide)]
    outs = outs + [((length // count, width), low)] * count
    return pl.pallas_call(
        functools.partial(attend_kernel, groups, count),
        in_specs=[pl.BlockSpec(memory_space=pltpu.SMEM)] + whole_specs(operands),
        out_specs=whole_specs(outs),
        out_shape=[jax.ShapeDtypeStruct(*out) for out in outs],
        scratch_shapes=[pltpu.VMEM((length, width), low)],
        compiler_params=pltpu.CompilerParams(vmem_limit_bytes=48 * 1024 * 1024),
    )(place, *operands)


def split_shards(
    tokens,
    span_order,
    w_query,
    key_matrix,
    value_matrix,
    w_output,
    w_gate,
    w_up,
    w_down,
    norm_gains,
    head_gains,
    cotangent,
):
    low, wide = jnp.bfloat16, jnp.float32
    dp_size, seq_size = lax.axis_size("dp"), lax.axis_size("seq")
    row_count, width = tokens.shape
    head_dim = head_gains.shape[1]
    groups = w_query.shape[1] // key_matrix.shape[1]
    pair_cols = groups * head_dim
    qkv_cols = pair_cols + 2 * head_dim
    unit_cols = w_gate.shape[1] // dp_size
    weight_rows = w_query.shape[0]
    length = seq_size * row_count
    span_len = row_count // 2
    seq_index = lax.axis_index("seq")

    def cut(weight, parts):
        return weight.reshape(weight_rows, parts, -1).transpose(1, 0, 2)

    seq_tokens = gathered(tokens, "seq")
    cotangent, tokens = lax.optimization_barrier((cotangent, tokens))

    gain_cols = jnp.pad(norm_gains.T, ((0, 0), (0, 126)))
    gain_cols = jnp.broadcast_to(gain_cols[None], (seq_size, weight_rows, 128))
    first_part = [cut(w, seq_size) for w in (w_query, key_matrix, value_matrix, w_output.T)]
    first_part = jnp.concatenate(first_part + [gain_cols], -1)
    first_part = to_seq(first_part)
    first_part = first_part.reshape(seq_size * weight_rows, -1)
    first_part = gather_dp(first_part)
    *first_part, w_gate, w_up, w_down = lax.optimization_barrier(
        (*first_part, w_gate, w_up, w_down)
    )
    second_part = jnp.concatenate([cut(w, dp_size) for w in (w_gate, w_up, w_down.T)], -1)
    second_part = over_dp(second_part).reshape(dp_size * weight_rows, -1)
    seq_tokens, second_part = lax.optimization_barrier((seq_tokens, second_part))
    second_part = gathered(second_part, "seq").reshape(seq_size, dp_size, weight_rows, -1)
    second_part = second_part.transpose(1, 0, 2, 3).reshape(width, -1)
    w_gate_up = second_part[:, : 2 * unit_cols]
    wd_turned = second_part[:, 2 * unit_cols :]
    offsets = jnp.arange(span_len, dtype=jnp.int32)
    positions = (span_order[0][:, None] * span_len + offsets).reshape(length)
    cosine, sine = rope_tables(positions, head_dim)
    half_dim = head_dim // 2
    sine = jnp.concatenate([-sine[:, :half_dim], sine[:, half_dim:]], 1)
    gains_head = head_gains.astype(wide)
    inputs = tokens.astype(wide)
    place = jnp.stack([seq_index, lax.axis_index("dp")]).astype(jnp.int32)
    matrix, gains, normed_low, qkv_pre, query_low, key_low, value_low = prepare(
        place, seq_tokens, first_part, cosine, sine, gains_head, groups
    )

    query_pos = jnp.concatenate([positions] * groups)[:, None]
    key_pos = positions[None, :]
    operands = (query_low, key_low, value_low, query_pos, key_pos, matrix)
    attended, log_total, *blocks = attend(place, operands, groups, seq_size)
    middle = inputs + scatter_seq(blocks)

    team_cotangent = gather_team(cotangent)
    normed_two, norm_two_back = jax.vjp(rms_scale, middle, gains[1])
    normed_two_low = gather_team(normed_two.astype(low))
    gate_up = jnp.dot(normed_two_low, w_gate_up, preferred_element_type=wide)
    hidden, swiglu_back = jax.vjp(swiglu, gate_up[:, :unit_cols], gate_up[:, unit_cols:])
    hidden_low = hidden.astype(low)
    grad_hidden = jnp.dot(team_cotangent, wd_turned, preferred_element_type=wide)
    grad_gate, grad_up = swiglu_back(grad_hidden)
    gate_up_low = jnp.concatenate([grad_gate.astype(low), grad_up.astype(low)], -1)
    partial = contract_cols(gate_up_low, w_gate_up)
    partial, normed_two_low, gate_up_low = lax.optimization_barrier(
        (partial, normed_two_low, gate_up_low)
    )
    second_grads = jnp.concatenate(
        [contract_rows(normed_two_low, gate_up_low), contract_rows(team_cotangent, hidden_low)], -1
    ).astype(low)
    second_grads = second_grads.reshape(dp_size, seq_size, weight_rows, -1)
    second_grads = second_grads.transpose(1, 0, 2, 3).reshape(width, -1)
    partial = scatter_step(partial, 1)
    partial, second_grads = lax.optimization_barrier((partial, second_grads))
    second_grads = summed(second_grads, "seq")
    grad_middle_norm, grad_gain_two = norm_two_back(scatter_rest(partial))
    grad_middle = cotangent.astype(wide) + grad_middle_norm
    middle_low = gather_seq(grad_middle.astype(low))
    out_partial = contract_cols(hidden_low, wd_turned)
    out_partial, *middle_low = lax.optimization_barrier((out_partial, *middle_low))
    out_partial = scatter_step(out_partial, 1)

    middle_low[0], out_partial = lax.optimization_barrier((middle_low[0], out_partial))
    output = middle + scatter_rest(out_partial)
    operands = (matrix, query_low, key_low, value_low, query_pos, key_pos, attended, log_total)
    operands = operands + (qkv_pre, cosine, sine, gains_head, seq_tokens, normed_low)
    first_grads, grad_gain_one, head_gain, *blocks = attend_back(place, middle_low, operands, groups)
    first_grads, output, *blocks = lax.optimization_barrier((first_grads, output, *blocks))
    _, norm_back = jax.vjp(lambda values: rms_scale(values, gains[0]), inputs)
    def in_columns(cols):
        return jnp.pad(cols, ((0, 0), (0, 128 - cols.shape[1])))

    seq_rows = seq_size * weight_rows
    head_gain = head_gain[:2].T
    head_gain = jnp.pad(head_gain, ((0, seq_rows - head_dim), (0, 0)))
    head_gain = jnp.concatenate([head_gain] * dp_size, 0)
    gain_cols = jnp.concatenate([jnp.stack([grad_gain_one[0], grad_gain_two], 1), head_gain], 1)
    first_grads = jnp.concatenate([first_grads, in_columns(gain_cols).astype(low)], 1)
    dp_index = lax.axis_index("dp")

    def rows_for(n):
        return lax.dynamic_slice_in_dim(first_grads, (dp_index ^ n) * seq_rows, seq_rows)

    others = [swapped(rows_for(n), "dp", n) for n in range(1, dp_size)]
    grad_normed, second_grads, *others = scatter_seq(blocks, (second_grads, *others))
    first_grads = rows_for(0).astype(wide)
    for other in others:
        first_grads = first_grads + other.astype(wide)
    first_grads = first_grads.astype(low)
    second_grads = over_dp(second_grads.reshape(dp_size, weight_rows, -1))
    _, norm_back = jax.vjp(lambda values: rms_scale(values, gains[0]), inputs)
    grad_input = grad_middle + norm_back(grad_normed)[0]

    matrix_cols = qkv_cols + pair_cols
    gain_cols = first_grads[:, matrix_cols:]
    head_gain = gain_cols[:head_dim, 2:4].reshape(weight_rows, -1)
    head_width = head_gain.shape[1]
    head_gain = jnp.concatenate([head_gain] * seq_size, 0)
    gain_cols = in_columns(jnp.concatenate([gain_cols[:, :2], head_gain], 1))
    first_grads = jnp.concatenate([first_grads[:, :matrix_cols], gain_cols], 1)
    first_grads, second_grads = lax.optimization_barrier((first_grads, second_grads))
    first_grads = to_seq(first_grads.reshape(seq_size, weight_rows, -1))
    gain_cols = jnp.sum(first_grads[..., matrix_cols:].astype(wide), 0)
    grad_norm = gain_cols[:, :2].T
    grad_head = gain_cols[:, 2 : 2 + head_width].reshape(head_dim, 2).T

    def joined(blocks, start, cols):
        parts = [blocks[n, :, start : start + cols] for n in range(blocks.shape[0])]
        return jnp.concatenate(parts, 1).astype(wide)

    return (
        output.astype(low),
        grad_input.astype(low),
        joined(first_grads, 0, pair_cols),
        joined(first_grads, pair_cols, head_dim),
        joined(first_grads, pair_cols + head_dim, head_dim),
        joined(first_grads, qkv_cols, pair_cols).T,
        joined(second_grads, 0, unit_cols),
        joined(second_grads, unit_cols, unit_cols),
        joined(second_grads, 2 * unit_cols, unit_cols).T,
        grad_norm,
        grad_head,
    )


def solution(mesh):
    sizes = dict(mesh.shape)

    def layer(*arrays):
        query_cols, key_cols = arrays[2].shape[1], arrays[3].shape[1]
        kv_heads = key_cols // arrays[10].shape[1]
        dp, seq = sizes["dp"], sizes["seq"]
        fits = dp > 1 and dp & (dp - 1) == 0 and seq & (seq - 1) == 0 and kv_heads == seq
        fits = fits and arrays[6].shape[1] % (128 * dp) == 0
        return mapped(split_shards if fits else shards, mesh)(*arrays)

    return layer


def mapped(function, mesh):
    return jax.shard_map(
        function,
        mesh=mesh,
        in_specs=(
            P(("dp", "seq"), None),
            P("dp", None),
            P(("dp", "seq"), None),
            P(("dp", "seq"), None),
            P(("dp", "seq"), None),
            P(None, ("dp", "seq")),
            P(("dp", "seq"), None),
            P(("dp", "seq"), None),
            P(None, ("dp", "seq")),
            P(None, ("dp", "seq")),
            P(),
            P(("dp", "seq"), None),
        ),
        out_specs=(
            P(("dp", "seq"), None),
            P(("dp", "seq"), None),
            P(("dp", "seq"), None),
            P(("dp", "seq"), None),
            P(("dp", "seq"), None),
            P(None, ("dp", "seq")),
            P(("dp", "seq"), None),
            P(("dp", "seq"), None),
            P(None, ("dp", "seq")),
            P(None, ("dp", "seq")),
            P(),
        ),
        check_vma=False,
    )
```
